32 devices in a mesh: fgrp: 8 (over z, x), tile: 2 (over core), pol: 2 (over y).
Axes of the slice: x: 2, y: 2, z: 4, core: 2. Of those that a mesh axis runs over, the one named last changes fastest.
Arguments:
- voltages: bfloat16 [2, 2048, 131072], P(None, ('tile', 'pol'), 'fgrp'), may hold values from -4 to 4
- gains: float32 [2, 2048, 64], P(None, ('tile', 'pol')), may hold values from -4 to 4
Outputs:
- visibilities: float32 [64, 2, 2048, 2048], P('fgrp', None, ('tile', 'pol'))
The draws below stay inside these ranges and needn't reach their ends.
All inputs are finite; a program needn't handle non-finite values.
Results may differ from the reference program's by a relative error of at most 0.0039.
Values may be sent and summed in bfloat16 or wider, within the bound.
No kernel may reach another device: no remote copies, remote signals or barrier semaphores. Data moves between devices by JAX's collectives and lax.ppermute only.
A program may use at most 256 MiB of HBM per device.

```python
import math
import jax
import jax.numpy as jnp
from jax import lax

INPUTS = 2048
NFFT = 4096
TAPS = 4
SPECTRA = 32
CHANNELS = 64
SAMPLES = 131072


def level_of(rng, shape, cuts, low, largest):
    def one(dim, shards_of):
        draws = jax.random.uniform(jax.random.fold_in(jax.random.fold_in(rng, 6), dim), (shards_of,), jnp.float32, low / len(cuts), largest / len(cuts))
        return jnp.repeat(jnp.exp(draws), shape[dim] // shards_of).reshape((-1,) + (1,) * (len(shape) - dim - 1))

    level = one(*cuts[0])
    for cut in cuts[1:]:
        level = level * one(*cut)
    return level


def normal_values(rng, extent, spread, reach, cuts=(), kind=jnp.bfloat16):
    array = spread * jax.random.normal(rng, extent, jnp.float32)
    if cuts:
        array = array * level_of(rng, extent, cuts, -0.22, 0.18)
    return jnp.clip(array, -reach, reach).astype(kind)


def setup_inputs(seed: int = 0) -> dict:
    key_of = jax.random.split(jax.random.key(seed), 3)
    voltages = normal_values(key_of[0], (2, INPUTS, SAMPLES), 1.0, 4.0, ((1, 4), (2, 8)))
    gains = normal_values(key_of[1], (2, INPUTS, CHANNELS), 1.0, 4.0, ((1, 4),), jnp.float32)
    return {"voltages": voltages, "gains": gains}


def make_taps(tap_count, length):
    span_total = tap_count * length
    position = jnp.arange(span_total, dtype=jnp.int32).astype(jnp.float32)
    centred = (position - span_total / 2 + 0.5) / length
    window = 0.5 - 0.5 * jnp.cos(2.0 * math.pi * (position + 0.5) / span_total)
    return (jnp.sinc(centred) * window).reshape(tap_count, length)

def dft_table(length, channels):
    sample = jnp.arange(length, dtype=jnp.int32)
    column = jnp.arange(channels, dtype=jnp.int32)
    phases = sample[:, None] * column[None, :] % length
    angles = phases.astype(jnp.float32) * (2.0 * math.pi / length)
    return jnp.concatenate([jnp.cos(angles), jnp.sin(angles)], axis=1) / math.sqrt(length)

def filter_sum(padded, filter_taps, spectra_count):
    result = filter_taps[0] * padded[:, :, 0:spectra_count, :].astype(jnp.float32)
    for tap_index in range(1, filter_taps.shape[0]):
        result = result + filter_taps[tap_index] * padded[:, :, tap_index:tap_index + spectra_count, :].astype(jnp.float32)
    return result

def transform(filtered, table, channels):
    inputs_count = filtered.shape[1]
    spectra_count = filtered.shape[2]
    rows_flat = filtered.reshape(2, inputs_count * spectra_count, filtered.shape[3])
    product = jnp.einsum('prk,kq->prq', rows_flat, table, precision=lax.Precision.HIGHEST, preferred_element_type=jnp.float32)
    real_part = product[0, :, :channels] + product[1, :, channels:]
    imag_part = product[1, :, :channels] - product[0, :, channels:]
    return (real_part.reshape(inputs_count, spectra_count, channels), imag_part.reshape(inputs_count, spectra_count, channels))

def apply_gain(real_part, imag_part, gain_block):
    gain_real = gain_block[0][:, None, :]
    gain_imag = gain_block[1][:, None, :]
    out_real = gain_real * real_part - gain_imag * imag_part
    out_imag = gain_real * imag_part + gain_imag * real_part
    return jnp.stack([out_real, out_imag]).astype(jnp.bfloat16)

def reference(voltages, gains):
    filter_taps = make_taps(TAPS, NFFT)
    table = dft_table(NFFT, CHANNELS)
    block_size = 64
    blocks_count = INPUTS // block_size
    voltage_blocks = jnp.moveaxis(voltages.reshape(2, blocks_count, block_size, SPECTRA, NFFT), 1, 0)
    gain_blocks = jnp.moveaxis(gains.reshape(2, blocks_count, block_size, CHANNELS), 1, 0)

    def channelize(pieces):
        frames, gain_block = pieces
        padded = jnp.concatenate([jnp.zeros((2, block_size, TAPS - 1, NFFT), jnp.bfloat16), frames], axis=2)
        filtered = filter_sum(padded, filter_taps, SPECTRA)
        real_part, imag_part = transform(filtered, table, CHANNELS)
        return apply_gain(real_part, imag_part, gain_block)
    spectra = lax.map(channelize, (voltage_blocks, gain_blocks))
    spectra = jnp.moveaxis(spectra, 0, 1).reshape(2, INPUTS, SPECTRA, CHANNELS)
    by_channel = jnp.transpose(spectra, (3, 0, 1, 2))
    norm_factor = SPECTRA ** (-0.5)

    def correlate(channel_data):
        left_real = channel_data[0]
        left_imag = channel_data[1]
        real_sum = jnp.dot(left_real, left_real.T, preferred_element_type=jnp.float32) + jnp.dot(left_imag, left_imag.T, preferred_element_type=jnp.float32)
        imag_sum = jnp.dot(left_imag, left_real.T, preferred_element_type=jnp.float32) - jnp.dot(left_real, left_imag.T, preferred_element_type=jnp.float32)
        return jnp.stack([real_sum, imag_sum]) * norm_factor
    return lax.map(correlate, by_channel)
```

```python
import functools
import math

import jax
import jax.numpy as jnp
import ml_dtypes
import numpy as np
from jax import lax
from jax.experimental import pallas as pl
from jax.experimental.pallas import tpu as pltpu
from jax.sharding import PartitionSpec as P

NFFT = 4096
TAPS = 4
VMEM = 56 * 2**20


def filter_taps():
    span = TAPS * NFFT
    position = np.arange(span, dtype=np.float64)
    centred = (position - span / 2 + 0.5) / NFFT
    window = 0.5 - 0.5 * np.cos(2.0 * np.pi * (position + 0.5) / span)
    return (np.sinc(centred) * window).reshape(TAPS, NFFT)


def low_taps():
    energy = (filter_taps() ** 2).sum(axis=1)
    return [t for t in range(TAPS) if energy[t] > 0.01 * energy.sum()]


def filter_table(channels):
    phases = np.arange(NFFT)[:, None] * np.arange(channels)[None, :] % NFFT
    angles = phases * (2.0 * np.pi / NFFT)
    transform = np.concatenate([np.cos(angles), np.sin(angles)], axis=1) / math.sqrt(NFFT)
    blocks = [tap[:, None] * transform for tap in filter_taps()]
    high = [b.astype(np.float32).astype(ml_dtypes.bfloat16) for b in blocks]
    low = [
        (blocks[t] - high[t].astype(np.float64)).astype(np.float32).astype(ml_dtypes.bfloat16)
        for t in low_taps()
    ]
    return np.concatenate(high + low, axis=1)


def filter_kernel(volt_ref, table_ref, gain_a_ref, gain_b_ref, out_ref, sums):
    step_k, frame = pl.program_id(0), pl.program_id(1)
    frames = pl.num_programs(1)
    rows = volt_ref.shape[1]
    width = sums.shape[3]
    half = width // 2
    slots = sums.shape[0]

    @pl.when((step_k == 0) & (frame == 0))
    def _():
        sums[...] = jnp.zeros_like(sums)

    product = jnp.dot(
        volt_ref[...].reshape(2 * rows, volt_ref.shape[2]),
        table_ref[...],
        preferred_element_type=jnp.float32,
    )
    low = low_taps()
    for tap in range(TAPS):
        term = product[:, tap * width : (tap + 1) * width]
        if tap in low:
            at = (TAPS + low.index(tap)) * width
            term = term + product[:, at : at + width]
        sums[frame + TAPS - 1 - tap] += term.reshape(2, rows, width)

    @pl.when((step_k == pl.num_programs(0) - 1) & (frame == frames - 1))
    def _():
        owners = out_ref.shape[0]
        share = half // owners
        lane = lax.broadcasted_iota(jnp.int32, (rows, width), 1)
        for slot in range(slots):
            turned = pltpu.roll(sums[slot, 1], half, 1)
            raw = jnp.where(lane < half, turned + sums[slot, 0], turned - sums[slot, 0])
            value = gain_a_ref[...] * raw + gain_b_ref[...] * pltpu.roll(raw, half, 1)
            value = value.T
            for owner in range(owners):
                at = owner * share
                both = jnp.concatenate(
                    [value[at : at + share], value[half + at : half + at + share]], axis=0
                )
                out_ref[owner, 2 * share * slot : 2 * share * (slot + 1), :] = both.astype(
                    jnp.bfloat16
                )


def filter_part(voltages, table, gain_a, gain_b, part, rows, owners):
    frames = voltages.shape[2] // NFFT
    width = gain_a.shape[1]
    steps = 4
    depth = NFFT // steps
    slots = frames + TAPS - 1
    out_rows = slots * width // owners
    columns = table.shape[1]
    return pl.pallas_call(
        filter_kernel,
        grid=(steps, frames),
        in_specs=[
            pl.BlockSpec((2, rows, depth), lambda k, f: (0, part, f * steps + k)),
            pl.BlockSpec((depth, columns), lambda k, f: (k, 0)),
            pl.BlockSpec((rows, width), lambda k, f: (part, 0)),
            pl.BlockSpec((rows, width), lambda k, f: (part, 0)),
        ],
        out_specs=pl.BlockSpec((owners, out_rows, rows), lambda k, f: (0, 0, 0)),
        out_shape=jax.ShapeDtypeStruct((owners, out_rows, rows), jnp.bfloat16),
        scratch_shapes=[pltpu.VMEM((slots, 2, rows, width), jnp.float32)],
        compiler_params=pltpu.CompilerParams(vmem_limit_bytes=VMEM),
        cost_estimate=pl.CostEstimate(
            flops=2 * 2 * rows * frames * NFFT * columns,
            bytes_accessed=2 * (2 * rows * frames * NFFT + NFFT * columns),
            transcendentals=0,
        ),
        name="filter_part",
    )(voltages, table, gain_a, gain_b)


def merge_kernel(frames, share, in_ref, out_ref, scratch):
    owners = in_ref.shape[0]
    depth = 2 * owners * frames
    blocks = scratch.shape[0]
    for group in range(owners):
        for frame in range(frames):
            at = 2 * share * frame
            value = in_ref[group, at : at + 2 * share, :].astype(jnp.float32)
            if group > 0 and frame < TAPS - 1:
                at = 2 * share * (frame + frames)
                value = value + in_ref[group - 1, at : at + 2 * share, :].astype(jnp.float32)
            if value.shape[1] < 128 * blocks:
                spare = jnp.zeros((2 * share, 128 * blocks - value.shape[1]), jnp.float32)
                value = jnp.concatenate([value, spare], axis=1)
            for part in range(2):
                row = (part * owners + group) * frames + frame
                for block in range(blocks):
                    scratch[block, pl.ds(row, share, stride=depth), :] = value[
                        part * share : (part + 1) * share, block * 128 : (block + 1) * 128
                    ]
    for block in range(blocks):
        lanes = min(128, out_ref.shape[1] - block * 128)
        out_ref[:, block * 128 : block * 128 + lanes] = scratch[block, :, :lanes].astype(
            jnp.bfloat16
        )


def merge(turned, frames, share):
    owners, _, rows = turned.shape
    out_rows = share * 2 * owners * frames
    return pl.pallas_call(
        functools.partial(merge_kernel, frames, share),
        out_shape=jax.ShapeDtypeStruct((out_rows, rows), jnp.bfloat16),
        scratch_shapes=[pltpu.VMEM((pl.cdiv(rows, 128), out_rows, 128), jnp.float32)],
        compiler_params=pltpu.CompilerParams(vmem_limit_bytes=VMEM),
        name="merge",
    )(turned)


def correlate_kernel(norm, parts, *refs):
    own_refs, all_refs, out_ref = refs[:parts], refs[parts : 2 * parts], refs[2 * parts]
    rows = own_refs[0].shape[1]
    groups = all_refs[0].shape[0]
    for part in range(parts):

        @pl.when(pl.program_id(1) == part)
        def _():
            own = own_refs[part][...]
            half = own.shape[0] // 2
            swapped = jnp.concatenate([own[half:], -own[:half]], axis=0)
            left = jnp.concatenate([own, swapped], axis=1)
            for group in range(groups):
                for other in range(parts):
                    product = norm * lax.dot_general(
                        left,
                        all_refs[other][group],
                        (((0,), (0,)), ((), ())),
                        preferred_element_type=jnp.float32,
                    )
                    at = (group * parts + other) * rows
                    out_ref[0, 0, :, at : at + rows] = product[:rows]
                    out_ref[0, 1, :, at : at + rows] = product[rows:]


def correlate(own, gathered, share, norm):
    parts = len(own)
    out_rows, rows = own[0].shape
    depth = out_rows // share
    groups = gathered[0].shape[0]
    total = groups * parts * rows
    return pl.pallas_call(
        functools.partial(correlate_kernel, norm, parts),
        grid=(share, parts),
        in_specs=[pl.BlockSpec((depth, rows), lambda c, r: (c, 0))] * parts
        + [pl.BlockSpec((groups, depth, rows), lambda c, r: (0, c, 0))] * parts,
        out_specs=pl.BlockSpec((1, 2, rows, total), lambda c, r: (c, 0, r, 0)),
        out_shape=jax.ShapeDtypeStruct((share, 2, parts * rows, total), jnp.float32),
        compiler_params=pltpu.CompilerParams(vmem_limit_bytes=VMEM),
        cost_estimate=pl.CostEstimate(
            flops=2 * share * 2 * parts * rows * total * depth,
            bytes_accessed=4 * share * 2 * parts * rows * total,
            transcendentals=0,
        ),
        name="correlate",
    )(*own, *gathered)


def body(voltages, gains):
    inputs_here = voltages.shape[1]
    frames_here = voltages.shape[2] // NFFT
    channels = gains.shape[2]
    owners = lax.axis_size("fgrp")
    share = channels // owners
    rows = 256 if inputs_here % 256 == 0 else inputs_here
    parts = inputs_here // rows
    norm = 1.0 / math.sqrt(frames_here * owners)
    table = jnp.asarray(filter_table(channels))
    gain_a = jnp.concatenate([gains[0], gains[0]], axis=1)
    gain_b = jnp.concatenate([-gains[1], gains[1]], axis=1)
    own, gathered = [], []
    for part in range(parts):
        partial = filter_part(voltages, table, gain_a, gain_b, part, rows, owners)
        turned = lax.all_to_all(partial, "fgrp", split_axis=0, concat_axis=0, tiled=True)
        merged = merge(turned, frames_here, share)
        wide = lax.all_gather(merged, "pol", axis=0)
        wide = lax.all_gather(wide, "tile", axis=0)
        own.append(merged)
        gathered.append(wide.reshape((-1,) + merged.shape))
    return correlate(own, gathered, share, norm)


def solution(mesh):
    placed = (P(None, ("tile", "pol"), "fgrp"), P(None, ("tile", "pol"), None))
    return jax.shard_map(
        body,
        mesh=mesh,
        in_specs=placed,
        out_specs=P("fgrp", None, ("tile", "pol"), None),
        check_vma=False,
    )
```

```python
import functools
import math

import jax
import jax.numpy as jnp
import ml_dtypes
import numpy as np
from jax import lax
from jax.experimental import pallas as pl
from jax.experimental.pallas import tpu as pltpu
from jax.sharding import PartitionSpec as P

NFFT = 4096
TAPS = 4
VMEM = 56 * 2**20


def filter_taps():
    span = TAPS * NFFT
    position = np.arange(span, dtype=np.float64)
    centred = (position - span / 2 + 0.5) / NFFT
    window = 0.5 - 0.5 * np.cos(2.0 * np.pi * (position + 0.5) / span)
    return (np.sinc(centred) * window).reshape(TAPS, NFFT)


def low_taps():
    energy = (filter_taps() ** 2).sum(axis=1)
    return [t for t in range(TAPS) if energy[t] > 0.01 * energy.sum()]


def filter_table(channels):
    phases = np.arange(NFFT)[:, None] * np.arange(channels)[None, :] % NFFT
    angles = phases * (2.0 * np.pi / NFFT)
    transform = np.concatenate([np.cos(angles), np.sin(angles)], axis=1) / math.sqrt(NFFT)
    blocks = [tap[:, None] * transform for tap in filter_taps()]
    high = [b.astype(np.float32).astype(ml_dtypes.bfloat16) for b in blocks]
    low = [
        (blocks[t] - high[t].astype(np.float64)).astype(np.float32).astype(ml_dtypes.bfloat16)
        for t in low_taps()
    ]
    return np.ascontiguousarray(np.concatenate(high + low, axis=1).T)


def filter_kernel(volt_ref, table_ref, gain_ref, out_ref, sums):
    frame, part = pl.program_id(0), pl.program_id(1)
    width, rows = sums.shape[2], sums.shape[3]
    half = width // 2
    slots = sums.shape[0]

    @pl.when((frame == 0) & (part == 0))
    def _():
        sums[...] = jnp.zeros_like(sums)

    product = lax.dot_general(
        table_ref[...],
        volt_ref[0],
        (((1,), (1,)), ((), ())),
        preferred_element_type=jnp.float32,
    )
    low = low_taps()
    for tap in range(TAPS):
        term = product[tap * width : (tap + 1) * width]
        if tap in low:
            at = (TAPS + low.index(tap)) * width
            term = term + product[at : at + width]
        sums[frame + TAPS - 1 - tap, part] += term

    @pl.when((frame == pl.num_programs(0) - 1) & (part == 1))
    def _():
        owners = out_ref.shape[0]
        share = half // owners
        for slot in range(slots):
            real = sums[slot, 0, :half] + sums[slot, 1, half:]
            imag = sums[slot, 1, :half] - sums[slot, 0, half:]
            out_real = gain_ref[0] * real - gain_ref[1] * imag
            out_imag = gain_ref[0] * imag + gain_ref[1] * real
            for owner in range(owners):
                at = owner * share
                both = jnp.concatenate(
                    [out_real[at : at + share], out_imag[at : at + share]], axis=0
                )
                out_ref[owner, 2 * share * slot : 2 * share * (slot + 1), :] = both.astype(
                    jnp.bfloat16
                )


def filter_all(voltages, table, gains, owners):
    rows = voltages.shape[1]
    frames = voltages.shape[2] // NFFT
    half = gains.shape[1]
    slots = frames + TAPS - 1
    out_rows = slots * 2 * half // owners
    columns = table.shape[0]
    return pl.pallas_call(
        filter_kernel,
        grid=(frames, 2),
        in_specs=[
            pl.BlockSpec((1, rows, NFFT), lambda f, c: (c, 0, f)),
            pl.BlockSpec((columns, NFFT), lambda f, c: (0, 0)),
            pl.BlockSpec((2, half, rows), lambda f, c: (0, 0, 0)),
        ],
        out_specs=pl.BlockSpec((owners, out_rows, rows), lambda f, c: (0, 0, 0)),
        out_shape=jax.ShapeDtypeStruct((owners, out_rows, rows), jnp.bfloat16),
        scratch_shapes=[pltpu.VMEM((slots, 2, 2 * half, rows), jnp.float32)],
        compiler_params=pltpu.CompilerParams(vmem_limit_bytes=VMEM),
        cost_estimate=pl.CostEstimate(
            flops=2 * 2 * rows * frames * NFFT * columns,
            bytes_accessed=2 * (2 * rows * frames * NFFT + NFFT * columns),
            transcendentals=0,
        ),
        name="filter_all",
    )(voltages, table, gains)


def merge_kernel(frames, share, in_ref, out_ref, scratch):
    owners = in_ref.shape[0]
    depth = 2 * owners * frames
    blocks = scratch.shape[0]
    for group in range(owners):
        for frame in range(frames):
            at = 2 * share * frame
            value = in_ref[group, at : at + 2 * share, :].astype(jnp.float32)
            if group > 0 and frame < TAPS - 1:
                at = 2 * share * (frame + frames)
                value = value + in_ref[group - 1, at : at + 2 * share, :].astype(jnp.float32)
            if value.shape[1] < 128 * blocks:
                spare = jnp.zeros((2 * share, 128 * blocks - value.shape[1]), jnp.float32)
                value = jnp.concatenate([value, spare], axis=1)
            for part in range(2):
                row = (part * owners + group) * frames + frame
                for block in range(blocks):
                    scratch[block, pl.ds(row, share, stride=depth), :] = value[
                        part * share : (part + 1) * share, block * 128 : (block + 1) * 128
                    ]
    for block in range(blocks):
        lanes = min(128, out_ref.shape[1] - block * 128)
        out_ref[:, block * 128 : block * 128 + lanes] = scratch[block, :, :lanes].astype(
            jnp.bfloat16
        )


def merge(turned, frames, share):
    owners, _, rows = turned.shape
    out_rows = share * 2 * owners * frames
    return pl.pallas_call(
        functools.partial(merge_kernel, frames, share),
        out_shape=jax.ShapeDtypeStruct((out_rows, rows), jnp.bfloat16),
        scratch_shapes=[pltpu.VMEM((pl.cdiv(rows, 128), out_rows, 128), jnp.float32)],
        compiler_params=pltpu.CompilerParams(vmem_limit_bytes=VMEM),
        name="merge",
    )(turned)


def visibility(left, right, norm):
    half = left.shape[0] // 2
    swapped = jnp.concatenate([left[half:], -left[:half]], axis=0)
    return norm * lax.dot_general(
        jnp.concatenate([left, swapped], axis=1),
        right,
        (((0,), (0,)), ((), ())),
        preferred_element_type=jnp.float32,
    )


def correlate_kernel(norm, own_ref, all_ref, out_ref):
    rows = own_ref.shape[1]
    for group in range(all_ref.shape[0]):
        product = visibility(own_ref[...], all_ref[group], norm)
        out_ref[0, 0, :, group * rows : (group + 1) * rows] = product[:rows]
        out_ref[0, 1, :, group * rows : (group + 1) * rows] = product[rows:]


def correlate(own, gathered, share, norm):
    out_rows, rows = own.shape
    depth = out_rows // share
    groups = gathered.shape[0]
    return pl.pallas_call(
        functools.partial(correlate_kernel, norm),
        grid=(share,),
        in_specs=[
            pl.BlockSpec((depth, rows), lambda c: (c, 0)),
            pl.BlockSpec((groups, depth, rows), lambda c: (0, c, 0)),
        ],
        out_specs=pl.BlockSpec((1, 2, rows, groups * rows), lambda c: (c, 0, 0, 0)),
        out_shape=jax.ShapeDtypeStruct((share, 2, rows, groups * rows), jnp.float32),
        compiler_params=pltpu.CompilerParams(vmem_limit_bytes=VMEM),
        name="correlate",
    )(own, gathered)


def block_kernel(norm, place_ref, own_ref, other_ref, *refs):
    out_ref = refs[-1]
    rows = own_ref.shape[1]
    product = visibility(own_ref[...], other_ref[...], norm)
    out_ref[0, 0] = product[:rows]
    out_ref[0, 1] = product[rows:]


def correlate_block(own, other, place, total, result, share, norm):
    out_rows, rows = own.shape
    depth = out_rows // share
    specs = [pl.BlockSpec((depth, rows), lambda c, place: (c, 0))] * 2
    operands = [place, own, other]
    aliases = {}
    if result is not None:
        aliases = {len(operands): 0}
        operands.append(result)
        specs.append(pl.BlockSpec(memory_space=pl.ANY))
    return pl.pallas_call(
        functools.partial(block_kernel, norm),
        grid_spec=pltpu.PrefetchScalarGridSpec(
            num_scalar_prefetch=1,
            grid=(share,),
            in_specs=specs,
            out_specs=pl.BlockSpec((1, 2, rows, rows), lambda c, place: (c, 0, 0, place[0])),
        ),
        out_shape=jax.ShapeDtypeStruct((share, 2, rows, total), jnp.float32),
        input_output_aliases=aliases,
        compiler_params=pltpu.CompilerParams(vmem_limit_bytes=VMEM),
        cost_estimate=pl.CostEstimate(
            flops=4 * share * rows * rows * depth,
            bytes_accessed=4 * share * 2 * rows * rows,
            transcendentals=0,
        ),
        name="correlate_block",
    )(*operands)


def cycled(shard, axis, by):
    length = lax.axis_size(axis)
    if by == 0:
        return shard
    return lax.ppermute(shard, axis, [(i, (i + by) % length) for i in range(length)])


def body(voltages, gains):
    inputs_here = voltages.shape[1]
    frames_here = voltages.shape[2] // NFFT
    channels = gains.shape[2]
    owners = lax.axis_size("fgrp")
    share = channels // owners
    norm = 1.0 / math.sqrt(frames_here * owners)
    table = jnp.asarray(filter_table(channels))
    partial = filter_all(voltages, table, jnp.swapaxes(gains, 1, 2), owners)
    turned = lax.all_to_all(partial, "fgrp", split_axis=0, concat_axis=0, tiled=True)
    own = merge(turned, frames_here, share)
    tiles, pols = lax.axis_size("tile"), lax.axis_size("pol")
    if inputs_here % 128:
        wide = lax.all_gather(lax.all_gather(own, "pol", axis=0), "tile", axis=0)
        return correlate(own, wide.reshape((-1,) + own.shape), share, norm)
    tile, pol = lax.axis_index("tile"), lax.axis_index("pol")
    result = None
    for by_pol in range(pols):
        near = cycled(own, "pol", by_pol)
        if by_pol:
            near, result = lax.optimization_barrier((near, result))
        for by_tile in range(tiles):
            other = cycled(near, "tile", by_tile)
            place = (tile - by_tile) % tiles * pols + (pol - by_pol) % pols
            result = correlate_block(
                own,
                other,
                place.astype(jnp.int32).reshape(1),
                tiles * pols * inputs_here,
                result,
                share,
                norm,
            )
    return result


def solution(mesh):
    placed = (P(None, ("tile", "pol"), "fgrp"), P(None, ("tile", "pol"), None))
    return jax.shard_map(
        body,
        mesh=mesh,
        in_specs=placed,
        out_specs=P("fgrp", None, ("tile", "pol"), None),
        check_vma=False,
    )
```

```python
import functools
import math

import jax
import jax.numpy as jnp
import ml_dtypes
import numpy as np
from jax import lax
from jax.experimental import pallas as pl
from jax.experimental.pallas import tpu as pltpu
from jax.sharding import PartitionSpec as P

NFFT = 4096
TAPS = 4
VMEM = 56 * 2**20


def filter_taps():
    span = TAPS * NFFT
    position = np.arange(span, dtype=np.float64)
    centred = (position - span / 2 + 0.5) / NFFT
    window = 0.5 - 0.5 * np.cos(2.0 * np.pi * (position + 0.5) / span)
    return (np.sinc(centred) * window).reshape(TAPS, NFFT)


def low_taps():
    energy = (filter_taps() ** 2).sum(axis=1)
    return [t for t in range(TAPS) if energy[t] > 0.01 * energy.sum()]


def filter_table(channels):
    phases = np.arange(NFFT)[:, None] * np.arange(channels)[None, :] % NFFT
    angles = phases * (2.0 * np.pi / NFFT)
    transform = np.concatenate([np.cos(angles), np.sin(angles)], axis=1) / math.sqrt(NFFT)
    blocks = [tap[:, None] * transform for tap in filter_taps()]
    high = [b.astype(np.float32).astype(ml_dtypes.bfloat16) for b in blocks]
    low = [
        (blocks[t] - high[t].astype(np.float64)).astype(np.float32).astype(ml_dtypes.bfloat16)
        for t in low_taps()
    ]
    return np.ascontiguousarray(np.concatenate(high + low, axis=1).T)


def peer(me, step, length, way):
    if length & (length - 1):
        return (me + way * step) % length
    return me ^ step


def filter_kernel(me_ref, volt_ref, table_hbm, gain_ref, *refs):
    out_refs, (sums, table, arrived) = refs[:-3], refs[-3:]
    frame, part = pl.program_id(0), pl.program_id(1)
    slots, _, width, rows = sums.shape
    half = width // 2
    pieces = arrived.shape[0]
    depth = table.shape[1] // pieces

    def fetch(piece):
        columns = pl.ds(piece * depth, depth)
        return pltpu.make_async_copy(
            table_hbm.at[:, columns], table.at[:, columns], arrived.at[piece]
        )

    def product(start, size):
        return lax.dot_general(
            table[:, start : start + size],
            volt_ref[0, :, start : start + size],
            (((1,), (1,)), ((), ())),
            preferred_element_type=jnp.float32,
        )

    def add(term):
        low = low_taps()
        for tap in range(TAPS):
            value = term[tap * width : (tap + 1) * width]
            if tap in low:
                at = (TAPS + low.index(tap)) * width
                value = value + term[at : at + width]
            sums[frame + TAPS - 1 - tap, part] += value

    first = (frame == 0) & (part == 0)

    @pl.when(first)
    def _():
        for piece in range(pieces):
            fetch(piece).start()
        sums[...] = jnp.zeros_like(sums)
        for piece in range(pieces):
            fetch(piece).wait()
            add(product(piece * depth, depth))

    @pl.when(jnp.logical_not(first))
    def _():
        add(product(0, table.shape[1]))

    @pl.when((frame == pl.num_programs(0) - 1) & (part == 1))
    def _():
        owners = len(out_refs)
        share = half // owners
        for slot in range(slots):
            real = sums[slot, 0, :half] + sums[slot, 1, half:]
            imag = sums[slot, 1, :half] - sums[slot, 0, half:]
            sums[slot, 0, :half] = gain_ref[0] * real - gain_ref[1] * imag
            sums[slot, 1, :half] = gain_ref[0] * imag + gain_ref[1] * real
        for step in range(owners):
            owner = peer(me_ref[0], step, owners, 1)
            mine = pl.ds(pl.multiple_of(owner * share, share), share)
            for slot in range(slots):
                both = jnp.concatenate([sums[slot, 0, mine, :], sums[slot, 1, mine, :]], axis=0)
                at = 2 * share * slot
                out_refs[step][at : at + 2 * share, :] = both.astype(jnp.bfloat16)


def filter_part(me, voltages, table, gains, part, rows, owners):
    frames = voltages.shape[2] // NFFT
    half = gains.shape[1]
    slots = frames + TAPS - 1
    out_rows = slots * 2 * half // owners
    columns = table.shape[0]
    pieces = 4
    return pl.pallas_call(
        filter_kernel,
        grid=(frames, 2),
        in_specs=[
            pl.BlockSpec(memory_space=pltpu.SMEM),
            pl.BlockSpec((1, rows, NFFT), lambda f, c: (c, part, f)),
            pl.BlockSpec(memory_space=pl.ANY),
            pl.BlockSpec((2, half, rows), lambda f, c: (0, 0, part)),
        ],
        out_specs=[pl.BlockSpec((out_rows, rows), lambda f, c: (0, 0))] * owners,
        out_shape=[jax.ShapeDtypeStruct((out_rows, rows), jnp.bfloat16)] * owners,
        scratch_shapes=[
            pltpu.VMEM((slots, 2, 2 * half, rows), jnp.float32),
            pltpu.VMEM((columns, NFFT), jnp.bfloat16),
            pltpu.SemaphoreType.DMA((pieces,)),
        ],
        compiler_params=pltpu.CompilerParams(vmem_limit_bytes=VMEM),
        cost_estimate=pl.CostEstimate(
            flops=2 * 2 * rows * frames * NFFT * columns,
            bytes_accessed=2 * (2 * rows * frames * NFFT + NFFT * columns),
            transcendentals=0,
        ),
        name="filter_part",
    )(me, voltages, table, gains)


def merge_kernel(frames, share, me_ref, *refs):
    in_refs, (out_ref, turned_ref, stacked, scratch) = refs[:-4], refs[-4:]
    owners = len(in_refs)
    depth = 2 * owners * frames
    blocks = scratch.shape[0]
    for step in range(owners):
        stacked[peer(me_ref[0], step, owners, -1)] = in_refs[step][...].astype(jnp.float32)
    for group in range(owners):
        for frame in range(frames):
            at = 2 * share * frame
            value = stacked[group, at : at + 2 * share, :]
            if group > 0 and frame < TAPS - 1:
                at = 2 * share * (frame + frames)
                value = value + stacked[group - 1, at : at + 2 * share, :]
            if value.shape[1] < 128 * blocks:
                spare = jnp.zeros((2 * share, 128 * blocks - value.shape[1]), jnp.float32)
                value = jnp.concatenate([value, spare], axis=1)
            for part in range(2):
                row = (part * owners + group) * frames + frame
                for block in range(blocks):
                    scratch[block, pl.ds(row, share, stride=depth), :] = value[
                        part * share : (part + 1) * share, block * 128 : (block + 1) * 128
                    ]
    for block in range(blocks):
        lanes = min(128, out_ref.shape[1] - block * 128)
        at = block * 128
        out_ref[:, at : at + lanes] = scratch[block, :, :lanes].astype(jnp.bfloat16)
        turned_ref[at : at + lanes, :] = scratch[block].T[:lanes].astype(jnp.bfloat16)


def merge(me, received, frames, share):
    owners = len(received)
    in_rows, rows = received[0].shape
    out_rows = share * 2 * owners * frames
    return pl.pallas_call(
        functools.partial(merge_kernel, frames, share),
        in_specs=[pl.BlockSpec(memory_space=pltpu.SMEM)]
        + [pl.BlockSpec(memory_space=pltpu.VMEM)] * owners,
        out_shape=[
            jax.ShapeDtypeStruct((out_rows, rows), jnp.bfloat16),
            jax.ShapeDtypeStruct((rows, out_rows), jnp.bfloat16),
        ],
        scratch_shapes=[
            pltpu.VMEM((owners, in_rows, rows), jnp.float32),
            pltpu.VMEM((pl.cdiv(rows, 128), out_rows, 128), jnp.float32),
        ],
        compiler_params=pltpu.CompilerParams(vmem_limit_bytes=16 * 2**20),
        name="merge",
    )(me, *received)


def block_kernel(norm, parts, blocks, place_ref, *refs):
    left_refs, right_refs, out_ref = refs[:parts], refs[parts : parts * (1 + blocks)], refs[-1]
    rows = left_refs[0].shape[0]
    depth = right_refs[0].shape[0]
    odd = lax.rem(pl.program_id(0), 2) == 1
    for block in range(blocks):

        @pl.when(pl.program_id(1) == block)
        def _():
            for other in range(parts):
                right = right_refs[block * parts + other][...]
                crossed = jnp.concatenate([-right[depth // 2 :], right[: depth // 2]], axis=0)
                for kind, value in enumerate((right, crossed)):
                    none = jnp.zeros_like(value)
                    wide = jnp.concatenate(
                        [jnp.where(odd, none, value), jnp.where(odd, value, none)], axis=0
                    )
                    for part in range(parts):
                        out_ref[
                            0,
                            kind,
                            part * rows : (part + 1) * rows,
                            other * rows : (other + 1) * rows,
                        ] = norm * jnp.dot(
                            left_refs[part][...], wide, preferred_element_type=jnp.float32
                        )


def correlate(left, rights, places, total, result, share, norm):
    parts, blocks = len(left), len(rights)
    rows, out_rows = left[0].shape
    depth = out_rows // share
    width = parts * rows
    operands = [places, *left, *(shard for right in rights for shard in right)]
    specs = [pl.BlockSpec((rows, 2 * depth), lambda c, b, places: (0, c // 2))] * parts
    specs += [pl.BlockSpec((depth, rows), lambda c, b, places: (c, 0))] * (blocks * parts)
    aliases = {}
    if result is not None:
        aliases = {len(operands): 0}
        operands.append(result)
        specs.append(pl.BlockSpec(memory_space=pl.ANY))
    return pl.pallas_call(
        functools.partial(block_kernel, norm, parts, blocks),
        grid_spec=pltpu.PrefetchScalarGridSpec(
            num_scalar_prefetch=1,
            grid=(share, blocks),
            in_specs=specs,
            out_specs=pl.BlockSpec((1, 2, width, width), lambda c, b, places: (c, 0, 0, places[b])),
        ),
        out_shape=jax.ShapeDtypeStruct((share, 2, width, total), jnp.float32),
        input_output_aliases=aliases,
        compiler_params=pltpu.CompilerParams(vmem_limit_bytes=24 * 2**20),
        cost_estimate=pl.CostEstimate(
            flops=4 * share * blocks * width * width * depth,
            bytes_accessed=4 * share * 2 * blocks * width * width,
            transcendentals=0,
        ),
        name="correlate",
    )(*operands)


def whole_kernel(norm, left_ref, all_ref, out_ref):
    rows = left_ref.shape[0]
    depth = all_ref.shape[1]
    odd = lax.rem(pl.program_id(0), 2) == 1
    for group in range(all_ref.shape[0]):
        right = all_ref[group]
        crossed = jnp.concatenate([-right[depth // 2 :], right[: depth // 2]], axis=0)
        for kind, value in enumerate((right, crossed)):
            none = jnp.zeros_like(value)
            wide = jnp.concatenate(
                [jnp.where(odd, none, value), jnp.where(odd, value, none)], axis=0
            )
            out_ref[0, kind, :, group * rows : (group + 1) * rows] = norm * jnp.dot(
                left_ref[...], wide, preferred_element_type=jnp.float32
            )


def correlate_whole(left, gathered, share, norm):
    rows, out_rows = left.shape
    depth = out_rows // share
    groups = gathered.shape[0]
    return pl.pallas_call(
        functools.partial(whole_kernel, norm),
        grid=(share,),
        in_specs=[
            pl.BlockSpec((rows, 2 * depth), lambda c: (0, c // 2)),
            pl.BlockSpec((groups, depth, rows), lambda c: (0, c, 0)),
        ],
        out_specs=pl.BlockSpec((1, 2, rows, groups * rows), lambda c: (c, 0, 0, 0)),
        out_shape=jax.ShapeDtypeStruct((share, 2, rows, groups * rows), jnp.float32),
        compiler_params=pltpu.CompilerParams(vmem_limit_bytes=24 * 2**20),
        name="correlate_whole",
    )(left, gathered)


def swapped(shard, axis, step):
    if step == 0:
        return shard
    length = lax.axis_size(axis)
    return lax.ppermute(shard, axis, [(i, peer(i, step, length, 1)) for i in range(length)])


def body(voltages, gains):
    inputs_here = voltages.shape[1]
    frames_here = voltages.shape[2] // NFFT
    channels = gains.shape[2]
    owners = lax.axis_size("fgrp")
    share = channels // owners
    rows = 256 if inputs_here % 256 == 0 else inputs_here
    parts = inputs_here // rows
    norm = 1.0 / math.sqrt(frames_here * owners)
    table = jnp.asarray(filter_table(channels))
    by_channel = jnp.swapaxes(gains, 1, 2)
    me = lax.axis_index("fgrp").astype(jnp.int32).reshape(1)
    own, left = [], []
    blocks = filter_part(me, voltages, table, by_channel, 0, rows, owners)
    for part in range(parts):
        received = [swapped(block, "fgrp", step) for step, block in enumerate(blocks)]
        if part + 1 < parts:
            blocks = filter_part(me, voltages, table, by_channel, part + 1, rows, owners)
            received, blocks = lax.optimization_barrier((received, blocks))
        merged, turned = merge(me, received, frames_here, share)
        own.append(merged)
        left.append(turned)
    tiles, pols = lax.axis_size("tile"), lax.axis_size("pol")
    if inputs_here % 128:
        wide = lax.all_gather(lax.all_gather(own[0], "pol", axis=0), "tile", axis=0)
        return correlate_whole(left[0], wide.reshape((-1,) + own[0].shape), share, norm)
    tile, pol = lax.axis_index("tile"), lax.axis_index("pol")

    def place(by_tile, by_pol):
        return (peer(tile, by_tile, tiles, -1) * pols + peer(pol, by_pol, pols, -1)).astype(jnp.int32)

    total = tiles * pols * inputs_here
    far = [[swapped(shard, "pol", by_pol) for shard in own] for by_pol in range(1, pols)]
    result = correlate(left, [own], place(0, 0).reshape(1), total, None, share, norm)
    far, result = lax.optimization_barrier((far, result))
    for by_pol in range(pols):
        near = own if by_pol == 0 else far[by_pol - 1]
        rights = [
            [swapped(shard, "tile", by_tile) for shard in near] for by_tile in range(tiles)
        ]
        steps = range(1 if by_pol == 0 else 0, tiles)
        result = correlate(
            left,
            [rights[step] for step in steps],
            jnp.stack([place(step, by_pol) for step in steps]),
            total,
            result,
            share,
            norm,
        )
    return result


def solution(mesh):
    placed = (P(None, ("tile", "pol"), "fgrp"), P(None, ("tile", "pol"), None))
    return jax.shard_map(
        body,
        mesh=mesh,
        in_specs=placed,
        out_specs=P("fgrp", None, ("tile", "pol"), None),
        check_vma=False,
    )
```

```python
import functools
import math

import jax
import jax.numpy as jnp
import ml_dtypes
import numpy as np
from jax import lax
from jax.experimental import pallas as pl
from jax.experimental.pallas import tpu as pltpu
from jax.sharding import PartitionSpec as P

NFFT = 4096
TAPS = 4
VMEM = 56 * 2**20


def filter_taps():
    span = TAPS * NFFT
    position = np.arange(span, dtype=np.float64)
    centred = (position - span / 2 + 0.5) / NFFT
    window = 0.5 - 0.5 * np.cos(2.0 * np.pi * (position + 0.5) / span)
    return (np.sinc(centred) * window).reshape(TAPS, NFFT)


def low_taps():
    energy = (filter_taps() ** 2).sum(axis=1)
    return [t for t in range(TAPS) if energy[t] > 0.01 * energy.sum()]


def filter_table(channels):
    phases = np.arange(NFFT)[:, None] * np.arange(channels)[None, :] % NFFT
    angles = phases * (2.0 * np.pi / NFFT)
    transform = np.concatenate([np.cos(angles), np.sin(angles)], axis=1) / math.sqrt(NFFT)
    blocks = [tap[:, None] * transform for tap in filter_taps()]
    high = [b.astype(np.float32).astype(ml_dtypes.bfloat16) for b in blocks]
    low = [
        (blocks[t] - high[t].astype(np.float64)).astype(np.float32).astype(ml_dtypes.bfloat16)
        for t in low_taps()
    ]
    return np.ascontiguousarray(np.concatenate(high + low, axis=1).T)


def peer(me, step, length, way):
    if length & (length - 1):
        return (me + way * step) % length
    return me ^ step


def filter_kernel(volt_ref, table_hbm, gain_ref, out_ref, sums, table, arrived):
    frame = pl.program_id(0)
    slots, _, width, rows = sums.shape
    half = width // 2
    pieces = arrived.shape[0]
    depth = table.shape[1] // pieces

    def fetch(piece):
        columns = pl.ds(piece * depth, depth)
        return pltpu.make_async_copy(
            table_hbm.at[:, columns], table.at[:, columns], arrived.at[piece]
        )

    def product(start, size):
        return lax.dot_general(
            table[:, start : start + size],
            volt_ref[:, :, start : start + size].reshape(2 * rows, size),
            (((1,), (1,)), ((), ())),
            preferred_element_type=jnp.float32,
        )

    def add(term):
        low = low_taps()
        for tap in range(TAPS):
            value = term[tap * width : (tap + 1) * width]
            if tap in low:
                at = (TAPS + low.index(tap)) * width
                value = value + term[at : at + width]
            for part in range(2):
                sums[frame + TAPS - 1 - tap, part] += value[:, part * rows : (part + 1) * rows]

    @pl.when(frame == 0)
    def _():
        for piece in range(pieces):
            fetch(piece).start()
        sums[...] = jnp.zeros_like(sums)
        for piece in range(pieces):
            fetch(piece).wait()
            add(product(piece * depth, depth))

    @pl.when(frame > 0)
    def _():
        add(product(0, table.shape[1]))

    @pl.when(frame == pl.num_programs(0) - 1)
    def _():
        owners = out_ref.shape[0]
        share = half // owners
        for slot in range(slots):
            real = sums[slot, 0, :half] + sums[slot, 1, half:]
            imag = sums[slot, 1, :half] - sums[slot, 0, half:]
            out_real = gain_ref[0] * real - gain_ref[1] * imag
            out_imag = gain_ref[0] * imag + gain_ref[1] * real
            for owner in range(owners):
                at = owner * share
                both = jnp.concatenate(
                    [out_real[at : at + share], out_imag[at : at + share]], axis=0
                )
                at = 2 * share * slot
                out_ref[owner, at : at + 2 * share, :] = both.astype(jnp.bfloat16)


def filter_all(voltages, table, gains, owners):
    rows = voltages.shape[1]
    frames = voltages.shape[2] // NFFT
    half = gains.shape[1]
    slots = frames + TAPS - 1
    out_rows = slots * 2 * half // owners
    columns = table.shape[0]
    pieces = 2
    return pl.pallas_call(
        filter_kernel,
        grid=(frames,),
        in_specs=[
            pl.BlockSpec((2, rows, NFFT), lambda f: (0, 0, f)),
            pl.BlockSpec(memory_space=pl.ANY),
            pl.BlockSpec((2, half, rows), lambda f: (0, 0, 0)),
        ],
        out_specs=pl.BlockSpec((owners, out_rows, rows), lambda f: (0, 0, 0)),
        out_shape=jax.ShapeDtypeStruct((owners, out_rows, rows), jnp.bfloat16),
        scratch_shapes=[
            pltpu.VMEM((slots, 2, 2 * half, rows), jnp.float32),
            pltpu.VMEM((columns, NFFT), jnp.bfloat16),
            pltpu.SemaphoreType.DMA((pieces,)),
        ],
        compiler_params=pltpu.CompilerParams(vmem_limit_bytes=VMEM),
        cost_estimate=pl.CostEstimate(
            flops=2 * 2 * rows * frames * NFFT * columns,
            bytes_accessed=2 * (2 * rows * frames * NFFT + NFFT * columns),
            transcendentals=0,
        ),
        name="filter_all",
    )(voltages, table, gains)


def merge_kernel(frames, share, norm, in_ref, out_ref, left_ref, scratch):
    owners = in_ref.shape[0]
    depth = 2 * owners * frames
    blocks = scratch.shape[0]
    for group in range(owners):
        for frame in range(frames):
            at = 2 * share * frame
            value = in_ref[group, at : at + 2 * share, :].astype(jnp.float32)
            if group > 0 and frame < TAPS - 1:
                at = 2 * share * (frame + frames)
                value = value + in_ref[group - 1, at : at + 2 * share, :].astype(jnp.float32)
            if value.shape[1] < 128 * blocks:
                spare = jnp.zeros((2 * share, 128 * blocks - value.shape[1]), jnp.float32)
                value = jnp.concatenate([value, spare], axis=1)
            for part in range(2):
                row = (part * owners + group) * frames + frame
                for block in range(blocks):
                    scratch[block, pl.ds(row, share, stride=depth), :] = value[
                        part * share : (part + 1) * share, block * 128 : (block + 1) * 128
                    ]
    for block in range(blocks):
        lanes = min(128, out_ref.shape[1] - block * 128)
        at = block * 128
        for channel in range(share):
            rounded = scratch[block, channel * depth : (channel + 1) * depth, :].astype(jnp.bfloat16)
            out_ref[channel * depth : (channel + 1) * depth, at : at + lanes] = rounded[:, :lanes]
            scaled = norm * rounded.astype(jnp.float32)
            high = scaled.astype(jnp.bfloat16).astype(jnp.float32)
            both = jnp.concatenate([high, scaled - high], axis=0).T
            left_ref[at : at + lanes, 2 * channel * depth : 2 * (channel + 1) * depth] = both[
                :lanes
            ].astype(jnp.bfloat16)


def merge(turned, frames, share, norm):
    owners, in_rows, rows = turned.shape
    out_rows = share * 2 * owners * frames
    return pl.pallas_call(
        functools.partial(merge_kernel, frames, share, norm),
        in_specs=[pl.BlockSpec(memory_space=pltpu.VMEM)],
        out_shape=[
            jax.ShapeDtypeStruct((out_rows, rows), jnp.bfloat16),
            jax.ShapeDtypeStruct((rows, 2 * out_rows), jnp.bfloat16),
        ],
        scratch_shapes=[pltpu.VMEM((pl.cdiv(rows, 128), out_rows, 128), jnp.float32)],
        compiler_params=pltpu.CompilerParams(vmem_limit_bytes=16 * 2**20),
        name="merge",
    )(turned)


def visibility(left, right):
    half = right.shape[0] // 2
    crossed = jnp.concatenate([-right[half:], right[:half]], axis=0)
    return [
        jnp.dot(
            left, jnp.concatenate([value, value], axis=0), preferred_element_type=jnp.float32
        )
        for value in (right, crossed)
    ]


def block_kernel(blocks, place_ref, left_ref, *refs):
    right_refs, out_ref = refs[:blocks], refs[-1]
    count = out_ref.shape[0]
    depth = right_refs[0].shape[0] // count
    for block in range(blocks):

        @pl.when(pl.program_id(1) == block)
        def _():
            for channel in range(count):
                out_ref[channel, 0], out_ref[channel, 1] = visibility(
                    left_ref[:, 2 * depth * channel : 2 * depth * (channel + 1)],
                    right_refs[block][depth * channel : depth * (channel + 1), :],
                )


def correlate(left, rights, places, total, result, share):
    blocks = len(rights)
    out_rows, rows = rights[0].shape
    depth = out_rows // share
    count = 2
    operands = [places, left, *rights]
    specs = [pl.BlockSpec((rows, 2 * depth * count), lambda c, b, places: (0, c))]
    specs += [pl.BlockSpec((depth * count, rows), lambda c, b, places: (c, 0))] * blocks
    aliases = {}
    if result is not None:
        aliases = {len(operands): 0}
        operands.append(result)
        specs.append(pl.BlockSpec(memory_space=pl.ANY))
    return pl.pallas_call(
        functools.partial(block_kernel, blocks),
        grid_spec=pltpu.PrefetchScalarGridSpec(
            num_scalar_prefetch=1,
            grid=(share // count, blocks),
            in_specs=specs,
            out_specs=pl.BlockSpec(
                (count, 2, rows, rows), lambda c, b, places: (c, 0, 0, places[b])
            ),
        ),
        out_shape=jax.ShapeDtypeStruct((share, 2, rows, total), jnp.float32),
        input_output_aliases=aliases,
        compiler_params=pltpu.CompilerParams(vmem_limit_bytes=24 * 2**20),
        cost_estimate=pl.CostEstimate(
            flops=8 * share * blocks * rows * rows * depth,
            bytes_accessed=4 * share * 2 * blocks * rows * rows,
            transcendentals=0,
        ),
        name="correlate",
    )(*operands)


def whole_kernel(left_ref, all_ref, out_ref):
    rows = left_ref.shape[0]
    for group in range(all_ref.shape[0]):
        values = visibility(left_ref[...], all_ref[group])
        for kind in range(2):
            out_ref[0, kind, :, group * rows : (group + 1) * rows] = values[kind]


def correlate_whole(left, gathered, share):
    groups, out_rows, rows = gathered.shape
    depth = out_rows // share
    return pl.pallas_call(
        whole_kernel,
        grid=(share,),
        in_specs=[
            pl.BlockSpec((rows, 2 * depth), lambda c: (0, c)),
            pl.BlockSpec((groups, depth, rows), lambda c: (0, c, 0)),
        ],
        out_specs=pl.BlockSpec((1, 2, rows, groups * rows), lambda c: (c, 0, 0, 0)),
        out_shape=jax.ShapeDtypeStruct((share, 2, rows, groups * rows), jnp.float32),
        compiler_params=pltpu.CompilerParams(vmem_limit_bytes=24 * 2**20),
        name="correlate_whole",
    )(left, gathered)


def swapped(shard, axis, step):
    if step == 0:
        return shard
    length = lax.axis_size(axis)
    return lax.ppermute(shard, axis, [(i, peer(i, step, length, 1)) for i in range(length)])


def body(voltages, gains):
    inputs_here = voltages.shape[1]
    frames_here = voltages.shape[2] // NFFT
    channels = gains.shape[2]
    owners = lax.axis_size("fgrp")
    share = channels // owners
    norm = 1.0 / math.sqrt(frames_here * owners)
    table = jnp.asarray(filter_table(channels))
    partial = filter_all(voltages, table, jnp.swapaxes(gains, 1, 2), owners)
    turned = lax.all_to_all(partial, "fgrp", split_axis=0, concat_axis=0, tiled=True)
    own, left = merge(turned, frames_here, share, norm)
    tiles, pols = lax.axis_size("tile"), lax.axis_size("pol")
    if inputs_here % 128:
        wide = lax.all_gather(lax.all_gather(own, "pol", axis=0), "tile", axis=0)
        return correlate_whole(left, wide.reshape((-1,) + own.shape), share)
    tile, pol = lax.axis_index("tile"), lax.axis_index("pol")

    def place(by_tile, by_pol):
        return (peer(tile, by_tile, tiles, -1) * pols + peer(pol, by_pol, pols, -1)).astype(jnp.int32)

    total = tiles * pols * inputs_here
    far = [swapped(own, "pol", by_pol) for by_pol in range(1, pols)]
    result = correlate(left, [own], place(0, 0).reshape(1), total, None, share)
    far, result = lax.optimization_barrier((far, result))
    for by_pol in range(pols):
        near = own if by_pol == 0 else far[by_pol - 1]
        rights = [swapped(near, "tile", by_tile) for by_tile in range(tiles)]
        steps = range(1 if by_pol == 0 else 0, tiles)
        result = correlate(
            left,
            [rights[step] for step in steps],
            jnp.stack([place(step, by_pol) for step in steps]),
            total,
            result,
            share,
        )
    return result


def solution(mesh):
    placed = (P(None, ("tile", "pol"), "fgrp"), P(None, ("tile", "pol"), None))
    return jax.shard_map(
        body,
        mesh=mesh,
        in_specs=placed,
        out_specs=P("fgrp", None, ("tile", "pol"), None),
        check_vma=False,
    )
```

```python
import functools
import math

import jax
import jax.numpy as jnp
import ml_dtypes
import numpy as np
from jax import lax
from jax.experimental import pallas as pl
from jax.experimental.pallas import tpu as pltpu
from jax.sharding import PartitionSpec as P

NFFT = 4096
TAPS = 4
VMEM = 56 * 2**20


def filter_taps():
    span = TAPS * NFFT
    position = np.arange(span, dtype=np.float64)
    centred = (position - span / 2 + 0.5) / NFFT
    window = 0.5 - 0.5 * np.cos(2.0 * np.pi * (position + 0.5) / span)
    return (np.sinc(centred) * window).reshape(TAPS, NFFT)


def tap_order():
    energy = (filter_taps() ** 2).sum(axis=1)
    order = list(range(TAPS))[::-1]
    return order, [t for t in order if energy[t] > 0.01 * energy.sum()]


def filter_table(channels):
    order, low_order = tap_order()
    phases = np.arange(NFFT)[:, None] * np.arange(channels)[None, :] % NFFT
    angles = phases * (2.0 * np.pi / NFFT)
    transform = np.concatenate([np.cos(angles), np.sin(angles)], axis=1) / math.sqrt(NFFT)
    blocks = {t: filter_taps()[t][:, None] * transform for t in order}
    high = {t: b.astype(np.float32).astype(ml_dtypes.bfloat16) for t, b in blocks.items()}
    low = [
        (blocks[t] - high[t].astype(np.float64)).astype(np.float32).astype(ml_dtypes.bfloat16)
        for t in low_order
    ]
    return np.ascontiguousarray(np.concatenate([high[t] for t in order] + low, axis=1).T)


def peer(me, step, length, way):
    if length & (length - 1):
        return (me + way * step) % length
    return me ^ step


def filter_kernel(volt_ref, table_hbm, gain_ref, out_ref, sums, low_sums, table, arrived):
    frame, part = pl.program_id(0), pl.program_id(1)
    rows = sums.shape[2]
    half = gain_ref.shape[1]
    width = 2 * half
    pieces = arrived.shape[0]
    depth = table.shape[1] // pieces
    order, low_order = tap_order()
    here = pl.ds(pl.multiple_of(frame * width, width), len(order) * width)
    low_here = pl.ds(pl.multiple_of(frame * width, width), len(low_order) * width)

    def fetch(piece):
        columns = pl.ds(piece * depth, depth)
        return pltpu.make_async_copy(
            table_hbm.at[:, columns], table.at[:, columns], arrived.at[piece]
        )

    def add(start, size):
        before = jnp.concatenate([sums[part, here, :], low_sums[part, low_here, :]], axis=0)
        after = before + lax.dot_general(
            table[:, start : start + size],
            volt_ref[0, :, start : start + size],
            (((1,), (1,)), ((), ())),
            preferred_element_type=jnp.float32,
        )
        sums[part, here, :] = after[: len(order) * width]
        low_sums[part, low_here, :] = after[len(order) * width :]

    first = (frame == 0) & (part == 0)

    @pl.when(first)
    def _():
        for piece in range(pieces):
            fetch(piece).start()
        sums[...] = jnp.zeros_like(sums)
        low_sums[...] = jnp.zeros_like(low_sums)
        for piece in range(pieces):
            fetch(piece).wait()
            add(piece * depth, depth)

    @pl.when(jnp.logical_not(first))
    def _():
        add(0, table.shape[1])

    @pl.when((frame == pl.num_programs(0) - 1) & (part == 1))
    def _():
        owners = out_ref.shape[0]
        share = half // owners
        for slot in range(sums.shape[1] // width):
            both = [sums[c, slot * width : (slot + 1) * width, :] for c in range(2)]
            at = (slot - order.index(low_order[0])) * width
            if 0 <= at < low_sums.shape[1]:
                both = [both[c] + low_sums[c, at : at + width, :] for c in range(2)]
            real = both[0][:half] + both[1][half:]
            imag = both[1][:half] - both[0][half:]
            out_real = gain_ref[0] * real - gain_ref[1] * imag
            out_imag = gain_ref[0] * imag + gain_ref[1] * real
            for owner in range(owners):
                at = owner * share
                pair = jnp.concatenate(
                    [out_real[at : at + share], out_imag[at : at + share]], axis=0
                )
                at = 2 * share * slot
                out_ref[owner, at : at + 2 * share, :] = pair.astype(jnp.bfloat16)


def filter_all(voltages, table, gains, owners):
    rows = voltages.shape[1]
    frames = voltages.shape[2] // NFFT
    half = gains.shape[1]
    slots = frames + TAPS - 1
    low_slots = frames + len(tap_order()[1]) - 1
    out_rows = slots * 2 * half // owners
    columns = table.shape[0]
    pieces = 4
    return pl.pallas_call(
        filter_kernel,
        grid=(frames, 2),
        in_specs=[
            pl.BlockSpec((1, rows, NFFT), lambda f, c: (c, 0, f)),
            pl.BlockSpec(memory_space=pl.ANY),
            pl.BlockSpec((2, half, rows), lambda f, c: (0, 0, 0)),
        ],
        out_specs=pl.BlockSpec((owners, out_rows, rows), lambda f, c: (0, 0, 0)),
        out_shape=jax.ShapeDtypeStruct((owners, out_rows, rows), jnp.bfloat16),
        scratch_shapes=[
            pltpu.VMEM((2, slots * 2 * half, rows), jnp.float32),
            pltpu.VMEM((2, low_slots * 2 * half, rows), jnp.float32),
            pltpu.VMEM((columns, NFFT), jnp.bfloat16),
            pltpu.SemaphoreType.DMA((pieces,)),
        ],
        compiler_params=pltpu.CompilerParams(vmem_limit_bytes=VMEM),
        cost_estimate=pl.CostEstimate(
            flops=2 * 2 * rows * frames * NFFT * columns,
            bytes_accessed=2 * (2 * rows * frames * NFFT + NFFT * columns),
            transcendentals=0,
        ),
        name="filter_all",
    )(voltages, table, gains)


def merge_kernel(frames, share, norm, in_ref, out_ref, left_ref, scratch):
    owners = in_ref.shape[0]
    depth = 2 * owners * frames
    blocks = scratch.shape[0]
    for group in range(owners):
        for frame in range(frames):
            at = 2 * share * frame
            value = in_ref[group, at : at + 2 * share, :].astype(jnp.float32)
            if group > 0 and frame < TAPS - 1:
                at = 2 * share * (frame + frames)
                value = value + in_ref[group - 1, at : at + 2 * share, :].astype(jnp.float32)
            if value.shape[1] < 128 * blocks:
                spare = jnp.zeros((2 * share, 128 * blocks - value.shape[1]), jnp.float32)
                value = jnp.concatenate([value, spare], axis=1)
            for part in range(2):
                row = (part * owners + group) * frames + frame
                for block in range(blocks):
                    scratch[block, pl.ds(row, share, stride=depth), :] = value[
                        part * share : (part + 1) * share, block * 128 : (block + 1) * 128
                    ]
    for block in range(blocks):
        lanes = min(128, out_ref.shape[1] - block * 128)
        at = block * 128
        for channel in range(share):
            rounded = scratch[block, channel * depth : (channel + 1) * depth, :].astype(jnp.bfloat16)
            out_ref[channel * depth : (channel + 1) * depth, at : at + lanes] = rounded[:, :lanes]
            scaled = norm * rounded.astype(jnp.float32)
            high = scaled.astype(jnp.bfloat16).astype(jnp.float32)
            both = jnp.concatenate([high, scaled - high], axis=0).T
            left_ref[at : at + lanes, 2 * channel * depth : 2 * (channel + 1) * depth] = both[
                :lanes
            ].astype(jnp.bfloat16)


def merge(turned, frames, share, norm):
    owners, in_rows, rows = turned.shape
    out_rows = share * 2 * owners * frames
    return pl.pallas_call(
        functools.partial(merge_kernel, frames, share, norm),
        in_specs=[pl.BlockSpec(memory_space=pltpu.VMEM)],
        out_shape=[
            jax.ShapeDtypeStruct((out_rows, rows), jnp.bfloat16),
            jax.ShapeDtypeStruct((rows, 2 * out_rows), jnp.bfloat16),
        ],
        scratch_shapes=[pltpu.VMEM((pl.cdiv(rows, 128), out_rows, 128), jnp.float32)],
        compiler_params=pltpu.CompilerParams(vmem_limit_bytes=16 * 2**20),
        name="merge",
    )(turned)


def visibility(left, right):
    half = right.shape[0] // 2
    crossed = jnp.concatenate([-right[half:], right[:half]], axis=0)
    return [
        jnp.dot(
            left, jnp.concatenate([value, value], axis=0), preferred_element_type=jnp.float32
        )
        for value in (right, crossed)
    ]


def block_kernel(blocks, place_ref, left_ref, *refs):
    right_refs, out_ref = refs[:blocks], refs[-1]
    count = out_ref.shape[0]
    depth = right_refs[0].shape[0] // count
    for block in range(blocks):

        @pl.when(pl.program_id(1) == block)
        def _():
            for channel in range(count):
                out_ref[channel, 0], out_ref[channel, 1] = visibility(
                    left_ref[:, 2 * depth * channel : 2 * depth * (channel + 1)],
                    right_refs[block][depth * channel : depth * (channel + 1), :],
                )


def correlate(left, rights, places, total, result, share):
    blocks = len(rights)
    out_rows, rows = rights[0].shape
    depth = out_rows // share
    count = 2
    operands = [places, left, *rights]
    specs = [pl.BlockSpec((rows, 2 * depth * count), lambda c, b, places: (0, c))]
    specs += [pl.BlockSpec((depth * count, rows), lambda c, b, places: (c, 0))] * blocks
    aliases = {}
    if result is not None:
        aliases = {len(operands): 0}
        operands.append(result)
        specs.append(pl.BlockSpec(memory_space=pl.ANY))
    return pl.pallas_call(
        functools.partial(block_kernel, blocks),
        grid_spec=pltpu.PrefetchScalarGridSpec(
            num_scalar_prefetch=1,
            grid=(share // count, blocks),
            in_specs=specs,
            out_specs=pl.BlockSpec(
                (count, 2, rows, rows), lambda c, b, places: (c, 0, 0, places[b])
            ),
        ),
        out_shape=jax.ShapeDtypeStruct((share, 2, rows, total), jnp.float32),
        input_output_aliases=aliases,
        compiler_params=pltpu.CompilerParams(vmem_limit_bytes=24 * 2**20),
        cost_estimate=pl.CostEstimate(
            flops=8 * share * blocks * rows * rows * depth,
            bytes_accessed=4 * share * 2 * blocks * rows * rows,
            transcendentals=0,
        ),
        name="correlate",
    )(*operands)


def whole_kernel(left_ref, all_ref, out_ref):
    rows = left_ref.shape[0]
    for group in range(all_ref.shape[0]):
        values = visibility(left_ref[...], all_ref[group])
        for kind in range(2):
            out_ref[0, kind, :, group * rows : (group + 1) * rows] = values[kind]


def correlate_whole(left, gathered, share):
    groups, out_rows, rows = gathered.shape
    depth = out_rows // share
    return pl.pallas_call(
        whole_kernel,
        grid=(share,),
        in_specs=[
            pl.BlockSpec((rows, 2 * depth), lambda c: (0, c)),
            pl.BlockSpec((groups, depth, rows), lambda c: (0, c, 0)),
        ],
        out_specs=pl.BlockSpec((1, 2, rows, groups * rows), lambda c: (c, 0, 0, 0)),
        out_shape=jax.ShapeDtypeStruct((share, 2, rows, groups * rows), jnp.float32),
        compiler_params=pltpu.CompilerParams(vmem_limit_bytes=24 * 2**20),
        name="correlate_whole",
    )(left, gathered)


def swapped(shard, axis, step):
    if step == 0:
        return shard
    length = lax.axis_size(axis)
    return lax.ppermute(shard, axis, [(i, peer(i, step, length, 1)) for i in range(length)])


def body(voltages, gains):
    inputs_here = voltages.shape[1]
    frames_here = voltages.shape[2] // NFFT
    channels = gains.shape[2]
    owners = lax.axis_size("fgrp")
    share = channels // owners
    norm = 1.0 / math.sqrt(frames_here * owners)
    table = jnp.asarray(filter_table(channels))
    partial = filter_all(voltages, table, jnp.swapaxes(gains, 1, 2), owners)
    turned = lax.all_to_all(partial, "fgrp", split_axis=0, concat_axis=0, tiled=True)
    own, left = merge(turned, frames_here, share, norm)
    tiles, pols = lax.axis_size("tile"), lax.axis_size("pol")
    if inputs_here % 128:
        wide = lax.all_gather(lax.all_gather(own, "pol", axis=0), "tile", axis=0)
        return correlate_whole(left, wide.reshape((-1,) + own.shape), share)
    tile, pol = lax.axis_index("tile"), lax.axis_index("pol")

    def place(by_tile, by_pol):
        return (peer(tile, by_tile, tiles, -1) * pols + peer(pol, by_pol, pols, -1)).astype(jnp.int32)

    total = tiles * pols * inputs_here
    result = None
    for by_pol in range(pols):
        near = swapped(own, "pol", by_pol)
        if by_pol:
            near, result = lax.optimization_barrier((near, result))
        for by_tile in range(tiles):
            right = swapped(near, "tile", by_tile)
            where = place(by_tile, by_pol).reshape(1)
            result = correlate(left, [right], where, total, result, share)
    return result


def solution(mesh):
    placed = (P(None, ("tile", "pol"), "fgrp"), P(None, ("tile", "pol"), None))
    return jax.shard_map(
        body,
        mesh=mesh,
        in_specs=placed,
        out_specs=P("fgrp", None, ("tile", "pol"), None),
        check_vma=False,
    )
```

```python
import functools
import math

import jax
import jax.numpy as jnp
import ml_dtypes
import numpy as np
from jax import lax
from jax.experimental import pallas as pl
from jax.experimental.pallas import tpu as pltpu
from jax.sharding import PartitionSpec as P

NFFT = 4096
TAPS = 4
VMEM = 56 * 2**20


def filter_taps():
    span = TAPS * NFFT
    position = np.arange(span, dtype=np.float64)
    centred = (position - span / 2 + 0.5) / NFFT
    window = 0.5 - 0.5 * np.cos(2.0 * np.pi * (position + 0.5) / span)
    return (np.sinc(centred) * window).reshape(TAPS, NFFT)


def tap_order():
    energy = (filter_taps() ** 2).sum(axis=1)
    order = list(range(TAPS))[::-1]
    return order, [t for t in order if energy[t] > 0.01 * energy.sum()]


def filter_table(channels):
    order, low_order = tap_order()
    phases = np.arange(NFFT)[:, None] * np.arange(channels)[None, :] % NFFT
    angles = phases * (2.0 * np.pi / NFFT)
    transform = np.concatenate([np.cos(angles), np.sin(angles)], axis=1) / math.sqrt(NFFT)
    blocks = {t: filter_taps()[t][:, None] * transform for t in order}
    high = {t: b.astype(np.float32).astype(ml_dtypes.bfloat16) for t, b in blocks.items()}
    low = [
        (blocks[t] - high[t].astype(np.float64)).astype(np.float32).astype(ml_dtypes.bfloat16)
        for t in low_order
    ]
    return np.concatenate([high[t] for t in order] + low, axis=1)


def peer(me, step, length, way):
    if length & (length - 1):
        return (me + way * step) % length
    return me ^ step


def filter_kernel(volt_ref, table_hbm, gain_ref, out_ref, sums, table, arrived):
    frame, part = pl.program_id(0), pl.program_id(1)
    width = sums.shape[3]
    half = width // 2
    pieces = arrived.shape[0]
    depth = table.shape[0] // pieces
    order, low_order = tap_order()

    def fetch(piece):
        rows = pl.ds(piece * depth, depth)
        return pltpu.make_async_copy(table_hbm.at[rows, :], table.at[rows, :], arrived.at[piece])

    def add(start, size):
        product = jnp.dot(
            volt_ref[0, :, start : start + size],
            table[start : start + size, :],
            preferred_element_type=jnp.float32,
        )
        for at, tap in enumerate(order):
            value = product[:, at * width : (at + 1) * width]
            if tap in low_order:
                low = (len(order) + low_order.index(tap)) * width
                value = value + product[:, low : low + width]
            sums[frame + at, part] += value

    first = (frame == 0) & (part == 0)

    @pl.when(first)
    def _():
        for piece in range(pieces):
            fetch(piece).start()
        sums[...] = jnp.zeros_like(sums)
        for piece in range(pieces):
            fetch(piece).wait()
            add(piece * depth, depth)

    @pl.when(jnp.logical_not(first))
    def _():
        add(0, table.shape[0])

    @pl.when((frame == pl.num_programs(0) - 1) & (part == 1))
    def _():
        owners = out_ref.shape[0]
        share = half // owners
        lane = lax.broadcasted_iota(jnp.int32, sums.shape[2:], 1)
        for slot in range(sums.shape[0]):
            first_part, second = sums[slot, 0], pltpu.roll(sums[slot, 1], half, 1)
            raw = jnp.where(lane < half, second + first_part, second - first_part).T
            real, imag = raw[:half], raw[half:]
            out_real = gain_ref[0] * real - gain_ref[1] * imag
            out_imag = gain_ref[0] * imag + gain_ref[1] * real
            for owner in range(owners):
                at = owner * share
                pair = jnp.concatenate(
                    [out_real[at : at + share], out_imag[at : at + share]], axis=0
                )
                at = 2 * share * slot
                out_ref[owner, at : at + 2 * share, :] = pair.astype(jnp.bfloat16)


def filter_all(voltages, table, gains, owners):
    rows = voltages.shape[1]
    frames = voltages.shape[2] // NFFT
    half = gains.shape[1]
    slots = frames + TAPS - 1
    out_rows = slots * 2 * half // owners
    columns = table.shape[1]
    pieces = 4
    return pl.pallas_call(
        filter_kernel,
        grid=(frames, 2),
        in_specs=[
            pl.BlockSpec((1, rows, NFFT), lambda f, c: (c, 0, f)),
            pl.BlockSpec(memory_space=pl.ANY),
            pl.BlockSpec((2, half, rows), lambda f, c: (0, 0, 0)),
        ],
        out_specs=pl.BlockSpec((owners, out_rows, rows), lambda f, c: (0, 0, 0)),
        out_shape=jax.ShapeDtypeStruct((owners, out_rows, rows), jnp.bfloat16),
        scratch_shapes=[
            pltpu.VMEM((slots, 2, rows, 2 * half), jnp.float32),
            pltpu.VMEM((NFFT, columns), jnp.bfloat16),
            pltpu.SemaphoreType.DMA((pieces,)),
        ],
        compiler_params=pltpu.CompilerParams(vmem_limit_bytes=VMEM),
        cost_estimate=pl.CostEstimate(
            flops=2 * 2 * rows * frames * NFFT * columns,
            bytes_accessed=2 * (2 * rows * frames * NFFT + NFFT * columns),
            transcendentals=0,
        ),
        name="filter_all",
    )(voltages, table, gains)


def merge_kernel(frames, share, norm, in_ref, out_ref, left_ref, scratch):
    owners = in_ref.shape[0]
    depth = 2 * owners * frames
    blocks = scratch.shape[0]
    for group in range(owners):
        for frame in range(frames):
            at = 2 * share * frame
            value = in_ref[group, at : at + 2 * share, :].astype(jnp.float32)
            if group > 0 and frame < TAPS - 1:
                at = 2 * share * (frame + frames)
                value = value + in_ref[group - 1, at : at + 2 * share, :].astype(jnp.float32)
            if value.shape[1] < 128 * blocks:
                spare = jnp.zeros((2 * share, 128 * blocks - value.shape[1]), jnp.float32)
                value = jnp.concatenate([value, spare], axis=1)
            for part in range(2):
                row = (part * owners + group) * frames + frame
                for block in range(blocks):
                    scratch[block, pl.ds(row, share, stride=depth), :] = value[
                        part * share : (part + 1) * share, block * 128 : (block + 1) * 128
                    ]
    for block in range(blocks):
        lanes = min(128, out_ref.shape[1] - block * 128)
        at = block * 128
        for channel in range(share):
            rounded = scratch[block, channel * depth : (channel + 1) * depth, :].astype(jnp.bfloat16)
            out_ref[channel * depth : (channel + 1) * depth, at : at + lanes] = rounded[:, :lanes]
            scaled = norm * rounded.astype(jnp.float32)
            high = scaled.astype(jnp.bfloat16).astype(jnp.float32)
            both = jnp.concatenate([high, scaled - high], axis=0).T
            left_ref[at : at + lanes, 2 * channel * depth : 2 * (channel + 1) * depth] = both[
                :lanes
            ].astype(jnp.bfloat16)


def merge(turned, frames, share, norm):
    owners, in_rows, rows = turned.shape
    out_rows = share * 2 * owners * frames
    return pl.pallas_call(
        functools.partial(merge_kernel, frames, share, norm),
        in_specs=[pl.BlockSpec(memory_space=pltpu.VMEM)],
        out_shape=[
            jax.ShapeDtypeStruct((out_rows, rows), jnp.bfloat16),
            jax.ShapeDtypeStruct((rows, 2 * out_rows), jnp.bfloat16),
        ],
        scratch_shapes=[pltpu.VMEM((pl.cdiv(rows, 128), out_rows, 128), jnp.float32)],
        compiler_params=pltpu.CompilerParams(vmem_limit_bytes=16 * 2**20),
        name="merge",
    )(turned)


def visibility(left, right):
    half = right.shape[0] // 2
    crossed = jnp.concatenate([-right[half:], right[:half]], axis=0)
    return [
        jnp.dot(
            left, jnp.concatenate([value, value], axis=0), preferred_element_type=jnp.float32
        )
        for value in (right, crossed)
    ]


def block_kernel(blocks, place_ref, left_ref, *refs):
    right_refs, out_ref = refs[:blocks], refs[-1]
    count = out_ref.shape[0]
    depth = right_refs[0].shape[0] // count
    for block in range(blocks):

        @pl.when(pl.program_id(1) == block)
        def _():
            for channel in range(count):
                out_ref[channel, 0], out_ref[channel, 1] = visibility(
                    left_ref[:, 2 * depth * channel : 2 * depth * (channel + 1)],
                    right_refs[block][depth * channel : depth * (channel + 1), :],
                )


def correlate(left, rights, places, total, result, share):
    blocks = len(rights)
    out_rows, rows = rights[0].shape
    depth = out_rows // share
    count = 2
    operands = [places, left, *rights]
    specs = [pl.BlockSpec((rows, 2 * depth * count), lambda c, b, places: (0, c))]
    specs += [pl.BlockSpec((depth * count, rows), lambda c, b, places: (c, 0))] * blocks
    aliases = {}
    if result is not None:
        aliases = {len(operands): 0}
        operands.append(result)
        specs.append(pl.BlockSpec(memory_space=pl.ANY))
    return pl.pallas_call(
        functools.partial(block_kernel, blocks),
        grid_spec=pltpu.PrefetchScalarGridSpec(
            num_scalar_prefetch=1,
            grid=(share // count, blocks),
            in_specs=specs,
            out_specs=pl.BlockSpec(
                (count, 2, rows, rows), lambda c, b, places: (c, 0, 0, places[b])
            ),
        ),
        out_shape=jax.ShapeDtypeStruct((share, 2, rows, total), jnp.float32),
        input_output_aliases=aliases,
        compiler_params=pltpu.CompilerParams(vmem_limit_bytes=24 * 2**20),
        cost_estimate=pl.CostEstimate(
            flops=8 * share * blocks * rows * rows * depth,
            bytes_accessed=4 * share * 2 * blocks * rows * rows,
            transcendentals=0,
        ),
        name="correlate",
    )(*operands)


def whole_kernel(left_ref, all_ref, out_ref):
    rows = left_ref.shape[0]
    for group in range(all_ref.shape[0]):
        values = visibility(left_ref[...], all_ref[group])
        for kind in range(2):
            out_ref[0, kind, :, group * rows : (group + 1) * rows] = values[kind]


def correlate_whole(left, gathered, share):
    groups, out_rows, rows = gathered.shape
    depth = out_rows // share
    return pl.pallas_call(
        whole_kernel,
        grid=(share,),
        in_specs=[
            pl.BlockSpec((rows, 2 * depth), lambda c: (0, c)),
            pl.BlockSpec((groups, depth, rows), lambda c: (0, c, 0)),
        ],
        out_specs=pl.BlockSpec((1, 2, rows, groups * rows), lambda c: (c, 0, 0, 0)),
        out_shape=jax.ShapeDtypeStruct((share, 2, rows, groups * rows), jnp.float32),
        compiler_params=pltpu.CompilerParams(vmem_limit_bytes=24 * 2**20),
        name="correlate_whole",
    )(left, gathered)


def swapped(shard, axis, step):
    if step == 0:
        return shard
    length = lax.axis_size(axis)
    return lax.ppermute(shard, axis, [(i, peer(i, step, length, 1)) for i in range(length)])


def body(voltages, gains):
    inputs_here = voltages.shape[1]
    frames_here = voltages.shape[2] // NFFT
    channels = gains.shape[2]
    owners = lax.axis_size("fgrp")
    share = channels // owners
    norm = 1.0 / math.sqrt(frames_here * owners)
    table = jnp.asarray(filter_table(channels))
    partial = filter_all(voltages, table, jnp.swapaxes(gains, 1, 2), owners)
    turned = lax.all_to_all(partial, "fgrp", split_axis=0, concat_axis=0, tiled=True)
    own, left = merge(turned, frames_here, share, norm)
    tiles, pols = lax.axis_size("tile"), lax.axis_size("pol")
    if inputs_here % 128:
        wide = lax.all_gather(lax.all_gather(own, "pol", axis=0), "tile", axis=0)
        return correlate_whole(left, wide.reshape((-1,) + own.shape), share)
    tile, pol = lax.axis_index("tile"), lax.axis_index("pol")

    def place(by_tile, by_pol):
        return (peer(tile, by_tile, tiles, -1) * pols + peer(pol, by_pol, pols, -1)).astype(jnp.int32)

    total = tiles * pols * inputs_here
    result = None
    for by_pol in range(pols):
        near = swapped(own, "pol", by_pol)
        if by_pol:
            near, result = lax.optimization_barrier((near, result))
        for by_tile in range(tiles):
            right = swapped(near, "tile", by_tile)
            where = place(by_tile, by_pol).reshape(1)
            result = correlate(left, [right], where, total, result, share)
    return result


def solution(mesh):
    placed = (P(None, ("tile", "pol"), "fgrp"), P(None, ("tile", "pol"), None))
    return jax.shard_map(
        body,
        mesh=mesh,
        in_specs=placed,
        out_specs=P("fgrp", None, ("tile", "pol"), None),
        check_vma=False,
    )
```

```python
import functools
import math

import jax
import jax.numpy as jnp
import ml_dtypes
import numpy as np
from jax import lax
from jax.experimental import pallas as pl
from jax.experimental.pallas import tpu as pltpu
from jax.sharding import PartitionSpec as P

NFFT = 4096
TAPS = 4
VMEM = 56 * 2**20


def filter_taps():
    span = TAPS * NFFT
    position = np.arange(span, dtype=np.float64)
    centred = (position - span / 2 + 0.5) / NFFT
    window = 0.5 - 0.5 * np.cos(2.0 * np.pi * (position + 0.5) / span)
    return (np.sinc(centred) * window).reshape(TAPS, NFFT)


def tap_order():
    energy = (filter_taps() ** 2).sum(axis=1)
    order = list(range(TAPS))[::-1]
    return order, [t for t in order if energy[t] > 0.01 * energy.sum()]


def filter_table(channels):
    order, low_order = tap_order()
    phases = np.arange(NFFT)[:, None] * np.arange(channels)[None, :] % NFFT
    angles = phases * (2.0 * np.pi / NFFT)
    transform = np.concatenate([np.cos(angles), np.sin(angles)], axis=1) / math.sqrt(NFFT)
    blocks = {t: filter_taps()[t][:, None] * transform for t in order}
    high = {t: b.astype(np.float32).astype(ml_dtypes.bfloat16) for t, b in blocks.items()}
    low = [
        (blocks[t] - high[t].astype(np.float64)).astype(np.float32).astype(ml_dtypes.bfloat16)
        for t in low_order
    ]
    return np.concatenate([high[t] for t in order] + low, axis=1)


def peer(me, step, length, way):
    if length & (length - 1):
        return (me + way * step) % length
    return me ^ step


def combine_kernel(*refs):
    product_refs, gain_ref, out_ref = refs[:-2], refs[-2], refs[-1]
    half = gain_ref.shape[1]
    width = 2 * half
    owners = out_ref.shape[0]
    share = half // owners
    order, low_order = tap_order()
    frames = len(product_refs)

    def term(frame, at, part):
        value = product_refs[frame][part, :, at * width : (at + 1) * width]
        if order[at] in low_order:
            low = (len(order) + low_order.index(order[at])) * width
            value = value + product_refs[frame][part, :, low : low + width]
        return value

    lane = lax.broadcasted_iota(jnp.int32, (product_refs[0].shape[1], width), 1)
    for slot in range(frames + TAPS - 1):
        used = [f for f in range(frames) if 0 <= slot - f < TAPS]
        first, second = (sum(term(f, slot - f, part) for f in used) for part in range(2))
        second = pltpu.roll(second, half, 1)
        raw = jnp.where(lane < half, second + first, second - first).T
        real, imag = raw[:half], raw[half:]
        out_real = gain_ref[0] * real - gain_ref[1] * imag
        out_imag = gain_ref[0] * imag + gain_ref[1] * real
        for owner in range(owners):
            at = owner * share
            pair = jnp.concatenate([out_real[at : at + share], out_imag[at : at + share]], axis=0)
            at = 2 * share * slot
            out_ref[owner, at : at + 2 * share, :] = pair.astype(jnp.bfloat16)


def filter_all(voltages, table, gains, owners):
    rows = voltages.shape[1]
    frames = voltages.shape[2] // NFFT
    half = gains.shape[1]
    slots = frames + TAPS - 1
    out_rows = slots * 2 * half // owners
    products = [
        lax.dot_general(
            voltages[:, :, frame * NFFT : (frame + 1) * NFFT],
            table,
            (((2,), (0,)), ((), ())),
            preferred_element_type=jnp.float32,
        )
        for frame in range(frames)
    ]
    return pl.pallas_call(
        combine_kernel,
        in_specs=[pl.BlockSpec(memory_space=pltpu.VMEM)] * (frames + 1),
        out_shape=jax.ShapeDtypeStruct((owners, out_rows, rows), jnp.bfloat16),
        compiler_params=pltpu.CompilerParams(vmem_limit_bytes=24 * 2**20),
        name="combine",
    )(*products, gains)


def merge_kernel(frames, share, norm, in_ref, out_ref, left_ref, scratch):
    owners = in_ref.shape[0]
    depth = 2 * owners * frames
    blocks = scratch.shape[0]
    for group in range(owners):
        for frame in range(frames):
            at = 2 * share * frame
            value = in_ref[group, at : at + 2 * share, :].astype(jnp.float32)
            if group > 0 and frame < TAPS - 1:
                at = 2 * share * (frame + frames)
                value = value + in_ref[group - 1, at : at + 2 * share, :].astype(jnp.float32)
            if value.shape[1] < 128 * blocks:
                spare = jnp.zeros((2 * share, 128 * blocks - value.shape[1]), jnp.float32)
                value = jnp.concatenate([value, spare], axis=1)
            for part in range(2):
                row = (part * owners + group) * frames + frame
                for block in range(blocks):
                    scratch[block, pl.ds(row, share, stride=depth), :] = value[
                        part * share : (part + 1) * share, block * 128 : (block + 1) * 128
                    ]
    for block in range(blocks):
        lanes = min(128, out_ref.shape[1] - block * 128)
        at = block * 128
        for channel in range(share):
            rounded = scratch[block, channel * depth : (channel + 1) * depth, :].astype(jnp.bfloat16)
            out_ref[channel * depth : (channel + 1) * depth, at : at + lanes] = rounded[:, :lanes]
            scaled = norm * rounded.astype(jnp.float32)
            high = scaled.astype(jnp.bfloat16).astype(jnp.float32)
            both = jnp.concatenate([high, scaled - high], axis=0).T
            left_ref[at : at + lanes, 2 * channel * depth : 2 * (channel + 1) * depth] = both[
                :lanes
            ].astype(jnp.bfloat16)


def merge(turned, frames, share, norm):
    owners, in_rows, rows = turned.shape
    out_rows = share * 2 * owners * frames
    return pl.pallas_call(
        functools.partial(merge_kernel, frames, share, norm),
        in_specs=[pl.BlockSpec(memory_space=pltpu.VMEM)],
        out_shape=[
            jax.ShapeDtypeStruct((out_rows, rows), jnp.bfloat16),
            jax.ShapeDtypeStruct((rows, 2 * out_rows), jnp.bfloat16),
        ],
        scratch_shapes=[pltpu.VMEM((pl.cdiv(rows, 128), out_rows, 128), jnp.float32)],
        compiler_params=pltpu.CompilerParams(vmem_limit_bytes=16 * 2**20),
        name="merge",
    )(turned)


def visibility(left, right):
    half = right.shape[0] // 2
    crossed = jnp.concatenate([-right[half:], right[:half]], axis=0)
    return [
        jnp.dot(
            left, jnp.concatenate([value, value], axis=0), preferred_element_type=jnp.float32
        )
        for value in (right, crossed)
    ]


def block_kernel(blocks, place_ref, left_ref, *refs):
    right_refs, out_ref = refs[:blocks], refs[-1]
    count = out_ref.shape[0]
    depth = right_refs[0].shape[0] // count
    for block in range(blocks):

        @pl.when(pl.program_id(1) == block)
        def _():
            for channel in range(count):
                out_ref[channel, 0], out_ref[channel, 1] = visibility(
                    left_ref[:, 2 * depth * channel : 2 * depth * (channel + 1)],
                    right_refs[block][depth * channel : depth * (channel + 1), :],
                )


def correlate(left, rights, places, total, result, share):
    blocks = len(rights)
    out_rows, rows = rights[0].shape
    depth = out_rows // share
    count = 2
    operands = [places, left, *rights]
    specs = [pl.BlockSpec((rows, 2 * depth * count), lambda c, b, places: (0, c))]
    specs += [pl.BlockSpec((depth * count, rows), lambda c, b, places: (c, 0))] * blocks
    aliases = {}
    if result is not None:
        aliases = {len(operands): 0}
        operands.append(result)
        specs.append(pl.BlockSpec(memory_space=pl.ANY))
    return pl.pallas_call(
        functools.partial(block_kernel, blocks),
        grid_spec=pltpu.PrefetchScalarGridSpec(
            num_scalar_prefetch=1,
            grid=(share // count, blocks),
            in_specs=specs,
            out_specs=pl.BlockSpec(
                (count, 2, rows, rows), lambda c, b, places: (c, 0, 0, places[b])
            ),
        ),
        out_shape=jax.ShapeDtypeStruct((share, 2, rows, total), jnp.float32),
        input_output_aliases=aliases,
        compiler_params=pltpu.CompilerParams(vmem_limit_bytes=24 * 2**20),
        cost_estimate=pl.CostEstimate(
            flops=8 * share * blocks * rows * rows * depth,
            bytes_accessed=4 * share * 2 * blocks * rows * rows,
            transcendentals=0,
        ),
        name="correlate",
    )(*operands)


def whole_kernel(left_ref, all_ref, out_ref):
    rows = left_ref.shape[0]
    for group in range(all_ref.shape[0]):
        values = visibility(left_ref[...], all_ref[group])
        for kind in range(2):
            out_ref[0, kind, :, group * rows : (group + 1) * rows] = values[kind]


def correlate_whole(left, gathered, share):
    groups, out_rows, rows = gathered.shape
    depth = out_rows // share
    return pl.pallas_call(
        whole_kernel,
        grid=(share,),
        in_specs=[
            pl.BlockSpec((rows, 2 * depth), lambda c: (0, c)),
            pl.BlockSpec((groups, depth, rows), lambda c: (0, c, 0)),
        ],
        out_specs=pl.BlockSpec((1, 2, rows, groups * rows), lambda c: (c, 0, 0, 0)),
        out_shape=jax.ShapeDtypeStruct((share, 2, rows, groups * rows), jnp.float32),
        compiler_params=pltpu.CompilerParams(vmem_limit_bytes=24 * 2**20),
        name="correlate_whole",
    )(left, gathered)


def swapped(shard, axis, step):
    if step == 0:
        return shard
    length = lax.axis_size(axis)
    return lax.ppermute(shard, axis, [(i, peer(i, step, length, 1)) for i in range(length)])


def body(voltages, gains):
    inputs_here = voltages.shape[1]
    frames_here = voltages.shape[2] // NFFT
    channels = gains.shape[2]
    owners = lax.axis_size("fgrp")
    share = channels // owners
    norm = 1.0 / math.sqrt(frames_here * owners)
    table = jnp.asarray(filter_table(channels))
    partial = filter_all(voltages, table, jnp.swapaxes(gains, 1, 2), owners)
    turned = lax.all_to_all(partial, "fgrp", split_axis=0, concat_axis=0, tiled=True)
    own, left = merge(turned, frames_here, share, norm)
    tiles, pols = lax.axis_size("tile"), lax.axis_size("pol")
    if inputs_here % 128:
        wide = lax.all_gather(lax.all_gather(own, "pol", axis=0), "tile", axis=0)
        return correlate_whole(left, wide.reshape((-1,) + own.shape), share)
    tile, pol = lax.axis_index("tile"), lax.axis_index("pol")

    def place(by_tile, by_pol):
        return (peer(tile, by_tile, tiles, -1) * pols + peer(pol, by_pol, pols, -1)).astype(jnp.int32)

    total = tiles * pols * inputs_here
    result = None
    for by_pol in range(pols):
        near = swapped(own, "pol", by_pol)
        if by_pol:
            near, result = lax.optimization_barrier((near, result))
        for by_tile in range(tiles):
            right = swapped(near, "tile", by_tile)
            where = place(by_tile, by_pol).reshape(1)
            result = correlate(left, [right], where, total, result, share)
    return result


def solution(mesh):
    placed = (P(None, ("tile", "pol"), "fgrp"), P(None, ("tile", "pol"), None))
    return jax.shard_map(
        body,
        mesh=mesh,
        in_specs=placed,
        out_specs=P("fgrp", None, ("tile", "pol"), None),
        check_vma=False,
    )
```

```python
import functools
import math

import jax
import jax.numpy as jnp
import ml_dtypes
import numpy as np
from jax import lax
from jax.experimental import pallas as pl
from jax.experimental.pallas import tpu as pltpu
from jax.sharding import PartitionSpec as P

NFFT = 4096
TAPS = 4
VMEM = 56 * 2**20


def filter_taps():
    span = TAPS * NFFT
    position = np.arange(span, dtype=np.float64)
    centred = (position - span / 2 + 0.5) / NFFT
    window = 0.5 - 0.5 * np.cos(2.0 * np.pi * (position + 0.5) / span)
    return (np.sinc(centred) * window).reshape(TAPS, NFFT)


def tap_order():
    energy = (filter_taps() ** 2).sum(axis=1)
    order = list(range(TAPS))[::-1]
    return order, [t for t in order if energy[t] > 0.01 * energy.sum()]


def filter_table(channels):
    order, low_order = tap_order()
    phases = np.arange(NFFT)[:, None] * np.arange(channels)[None, :] % NFFT
    angles = phases * (2.0 * np.pi / NFFT)
    transform = np.concatenate([np.cos(angles), np.sin(angles)], axis=1) / math.sqrt(NFFT)
    blocks = {t: filter_taps()[t][:, None] * transform for t in order}
    high = {t: b.astype(np.float32).astype(ml_dtypes.bfloat16) for t, b in blocks.items()}
    low = np.concatenate([blocks[t] - high[t].astype(np.float64) for t in low_order], axis=1)
    scale = 2.0 ** np.floor(np.log2(256.0 / np.abs(low).max()))
    low = (low * scale).astype(np.float32).astype(ml_dtypes.float8_e4m3fn)
    high = np.concatenate([high[t] for t in order], axis=1)
    return np.ascontiguousarray(high.T), np.ascontiguousarray(low.T), float(1.0 / scale)


def peer(me, step, length, way):
    if length & (length - 1):
        return (me + way * step) % length
    return me ^ step


def filter_kernel(
    low_scale, volt_ref, table_hbm, low_ref, gain_ref, out_ref, sums, low_sums, table, arrived
):
    frame, part = pl.program_id(0), pl.program_id(1)
    rows = sums.shape[2]
    half = gain_ref.shape[1]
    width = 2 * half
    pieces = arrived.shape[0]
    depth = table.shape[1] // pieces
    order, low_order = tap_order()
    here = pl.ds(pl.multiple_of(frame * width, width), len(order) * width)
    low_here = pl.ds(pl.multiple_of(frame * width, width), len(low_order) * width)

    def fetch(piece):
        columns = pl.ds(piece * depth, depth)
        return pltpu.make_async_copy(
            table_hbm.at[:, columns], table.at[:, columns], arrived.at[piece]
        )

    def product(left, right):
        return lax.dot_general(
            left, right, (((1,), (1,)), ((), ())), preferred_element_type=jnp.float32
        )

    def add(start, size):
        volts = volt_ref[0, :, start : start + size]
        sums[part, here, :] += product(table[:, start : start + size], volts)
        low_sums[part, low_here, :] += product(
            low_ref[:, start : start + size], volts.astype(jnp.float8_e4m3fn)
        )

    first = (frame == 0) & (part == 0)

    @pl.when(first)
    def _():
        for piece in range(pieces):
            fetch(piece).start()
        sums[...] = jnp.zeros_like(sums)
        low_sums[...] = jnp.zeros_like(low_sums)
        for piece in range(pieces):
            fetch(piece).wait()
            add(piece * depth, depth)

    @pl.when(jnp.logical_not(first))
    def _():
        add(0, table.shape[1])

    @pl.when((frame == pl.num_programs(0) - 1) & (part == 1))
    def _():
        owners = out_ref.shape[0]
        share = half // owners
        for slot in range(sums.shape[1] // width):
            both = [sums[c, slot * width : (slot + 1) * width, :] for c in range(2)]
            at = (slot - order.index(low_order[0])) * width
            if 0 <= at < low_sums.shape[1]:
                both = [both[c] + low_scale * low_sums[c, at : at + width, :] for c in range(2)]
            real = both[0][:half] + both[1][half:]
            imag = both[1][:half] - both[0][half:]
            out_real = gain_ref[0] * real - gain_ref[1] * imag
            out_imag = gain_ref[0] * imag + gain_ref[1] * real
            for owner in range(owners):
                at = owner * share
                pair = jnp.concatenate(
                    [out_real[at : at + share], out_imag[at : at + share]], axis=0
                )
                at = 2 * share * slot
                out_ref[owner, at : at + 2 * share, :] = pair.astype(jnp.bfloat16)


def filter_all(voltages, tables, gains, owners):
    rows = voltages.shape[1]
    frames = voltages.shape[2] // NFFT
    half = gains.shape[1]
    slots = frames + TAPS - 1
    low_slots = frames + len(tap_order()[1]) - 1
    out_rows = slots * 2 * half // owners
    table, low_table, low_scale = tables
    columns = table.shape[0]
    pieces = 4
    return pl.pallas_call(
        functools.partial(filter_kernel, low_scale),
        grid=(frames, 2),
        in_specs=[
            pl.BlockSpec((1, rows, NFFT), lambda f, c: (c, 0, f)),
            pl.BlockSpec(memory_space=pl.ANY),
            pl.BlockSpec(low_table.shape, lambda f, c: (0, 0)),
            pl.BlockSpec((2, half, rows), lambda f, c: (0, 0, 0)),
        ],
        out_specs=pl.BlockSpec((owners, out_rows, rows), lambda f, c: (0, 0, 0)),
        out_shape=jax.ShapeDtypeStruct((owners, out_rows, rows), jnp.bfloat16),
        scratch_shapes=[
            pltpu.VMEM((2, slots * 2 * half, rows), jnp.float32),
            pltpu.VMEM((2, low_slots * 2 * half, rows), jnp.float32),
            pltpu.VMEM((columns, NFFT), jnp.bfloat16),
            pltpu.SemaphoreType.DMA((pieces,)),
        ],
        compiler_params=pltpu.CompilerParams(vmem_limit_bytes=VMEM),
        cost_estimate=pl.CostEstimate(
            flops=2 * 2 * rows * frames * NFFT * columns,
            bytes_accessed=2 * (2 * rows * frames * NFFT + NFFT * columns),
            transcendentals=0,
        ),
        name="filter_all",
    )(voltages, jnp.asarray(table), jnp.asarray(low_table), gains)


def merge_kernel(frames, share, norm, in_ref, out_ref, left_ref, scratch):
    owners = in_ref.shape[0]
    depth = 2 * owners * frames
    blocks = scratch.shape[0]
    for group in range(owners):
        for frame in range(frames):
            at = 2 * share * frame
            value = in_ref[group, at : at + 2 * share, :].astype(jnp.float32)
            if group > 0 and frame < TAPS - 1:
                at = 2 * share * (frame + frames)
                value = value + in_ref[group - 1, at : at + 2 * share, :].astype(jnp.float32)
            if value.shape[1] < 128 * blocks:
                spare = jnp.zeros((2 * share, 128 * blocks - value.shape[1]), jnp.float32)
                value = jnp.concatenate([value, spare], axis=1)
            for part in range(2):
                row = (part * owners + group) * frames + frame
                for block in range(blocks):
                    scratch[block, pl.ds(row, share, stride=depth), :] = value[
                        part * share : (part + 1) * share, block * 128 : (block + 1) * 128
                    ]
    for block in range(blocks):
        lanes = min(128, out_ref.shape[1] - block * 128)
        at = block * 128
        for channel in range(share):
            rounded = scratch[block, channel * depth : (channel + 1) * depth, :].astype(jnp.bfloat16)
            out_ref[channel * depth : (channel + 1) * depth, at : at + lanes] = rounded[:, :lanes]
            scaled = norm * rounded.astype(jnp.float32)
            high = scaled.astype(jnp.bfloat16).astype(jnp.float32)
            both = jnp.concatenate([high, scaled - high], axis=0).T
            left_ref[at : at + lanes, 2 * channel * depth : 2 * (channel + 1) * depth] = both[
                :lanes
            ].astype(jnp.bfloat16)


def merge(turned, frames, share, norm):
    owners, in_rows, rows = turned.shape
    out_rows = share * 2 * owners * frames
    return pl.pallas_call(
        functools.partial(merge_kernel, frames, share, norm),
        in_specs=[pl.BlockSpec(memory_space=pltpu.VMEM)],
        out_shape=[
            jax.ShapeDtypeStruct((out_rows, rows), jnp.bfloat16),
            jax.ShapeDtypeStruct((rows, 2 * out_rows), jnp.bfloat16),
        ],
        scratch_shapes=[pltpu.VMEM((pl.cdiv(rows, 128), out_rows, 128), jnp.float32)],
        compiler_params=pltpu.CompilerParams(vmem_limit_bytes=16 * 2**20),
        name="merge",
    )(turned)


def visibility(left, right):
    half = right.shape[0] // 2
    crossed = jnp.concatenate([-right[half:], right[:half]], axis=0)
    return [
        jnp.dot(
            left, jnp.concatenate([value, value], axis=0), preferred_element_type=jnp.float32
        )
        for value in (right, crossed)
    ]


def block_kernel(blocks, place_ref, left_ref, *refs):
    right_refs, out_ref = refs[:blocks], refs[-1]
    count = out_ref.shape[0]
    depth = right_refs[0].shape[0] // count
    for block in range(blocks):

        @pl.when(pl.program_id(1) == block)
        def _():
            for channel in range(count):
                out_ref[channel, 0], out_ref[channel, 1] = visibility(
                    left_ref[:, 2 * depth * channel : 2 * depth * (channel + 1)],
                    right_refs[block][depth * channel : depth * (channel + 1), :],
                )


def correlate(left, rights, places, total, result, share):
    blocks = len(rights)
    out_rows, rows = rights[0].shape
    depth = out_rows // share
    count = 2
    operands = [places, left, *rights]
    specs = [pl.BlockSpec((rows, 2 * depth * count), lambda c, b, places: (0, c))]
    specs += [pl.BlockSpec((depth * count, rows), lambda c, b, places: (c, 0))] * blocks
    aliases = {}
    if result is not None:
        aliases = {len(operands): 0}
        operands.append(result)
        specs.append(pl.BlockSpec(memory_space=pl.ANY))
    return pl.pallas_call(
        functools.partial(block_kernel, blocks),
        grid_spec=pltpu.PrefetchScalarGridSpec(
            num_scalar_prefetch=1,
            grid=(share // count, blocks),
            in_specs=specs,
            out_specs=pl.BlockSpec(
                (count, 2, rows, rows), lambda c, b, places: (c, 0, 0, places[b])
            ),
        ),
        out_shape=jax.ShapeDtypeStruct((share, 2, rows, total), jnp.float32),
        input_output_aliases=aliases,
        compiler_params=pltpu.CompilerParams(vmem_limit_bytes=24 * 2**20),
        cost_estimate=pl.CostEstimate(
            flops=8 * share * blocks * rows * rows * depth,
            bytes_accessed=4 * share * 2 * blocks * rows * rows,
            transcendentals=0,
        ),
        name="correlate",
    )(*operands)


def whole_kernel(left_ref, all_ref, out_ref):
    rows = left_ref.shape[0]
    for group in range(all_ref.shape[0]):
        values = visibility(left_ref[...], all_ref[group])
        for kind in range(2):
            out_ref[0, kind, :, group * rows : (group + 1) * rows] = values[kind]


def correlate_whole(left, gathered, share):
    groups, out_rows, rows = gathered.shape
    depth = out_rows // share
    return pl.pallas_call(
        whole_kernel,
        grid=(share,),
        in_specs=[
            pl.BlockSpec((rows, 2 * depth), lambda c: (0, c)),
            pl.BlockSpec((groups, depth, rows), lambda c: (0, c, 0)),
        ],
        out_specs=pl.BlockSpec((1, 2, rows, groups * rows), lambda c: (c, 0, 0, 0)),
        out_shape=jax.ShapeDtypeStruct((share, 2, rows, groups * rows), jnp.float32),
        compiler_params=pltpu.CompilerParams(vmem_limit_bytes=24 * 2**20),
        name="correlate_whole",
    )(left, gathered)


def swapped(shard, axis, step):
    if step == 0:
        return shard
    length = lax.axis_size(axis)
    return lax.ppermute(shard, axis, [(i, peer(i, step, length, 1)) for i in range(length)])


def body(voltages, gains):
    inputs_here = voltages.shape[1]
    frames_here = voltages.shape[2] // NFFT
    channels = gains.shape[2]
    owners = lax.axis_size("fgrp")
    share = channels // owners
    norm = 1.0 / math.sqrt(frames_here * owners)
    partial = filter_all(voltages, filter_table(channels), jnp.swapaxes(gains, 1, 2), owners)
    turned = lax.all_to_all(partial, "fgrp", split_axis=0, concat_axis=0, tiled=True)
    own, left = merge(turned, frames_here, share, norm)
    tiles, pols = lax.axis_size("tile"), lax.axis_size("pol")
    if inputs_here % 128:
        wide = lax.all_gather(lax.all_gather(own, "pol", axis=0), "tile", axis=0)
        return correlate_whole(left, wide.reshape((-1,) + own.shape), share)
    tile, pol = lax.axis_index("tile"), lax.axis_index("pol")

    def place(by_tile, by_pol):
        return (peer(tile, by_tile, tiles, -1) * pols + peer(pol, by_pol, pols, -1)).astype(jnp.int32)

    total = tiles * pols * inputs_here
    result = None
    for by_pol in range(pols):
        near = swapped(own, "pol", by_pol)
        if by_pol:
            near, result = lax.optimization_barrier((near, result))
        for by_tile in range(tiles):
            right = swapped(near, "tile", by_tile)
            where = place(by_tile, by_pol).reshape(1)
            result = correlate(left, [right], where, total, result, share)
    return result


def solution(mesh):
    placed = (P(None, ("tile", "pol"), "fgrp"), P(None, ("tile", "pol"), None))
    return jax.shard_map(
        body,
        mesh=mesh,
        in_specs=placed,
        out_specs=P("fgrp", None, ("tile", "pol"), None),
        check_vma=False,
    )
```

```python
import functools
import math

import jax
import jax.numpy as jnp
import ml_dtypes
import numpy as np
from jax import lax
from jax.experimental import pallas as pl
from jax.experimental.pallas import tpu as pltpu
from jax.sharding import PartitionSpec as P

NFFT = 4096
TAPS = 4
VMEM = 56 * 2**20


def filter_taps():
    span = TAPS * NFFT
    position = np.arange(span, dtype=np.float64)
    centred = (position - span / 2 + 0.5) / NFFT
    window = 0.5 - 0.5 * np.cos(2.0 * np.pi * (position + 0.5) / span)
    return (np.sinc(centred) * window).reshape(TAPS, NFFT)


def tap_order():
    energy = (filter_taps() ** 2).sum(axis=1)
    order = list(range(TAPS))[::-1]
    return order, [t for t in order if energy[t] > 0.01 * energy.sum()]


def filter_table(channels):
    order, low_order = tap_order()
    phases = np.arange(NFFT)[:, None] * np.arange(channels)[None, :] % NFFT
    angles = phases * (2.0 * np.pi / NFFT)
    transform = np.concatenate([np.cos(angles), np.sin(angles)], axis=1) / math.sqrt(NFFT)
    blocks = {t: filter_taps()[t][:, None] * transform for t in order}
    high = {t: b.astype(np.float32).astype(ml_dtypes.bfloat16) for t, b in blocks.items()}
    low = np.concatenate([blocks[t] - high[t].astype(np.float64) for t in low_order], axis=1)
    scale = 2.0 ** np.floor(np.log2(256.0 / np.abs(low).max()))
    low = (low * scale).astype(np.float32).astype(ml_dtypes.float8_e4m3fn)
    high = np.concatenate([high[t] for t in order], axis=1)
    return np.ascontiguousarray(high.T), np.ascontiguousarray(low.T), float(1.0 / scale)


def peer(me, step, length, way):
    if length & (length - 1):
        return (me + way * step) % length
    return me ^ step


def filter_kernel(
    low_scale, volt_ref, table_hbm, low_ref, gain_ref, out_ref, sums, low_sums, table, arrived
):
    frame, part = pl.program_id(0), pl.program_id(1)
    rows = sums.shape[2]
    half = gain_ref.shape[1]
    width = 2 * half
    pieces = arrived.shape[0]
    depth = table.shape[1] // pieces
    order, low_order = tap_order()
    low_here = pl.ds(pl.multiple_of(frame * width, width), len(low_order) * width)

    def fetch(piece):
        columns = pl.ds(piece * depth, depth)
        return pltpu.make_async_copy(
            table_hbm.at[:, columns], table.at[:, columns], arrived.at[piece]
        )

    def product(left, right):
        return lax.dot_general(
            left, right, (((1,), (1,)), ((), ())), preferred_element_type=jnp.float32
        )

    def add(start, size):
        volts = volt_ref[0, :, start : start + size]
        for at in range(0, table.shape[0], 2 * width):
            to = pl.ds(pl.multiple_of(frame * width, width) + at, 2 * width)
            sums[part, to, :] += product(table[at : at + 2 * width, start : start + size], volts)
        low_sums[part, low_here, :] += product(
            low_ref[:, start : start + size], volts.astype(jnp.float8_e4m3fn)
        )

    first = (frame == 0) & (part == 0)

    @pl.when(first)
    def _():
        for piece in range(pieces):
            fetch(piece).start()
        sums[...] = jnp.zeros_like(sums)
        low_sums[...] = jnp.zeros_like(low_sums)
        for piece in range(pieces):
            fetch(piece).wait()
            add(piece * depth, depth)

    @pl.when(jnp.logical_not(first))
    def _():
        add(0, table.shape[1])

    @pl.when((frame == pl.num_programs(0) - 1) & (part == 1))
    def _():
        owners = out_ref.shape[0]
        share = half // owners
        for slot in range(sums.shape[1] // width):
            both = [sums[c, slot * width : (slot + 1) * width, :] for c in range(2)]
            at = (slot - order.index(low_order[0])) * width
            if 0 <= at < low_sums.shape[1]:
                both = [both[c] + low_scale * low_sums[c, at : at + width, :] for c in range(2)]
            real = both[0][:half] + both[1][half:]
            imag = both[1][:half] - both[0][half:]
            out_real = gain_ref[0] * real - gain_ref[1] * imag
            out_imag = gain_ref[0] * imag + gain_ref[1] * real
            for owner in range(owners):
                at = owner * share
                pair = jnp.concatenate(
                    [out_real[at : at + share], out_imag[at : at + share]], axis=0
                )
                at = 2 * share * slot
                out_ref[owner, at : at + 2 * share, :] = pair.astype(jnp.bfloat16)


def filter_all(voltages, tables, gains, owners):
    rows = voltages.shape[1]
    frames = voltages.shape[2] // NFFT
    half = gains.shape[1]
    slots = frames + TAPS - 1
    low_slots = frames + len(tap_order()[1]) - 1
    out_rows = slots * 2 * half // owners
    table, low_table, low_scale = tables
    columns = table.shape[0]
    pieces = 4
    return pl.pallas_call(
        functools.partial(filter_kernel, low_scale),
        grid=(frames, 2),
        in_specs=[
            pl.BlockSpec((1, rows, NFFT), lambda f, c: (c, 0, f)),
            pl.BlockSpec(memory_space=pl.ANY),
            pl.BlockSpec(low_table.shape, lambda f, c: (0, 0)),
            pl.BlockSpec((2, half, rows), lambda f, c: (0, 0, 0)),
        ],
        out_specs=pl.BlockSpec((owners, out_rows, rows), lambda f, c: (0, 0, 0)),
        out_shape=jax.ShapeDtypeStruct((owners, out_rows, rows), jnp.bfloat16),
        scratch_shapes=[
            pltpu.VMEM((2, slots * 2 * half, rows), jnp.float32),
            pltpu.VMEM((2, low_slots * 2 * half, rows), jnp.float32),
            pltpu.VMEM((columns, NFFT), jnp.bfloat16),
            pltpu.SemaphoreType.DMA((pieces,)),
        ],
        compiler_params=pltpu.CompilerParams(vmem_limit_bytes=VMEM),
        cost_estimate=pl.CostEstimate(
            flops=2 * 2 * rows * frames * NFFT * columns,
            bytes_accessed=2 * (2 * rows * frames * NFFT + NFFT * columns),
            transcendentals=0,
        ),
        name="filter_all",
    )(voltages, jnp.asarray(table), jnp.asarray(low_table), gains)


def merge_kernel(frames, share, norm, in_ref, out_ref, left_ref, scratch):
    owners = in_ref.shape[0]
    depth = 2 * owners * frames
    blocks = scratch.shape[0]
    for group in range(owners):
        for frame in range(frames):
            at = 2 * share * frame
            value = in_ref[group, at : at + 2 * share, :].astype(jnp.float32)
            if group > 0 and frame < TAPS - 1:
                at = 2 * share * (frame + frames)
                value = value + in_ref[group - 1, at : at + 2 * share, :].astype(jnp.float32)
            if value.shape[1] < 128 * blocks:
                spare = jnp.zeros((2 * share, 128 * blocks - value.shape[1]), jnp.float32)
                value = jnp.concatenate([value, spare], axis=1)
            for part in range(2):
                row = (part * owners + group) * frames + frame
                for block in range(blocks):
                    scratch[block, pl.ds(row, share, stride=depth), :] = value[
                        part * share : (part + 1) * share, block * 128 : (block + 1) * 128
                    ]
    for block in range(blocks):
        lanes = min(128, out_ref.shape[1] - block * 128)
        at = block * 128
        for channel in range(share):
            rounded = scratch[block, channel * depth : (channel + 1) * depth, :].astype(jnp.bfloat16)
            out_ref[channel * depth : (channel + 1) * depth, at : at + lanes] = rounded[:, :lanes]
            scaled = norm * rounded.astype(jnp.float32)
            high = scaled.astype(jnp.bfloat16).astype(jnp.float32)
            both = jnp.concatenate([high, scaled - high], axis=0).T
            left_ref[at : at + lanes, 2 * channel * depth : 2 * (channel + 1) * depth] = both[
                :lanes
            ].astype(jnp.bfloat16)


def merge(turned, frames, share, norm):
    owners, in_rows, rows = turned.shape
    out_rows = share * 2 * owners * frames
    return pl.pallas_call(
        functools.partial(merge_kernel, frames, share, norm),
        in_specs=[pl.BlockSpec(memory_space=pltpu.VMEM)],
        out_shape=[
            jax.ShapeDtypeStruct((out_rows, rows), jnp.bfloat16),
            jax.ShapeDtypeStruct((rows, 2 * out_rows), jnp.bfloat16),
        ],
        scratch_shapes=[pltpu.VMEM((pl.cdiv(rows, 128), out_rows, 128), jnp.float32)],
        compiler_params=pltpu.CompilerParams(vmem_limit_bytes=16 * 2**20),
        name="merge",
    )(turned)


def visibility(left, right):
    half = right.shape[0] // 2
    crossed = jnp.concatenate([-right[half:], right[:half]], axis=0)
    return [
        jnp.dot(
            left, jnp.concatenate([value, value], axis=0), preferred_element_type=jnp.float32
        )
        for value in (right, crossed)
    ]


def block_kernel(blocks, place_ref, left_ref, *refs):
    right_refs, out_ref = refs[:blocks], refs[-1]
    count = out_ref.shape[0]
    depth = right_refs[0].shape[0] // count
    for block in range(blocks):

        @pl.when(pl.program_id(1) == block)
        def _():
            for channel in range(count):
                out_ref[channel, 0], out_ref[channel, 1] = visibility(
                    left_ref[:, 2 * depth * channel : 2 * depth * (channel + 1)],
                    right_refs[block][depth * channel : depth * (channel + 1), :],
                )


def correlate(left, rights, places, total, result, share):
    blocks = len(rights)
    out_rows, rows = rights[0].shape
    depth = out_rows // share
    count = 1
    operands = [places, left, *rights]
    specs = [pl.BlockSpec((rows, 2 * depth * count), lambda c, b, places: (0, c))]
    specs += [pl.BlockSpec((depth * count, rows), lambda c, b, places: (c, 0))] * blocks
    aliases = {}
    if result is not None:
        aliases = {len(operands): 0}
        operands.append(result)
        specs.append(pl.BlockSpec(memory_space=pl.ANY))
    return pl.pallas_call(
        functools.partial(block_kernel, blocks),
        grid_spec=pltpu.PrefetchScalarGridSpec(
            num_scalar_prefetch=1,
            grid=(share // count, blocks),
            in_specs=specs,
            out_specs=pl.BlockSpec(
                (count, 2, rows, rows), lambda c, b, places: (c, 0, 0, places[b])
            ),
        ),
        out_shape=jax.ShapeDtypeStruct((share, 2, rows, total), jnp.float32),
        input_output_aliases=aliases,
        compiler_params=pltpu.CompilerParams(vmem_limit_bytes=24 * 2**20),
        cost_estimate=pl.CostEstimate(
            flops=8 * share * blocks * rows * rows * depth,
            bytes_accessed=4 * share * 2 * blocks * rows * rows,
            transcendentals=0,
        ),
        name="correlate",
    )(*operands)


def whole_kernel(left_ref, all_ref, out_ref):
    rows = left_ref.shape[0]
    for group in range(all_ref.shape[0]):
        values = visibility(left_ref[...], all_ref[group])
        for kind in range(2):
            out_ref[0, kind, :, group * rows : (group + 1) * rows] = values[kind]


def correlate_whole(left, gathered, share):
    groups, out_rows, rows = gathered.shape
    depth = out_rows // share
    return pl.pallas_call(
        whole_kernel,
        grid=(share,),
        in_specs=[
            pl.BlockSpec((rows, 2 * depth), lambda c: (0, c)),
            pl.BlockSpec((groups, depth, rows), lambda c: (0, c, 0)),
        ],
        out_specs=pl.BlockSpec((1, 2, rows, groups * rows), lambda c: (c, 0, 0, 0)),
        out_shape=jax.ShapeDtypeStruct((share, 2, rows, groups * rows), jnp.float32),
        compiler_params=pltpu.CompilerParams(vmem_limit_bytes=24 * 2**20),
        name="correlate_whole",
    )(left, gathered)


def swapped(shard, axis, step):
    if step == 0:
        return shard
    length = lax.axis_size(axis)
    return lax.ppermute(shard, axis, [(i, peer(i, step, length, 1)) for i in range(length)])


def body(voltages, gains):
    inputs_here = voltages.shape[1]
    frames_here = voltages.shape[2] // NFFT
    channels = gains.shape[2]
    owners = lax.axis_size("fgrp")
    share = channels // owners
    norm = 1.0 / math.sqrt(frames_here * owners)
    partial = filter_all(voltages, filter_table(channels), jnp.swapaxes(gains, 1, 2), owners)
    turned = lax.all_to_all(partial, "fgrp", split_axis=0, concat_axis=0, tiled=True)
    own, left = merge(turned, frames_here, share, norm)
    tiles, pols = lax.axis_size("tile"), lax.axis_size("pol")
    if inputs_here % 128:
        wide = lax.all_gather(lax.all_gather(own, "pol", axis=0), "tile", axis=0)
        return correlate_whole(left, wide.reshape((-1,) + own.shape), share)
    tile, pol = lax.axis_index("tile"), lax.axis_index("pol")

    def place(by_tile, by_pol):
        return (peer(tile, by_tile, tiles, -1) * pols + peer(pol, by_pol, pols, -1)).astype(jnp.int32)

    total = tiles * pols * inputs_here
    result = None
    for by_pol in range(pols):
        near = swapped(own, "pol", by_pol)
        if by_pol:
            near, result = lax.optimization_barrier((near, result))
        for by_tile in range(tiles):
            right = swapped(near, "tile", by_tile)
            where = place(by_tile, by_pol).reshape(1)
            result = correlate(left, [right], where, total, result, share)
    return result


def solution(mesh):
    placed = (P(None, ("tile", "pol"), "fgrp"), P(None, ("tile", "pol"), None))
    return jax.shard_map(
        body,
        mesh=mesh,
        in_specs=placed,
        out_specs=P("fgrp", None, ("tile", "pol"), None),
        check_vma=False,
    )
```

```python
import functools
import math

import jax
import jax.numpy as jnp
import ml_dtypes
import numpy as np
from jax import lax
from jax.experimental import pallas as pl
from jax.experimental.pallas import tpu as pltpu
from jax.sharding import PartitionSpec as P

NFFT = 4096
TAPS = 4


def filter_taps():
    span = TAPS * NFFT
    position = np.arange(span, dtype=np.float64)
    centred = (position - span / 2 + 0.5) / NFFT
    window = 0.5 - 0.5 * np.cos(2.0 * np.pi * (position + 0.5) / span)
    return (np.sinc(centred) * window).reshape(TAPS, NFFT)


def tap_order():
    energy = (filter_taps() ** 2).sum(axis=1)
    order = list(range(TAPS))[::-1]
    return order, [t for t in order if energy[t] > 0.01 * energy.sum()]


def filter_table(channels):
    order, low_order = tap_order()
    phases = np.arange(NFFT)[:, None] * np.arange(channels)[None, :] % NFFT
    angles = phases * (2.0 * np.pi / NFFT)
    transform = np.concatenate([np.cos(angles), np.sin(angles)], axis=1) / math.sqrt(NFFT)
    blocks = {t: filter_taps()[t][:, None] * transform for t in order}
    high = {t: b.astype(np.float32).astype(ml_dtypes.bfloat16) for t, b in blocks.items()}
    low = np.concatenate([blocks[t] - high[t].astype(np.float64) for t in low_order], axis=1)
    scale = 2.0 ** np.floor(np.log2(256.0 / np.abs(low).max()))
    low = (low * scale).astype(np.float32).astype(ml_dtypes.float8_e4m3fn)
    high = np.concatenate([high[t] for t in order], axis=1)
    return np.ascontiguousarray(high.T), np.ascontiguousarray(low.T), float(1.0 / scale)


def peer(me, step, length, way):
    if length & (length - 1):
        return (me + way * step) % length
    return me ^ step


def filter_kernel(low_scale, volt_hbm, table_hbm, low_hbm, gain_ref, out_ref, *scratch):
    sums, low_sums, volts, table, low_table, volt_here, first_here, table_here, low_here = scratch
    half = gain_ref.shape[1]
    width = 2 * half
    order, low_order = tap_order()
    steps = 2 * (volt_hbm.shape[2] // NFFT)
    pieces = first_here.shape[0]
    depth = NFFT // pieces

    def block(step):
        slot = lax.rem(step, 2)
        samples = pl.ds(pl.multiple_of(lax.div(step, 2) * NFFT, NFFT), NFFT)
        return pltpu.make_async_copy(
            volt_hbm.at[slot, :, samples], volts.at[slot], volt_here.at[slot]
        )

    def fetch(piece):
        part = pl.ds(piece * depth, depth)
        return [
            pltpu.make_async_copy(
                volt_hbm.at[0, :, part], volts.at[0, :, part], first_here.at[piece]
            ),
            pltpu.make_async_copy(table_hbm.at[:, part], table.at[:, part], table_here.at[piece]),
            pltpu.make_async_copy(low_hbm.at[:, part], low_table.at[:, part], low_here.at[piece]),
        ]

    def product(left, right):
        return lax.dot_general(
            left, right, (((1,), (1,)), ((), ())), preferred_element_type=jnp.float32
        )

    def add(step, start, size):
        part = lax.rem(step, 2)
        first = pl.multiple_of(lax.div(step, 2) * width, width)
        here = pl.ds(first, len(order) * width)
        low = pl.ds(first, len(low_order) * width)
        values = volts[part, :, start : start + size]
        sums[part, here, :] += product(table[:, start : start + size], values)
        low_sums[part, low, :] += product(
            low_table[:, start : start + size], values.astype(jnp.float8_e4m3fn)
        )

    for piece in range(pieces):
        for copy in fetch(piece):
            copy.start()
    block(1).start()
    sums[...] = jnp.zeros_like(sums)
    low_sums[...] = jnp.zeros_like(low_sums)
    for piece in range(pieces):
        for copy in fetch(piece):
            copy.wait()
        add(0, piece * depth, depth)

    @pl.loop(1, steps)
    def _(step):
        block(step).wait()

        @pl.when(step + 1 < steps)
        def _():
            block(step + 1).start()

        add(step, 0, NFFT)

    owners = out_ref.shape[0]
    share = half // owners
    for slot in range(sums.shape[1] // width):
        both = [sums[c, slot * width : (slot + 1) * width, :] for c in range(2)]
        at = (slot - order.index(low_order[0])) * width
        if 0 <= at < low_sums.shape[1]:
            both = [both[c] + low_scale * low_sums[c, at : at + width, :] for c in range(2)]
        real = both[0][:half] + both[1][half:]
        imag = both[1][:half] - both[0][half:]
        out_real = gain_ref[0] * real - gain_ref[1] * imag
        out_imag = gain_ref[0] * imag + gain_ref[1] * real
        for owner in range(owners):
            at = owner * share
            pair = jnp.concatenate([out_real[at : at + share], out_imag[at : at + share]], axis=0)
            at = 2 * share * slot
            out_ref[owner, at : at + 2 * share, :] = pair.astype(jnp.bfloat16)


def filter_all(voltages, tables, gains, owners):
    rows = voltages.shape[1]
    frames = voltages.shape[2] // NFFT
    half = gains.shape[1]
    slots = frames + TAPS - 1
    low_slots = frames + len(tap_order()[1]) - 1
    out_rows = slots * 2 * half // owners
    table, low_table, low_scale = tables
    pieces = 4
    return pl.pallas_call(
        functools.partial(filter_kernel, low_scale),
        in_specs=[pl.BlockSpec(memory_space=pl.ANY)] * 3 + [pl.BlockSpec(memory_space=pltpu.VMEM)],
        out_shape=jax.ShapeDtypeStruct((owners, out_rows, rows), jnp.bfloat16),
        scratch_shapes=[
            pltpu.VMEM((2, slots * 2 * half, rows), jnp.float32),
            pltpu.VMEM((2, low_slots * 2 * half, rows), jnp.float32),
            pltpu.VMEM((2, rows, NFFT), jnp.bfloat16),
            pltpu.VMEM(table.shape, jnp.bfloat16),
            pltpu.VMEM(low_table.shape, jnp.float8_e4m3fn),
            pltpu.SemaphoreType.DMA((2,)),
            pltpu.SemaphoreType.DMA((pieces,)),
            pltpu.SemaphoreType.DMA((pieces,)),
            pltpu.SemaphoreType.DMA((pieces,)),
        ],
        compiler_params=pltpu.CompilerParams(vmem_limit_bytes=40 * 2**20),
        cost_estimate=pl.CostEstimate(
            flops=2 * 2 * rows * frames * NFFT * (table.shape[0] + low_table.shape[0]),
            bytes_accessed=2 * (2 * rows * frames * NFFT + NFFT * table.shape[0]),
            transcendentals=0,
        ),
        name="filter_all",
    )(voltages, jnp.asarray(table), jnp.asarray(low_table), gains)


def merge_kernel(frames, share, norm, in_ref, out_ref, left_ref, scratch):
    owners = in_ref.shape[0]
    depth = 2 * owners * frames
    blocks = scratch.shape[0]
    for group in range(owners):
        for frame in range(frames):
            at = 2 * share * frame
            value = in_ref[group, at : at + 2 * share, :].astype(jnp.float32)
            if group > 0 and frame < TAPS - 1:
                at = 2 * share * (frame + frames)
                value = value + in_ref[group - 1, at : at + 2 * share, :].astype(jnp.float32)
            if value.shape[1] < 128 * blocks:
                spare = jnp.zeros((2 * share, 128 * blocks - value.shape[1]), jnp.float32)
                value = jnp.concatenate([value, spare], axis=1)
            for part in range(2):
                row = (part * owners + group) * frames + frame
                for block in range(blocks):
                    scratch[block, pl.ds(row, share, stride=depth), :] = value[
                        part * share : (part + 1) * share, block * 128 : (block + 1) * 128
                    ]
    for block in range(blocks):
        lanes = min(128, out_ref.shape[1] - block * 128)
        at = block * 128
        for channel in range(share):
            rounded = scratch[block, channel * depth : (channel + 1) * depth, :].astype(jnp.bfloat16)
            out_ref[channel * depth : (channel + 1) * depth, at : at + lanes] = rounded[:, :lanes]
            scaled = norm * rounded.astype(jnp.float32)
            high = scaled.astype(jnp.bfloat16).astype(jnp.float32)
            both = jnp.concatenate([high, scaled - high], axis=0).T
            left_ref[at : at + lanes, 2 * channel * depth : 2 * (channel + 1) * depth] = both[
                :lanes
            ].astype(jnp.bfloat16)


def merge(turned, frames, share, norm):
    owners, in_rows, rows = turned.shape
    out_rows = share * 2 * owners * frames
    return pl.pallas_call(
        functools.partial(merge_kernel, frames, share, norm),
        in_specs=[pl.BlockSpec(memory_space=pltpu.VMEM)],
        out_shape=[
            jax.ShapeDtypeStruct((out_rows, rows), jnp.bfloat16),
            jax.ShapeDtypeStruct((rows, 2 * out_rows), jnp.bfloat16),
        ],
        scratch_shapes=[pltpu.VMEM((pl.cdiv(rows, 128), out_rows, 128), jnp.float32)],
        compiler_params=pltpu.CompilerParams(vmem_limit_bytes=16 * 2**20),
        name="merge",
    )(turned)


def visibility(left, right):
    half = right.shape[0] // 2
    crossed = jnp.concatenate([-right[half:], right[:half]], axis=0)
    return [
        jnp.dot(
            left, jnp.concatenate([value, value], axis=0), preferred_element_type=jnp.float32
        )
        for value in (right, crossed)
    ]


def block_kernel(share, place_ref, left_ref, right_ref, *refs):
    out_hbm, (values, written) = refs[-3], refs[-2:]
    depth = right_ref.shape[0] // share
    rows = right_ref.shape[1]
    slots = values.shape[0]
    columns = pl.ds(pl.multiple_of(place_ref[0] * rows, rows), rows)

    def write(channel):
        slot = channel % slots
        return pltpu.make_async_copy(
            values.at[slot], out_hbm.at[channel, :, :, columns], written.at[slot]
        )

    for channel in range(share):
        slot = channel % slots
        if channel >= slots:
            write(channel - slots).wait()
        values[slot, 0], values[slot, 1] = visibility(
            left_ref[:, 2 * depth * channel : 2 * depth * (channel + 1)],
            right_ref[depth * channel : depth * (channel + 1), :],
        )
        write(channel).start()
    for channel in range(max(share - slots, 0), share):
        write(channel).wait()


def correlate(left, right, place, total, result, share):
    out_rows, rows = right.shape
    depth = out_rows // share
    slots = 4
    operands = [place, left, right]
    specs = [pl.BlockSpec(memory_space=pltpu.SMEM)] + [pl.BlockSpec(memory_space=pltpu.VMEM)] * 2
    aliases = {}
    if result is not None:
        aliases = {len(operands): 0}
        operands.append(result)
        specs.append(pl.BlockSpec(memory_space=pl.ANY))
    return pl.pallas_call(
        functools.partial(block_kernel, share),
        in_specs=specs,
        out_specs=pl.BlockSpec(memory_space=pl.ANY),
        out_shape=jax.ShapeDtypeStruct((share, 2, rows, total), jnp.float32),
        scratch_shapes=[
            pltpu.VMEM((slots, 2, rows, rows), jnp.float32),
            pltpu.SemaphoreType.DMA((slots,)),
        ],
        input_output_aliases=aliases,
        compiler_params=pltpu.CompilerParams(vmem_limit_bytes=24 * 2**20),
        cost_estimate=pl.CostEstimate(
            flops=8 * share * rows * rows * depth,
            bytes_accessed=4 * share * 2 * rows * rows,
            transcendentals=0,
        ),
        name="correlate",
    )(*operands)


def whole_kernel(left_ref, all_ref, out_ref):
    rows = left_ref.shape[0]
    for group in range(all_ref.shape[0]):
        values = visibility(left_ref[...], all_ref[group])
        for kind in range(2):
            out_ref[0, kind, :, group * rows : (group + 1) * rows] = values[kind]


def correlate_whole(left, gathered, share):
    groups, out_rows, rows = gathered.shape
    depth = out_rows // share
    return pl.pallas_call(
        whole_kernel,
        grid=(share,),
        in_specs=[
            pl.BlockSpec((rows, 2 * depth), lambda c: (0, c)),
            pl.BlockSpec((groups, depth, rows), lambda c: (0, c, 0)),
        ],
        out_specs=pl.BlockSpec((1, 2, rows, groups * rows), lambda c: (c, 0, 0, 0)),
        out_shape=jax.ShapeDtypeStruct((share, 2, rows, groups * rows), jnp.float32),
        compiler_params=pltpu.CompilerParams(vmem_limit_bytes=24 * 2**20),
        name="correlate_whole",
    )(left, gathered)


def swapped(shard, axis, step):
    if step == 0:
        return shard
    length = lax.axis_size(axis)
    return lax.ppermute(shard, axis, [(i, peer(i, step, length, 1)) for i in range(length)])


def body(voltages, gains):
    inputs_here = voltages.shape[1]
    frames_here = voltages.shape[2] // NFFT
    channels = gains.shape[2]
    owners = lax.axis_size("fgrp")
    share = channels // owners
    norm = 1.0 / math.sqrt(frames_here * owners)
    partial = filter_all(voltages, filter_table(channels), jnp.swapaxes(gains, 1, 2), owners)
    turned = lax.all_to_all(partial, "fgrp", split_axis=0, concat_axis=0, tiled=True)
    own, left = merge(turned, frames_here, share, norm)
    tiles, pols = lax.axis_size("tile"), lax.axis_size("pol")
    if inputs_here % 128:
        wide = lax.all_gather(lax.all_gather(own, "pol", axis=0), "tile", axis=0)
        return correlate_whole(left, wide.reshape((-1,) + own.shape), share)
    tile, pol = lax.axis_index("tile"), lax.axis_index("pol")

    def place(by_tile, by_pol):
        return (peer(tile, by_tile, tiles, -1) * pols + peer(pol, by_pol, pols, -1)).astype(jnp.int32)

    total = tiles * pols * inputs_here
    result = None
    for by_pol in range(pols):
        near = swapped(own, "pol", by_pol)
        if by_pol:
            near, result = lax.optimization_barrier((near, result))
        for by_tile in range(tiles):
            right = swapped(near, "tile", by_tile)
            where = place(by_tile, by_pol).reshape(1)
            result = correlate(left, right, where, total, result, share)
    return result


def solution(mesh):
    placed = (P(None, ("tile", "pol"), "fgrp"), P(None, ("tile", "pol"), None))
    return jax.shard_map(
        body,
        mesh=mesh,
        in_specs=placed,
        out_specs=P("fgrp", None, ("tile", "pol"), None),
        check_vma=False,
    )
```

```python
import functools
import math

import jax
import jax.numpy as jnp
import ml_dtypes
import numpy as np
from jax import lax
from jax.experimental import pallas as pl
from jax.experimental.pallas import tpu as pltpu
from jax.sharding import PartitionSpec as P

NFFT = 4096
TAPS = 4


def filter_taps():
    span = TAPS * NFFT
    position = np.arange(span, dtype=np.float64)
    centred = (position - span / 2 + 0.5) / NFFT
    window = 0.5 - 0.5 * np.cos(2.0 * np.pi * (position + 0.5) / span)
    return (np.sinc(centred) * window).reshape(TAPS, NFFT)


def tap_order():
    energy = (filter_taps() ** 2).sum(axis=1)
    order = list(range(TAPS))[::-1]
    return order, [t for t in order if energy[t] > 0.01 * energy.sum()]


def filter_table(channels):
    order, low_order = tap_order()
    phases = np.arange(NFFT)[:, None] * np.arange(channels)[None, :] % NFFT
    angles = phases * (2.0 * np.pi / NFFT)
    transform = np.concatenate([np.cos(angles), np.sin(angles)], axis=1) / math.sqrt(NFFT)
    blocks = {t: filter_taps()[t][:, None] * transform for t in order}
    high = {t: b.astype(np.float32).astype(ml_dtypes.bfloat16) for t, b in blocks.items()}
    low = np.concatenate([blocks[t] - high[t].astype(np.float64) for t in low_order], axis=1)
    scale = 2.0 ** np.floor(np.log2(256.0 / np.abs(low).max()))
    low = (low * scale).astype(np.float32).astype(ml_dtypes.float8_e4m3fn)
    high = np.concatenate([high[t] for t in order], axis=1)
    return np.ascontiguousarray(high.T), np.ascontiguousarray(low.T), float(1.0 / scale)


def peer(me, step, length, way):
    if length & (length - 1):
        return (me + way * step) % length
    return me ^ step


def filter_kernel(frame, low_scale, volt_hbm, table_hbm, low_hbm, *refs):
    out_refs, scratch = refs[:-9], refs[-9:]
    sums, low_sums, volts, table, low_table, volt_here, first_here, table_here, low_here = scratch
    order, low_order = tap_order()
    width = table.shape[0] // len(order)
    half = width // 2
    count = sums.shape[1] // width - (TAPS - 1)
    steps = 2 * count
    pieces = first_here.shape[0]
    depth = NFFT // pieces

    def block(step):
        slot = lax.rem(step, 2)
        samples = pl.ds(pl.multiple_of((lax.div(step, 2) + frame) * NFFT, NFFT), NFFT)
        return pltpu.make_async_copy(
            volt_hbm.at[slot, :, samples], volts.at[slot], volt_here.at[slot]
        )

    def fetch(piece):
        part = pl.ds(piece * depth, depth)
        samples = pl.ds(frame * NFFT + piece * depth, depth)
        return [
            pltpu.make_async_copy(
                volt_hbm.at[0, :, samples], volts.at[0, :, part], first_here.at[piece]
            ),
            pltpu.make_async_copy(table_hbm.at[:, part], table.at[:, part], table_here.at[piece]),
            pltpu.make_async_copy(low_hbm.at[:, part], low_table.at[:, part], low_here.at[piece]),
        ]

    def product(left, right):
        return lax.dot_general(
            left, right, (((1,), (1,)), ((), ())), preferred_element_type=jnp.float32
        )

    def add(step, start, size):
        part = lax.rem(step, 2)
        first = pl.multiple_of(lax.div(step, 2) * width, width)
        here = pl.ds(first, len(order) * width)
        low = pl.ds(first, len(low_order) * width)
        values = volts[part, :, start : start + size]
        sums[part, here, :] += product(table[:, start : start + size], values)
        low_sums[part, low, :] += product(
            low_table[:, start : start + size], values.astype(jnp.float8_e4m3fn)
        )

    for piece in range(pieces):
        for copy in fetch(piece):
            copy.start()
    block(1).start()
    sums[...] = jnp.zeros_like(sums)
    low_sums[...] = jnp.zeros_like(low_sums)
    for piece in range(pieces):
        for copy in fetch(piece):
            copy.wait()
        add(0, piece * depth, depth)

    @pl.loop(1, steps)
    def _(step):
        block(step).wait()

        @pl.when(step + 1 < steps)
        def _():
            block(step + 1).start()

        add(step, 0, NFFT)

    kept = out_refs[0].shape[0] // width
    for slot in range(sums.shape[1] // width):
        both = [sums[c, slot * width : (slot + 1) * width, :] for c in range(2)]
        at = (slot - order.index(low_order[0])) * width
        if 0 <= at < low_sums.shape[1]:
            both = [both[c] + low_scale * low_sums[c, at : at + width, :] for c in range(2)]
        raw = jnp.concatenate(
            [both[0][:half] + both[1][half:], both[1][:half] - both[0][half:]], axis=0
        )
        if slot < kept:
            out_refs[0][slot * width : (slot + 1) * width, :] = raw
        else:
            at = (slot - kept) * width
            out_refs[1][at : at + width, :] = raw.astype(jnp.bfloat16)


def filter_part(voltages, tables, frame, count, kept):
    rows = voltages.shape[1]
    table, low_table, low_scale = tables
    width = table.shape[0] // TAPS
    slots = count + TAPS - 1
    low_slots = count + len(tap_order()[1]) - 1
    shapes = [jax.ShapeDtypeStruct((kept * width, rows), jnp.float32)]
    if slots > kept:
        shapes.append(jax.ShapeDtypeStruct(((slots - kept) * width, rows), jnp.bfloat16))
    pieces = 4
    return pl.pallas_call(
        functools.partial(filter_kernel, frame, low_scale),
        in_specs=[pl.BlockSpec(memory_space=pl.ANY)] * 3,
        out_specs=[pl.BlockSpec(memory_space=pltpu.VMEM)] * len(shapes),
        out_shape=shapes,
        scratch_shapes=[
            pltpu.VMEM((2, slots * width, rows), jnp.float32),
            pltpu.VMEM((2, low_slots * width, rows), jnp.float32),
            pltpu.VMEM((2, rows, NFFT), jnp.bfloat16),
            pltpu.VMEM(table.shape, jnp.bfloat16),
            pltpu.VMEM(low_table.shape, jnp.float8_e4m3fn),
            pltpu.SemaphoreType.DMA((2,)),
            pltpu.SemaphoreType.DMA((pieces,)),
            pltpu.SemaphoreType.DMA((pieces,)),
            pltpu.SemaphoreType.DMA((pieces,)),
        ],
        compiler_params=pltpu.CompilerParams(vmem_limit_bytes=52 * 2**20),
        cost_estimate=pl.CostEstimate(
            flops=2 * 2 * rows * count * NFFT * (table.shape[0] + low_table.shape[0]),
            bytes_accessed=2 * (2 * rows * count * NFFT + NFFT * table.shape[0]),
            transcendentals=0,
        ),
        name="filter_part",
    )(voltages, jnp.asarray(table), jnp.asarray(low_table))


def combine_kernel(early_ref, late_ref, handed_ref, gain_ref, out_ref):
    half = gain_ref.shape[1]
    width = 2 * half
    owners = out_ref.shape[0]
    share = half // owners
    for slot in range(out_ref.shape[1] // (2 * share)):
        raw = early_ref[slot * width : (slot + 1) * width, :] if slot < TAPS else 0.0
        if slot:
            raw = raw + late_ref[(slot - 1) * width : slot * width, :]
        if slot < TAPS - 1:
            raw = raw + handed_ref[slot * width : (slot + 1) * width, :].astype(jnp.float32)
        real, imag = raw[:half], raw[half:]
        out_real = gain_ref[0] * real - gain_ref[1] * imag
        out_imag = gain_ref[0] * imag + gain_ref[1] * real
        for owner in range(owners):
            at = owner * share
            pair = jnp.concatenate([out_real[at : at + share], out_imag[at : at + share]], axis=0)
            at = 2 * share * slot
            out_ref[owner, at : at + 2 * share, :] = pair.astype(jnp.bfloat16)


def combine(early, late, handed, gains, frames, owners):
    _, half, rows = gains.shape
    return pl.pallas_call(
        combine_kernel,
        in_specs=[pl.BlockSpec(memory_space=pltpu.VMEM)] * 4,
        out_specs=pl.BlockSpec(memory_space=pltpu.VMEM),
        out_shape=jax.ShapeDtypeStruct((owners, frames * 2 * half // owners, rows), jnp.bfloat16),
        compiler_params=pltpu.CompilerParams(vmem_limit_bytes=16 * 2**20),
        name="combine",
    )(early, late, handed, gains)


def merge_kernel(frames, share, norm, in_ref, out_ref, left_ref, scratch):
    owners = in_ref.shape[0]
    depth = 2 * owners * frames
    blocks = scratch.shape[0]
    for group in range(owners):
        for frame in range(frames):
            at = 2 * share * frame
            value = in_ref[group, at : at + 2 * share, :].astype(jnp.float32)
            if value.shape[1] < 128 * blocks:
                spare = jnp.zeros((2 * share, 128 * blocks - value.shape[1]), jnp.float32)
                value = jnp.concatenate([value, spare], axis=1)
            for part in range(2):
                row = (part * owners + group) * frames + frame
                for block in range(blocks):
                    scratch[block, pl.ds(row, share, stride=depth), :] = value[
                        part * share : (part + 1) * share, block * 128 : (block + 1) * 128
                    ]
    for block in range(blocks):
        lanes = min(128, out_ref.shape[1] - block * 128)
        at = block * 128
        for channel in range(share):
            rounded = scratch[block, channel * depth : (channel + 1) * depth, :].astype(jnp.bfloat16)
            out_ref[channel * depth : (channel + 1) * depth, at : at + lanes] = rounded[:, :lanes]
            scaled = norm * rounded.astype(jnp.float32)
            high = scaled.astype(jnp.bfloat16).astype(jnp.float32)
            both = jnp.concatenate([high, scaled - high], axis=0).T
            left_ref[at : at + lanes, 2 * channel * depth : 2 * (channel + 1) * depth] = both[
                :lanes
            ].astype(jnp.bfloat16)


def merge(turned, frames, share, norm):
    owners, in_rows, rows = turned.shape
    out_rows = share * 2 * owners * frames
    return pl.pallas_call(
        functools.partial(merge_kernel, frames, share, norm),
        in_specs=[pl.BlockSpec(memory_space=pltpu.VMEM)],
        out_shape=[
            jax.ShapeDtypeStruct((out_rows, rows), jnp.bfloat16),
            jax.ShapeDtypeStruct((rows, 2 * out_rows), jnp.bfloat16),
        ],
        scratch_shapes=[pltpu.VMEM((pl.cdiv(rows, 128), out_rows, 128), jnp.float32)],
        compiler_params=pltpu.CompilerParams(vmem_limit_bytes=16 * 2**20),
        name="merge",
    )(turned)


def visibility(left, right):
    half = right.shape[0] // 2
    crossed = jnp.concatenate([-right[half:], right[:half]], axis=0)
    return [
        jnp.dot(
            left, jnp.concatenate([value, value], axis=0), preferred_element_type=jnp.float32
        )
        for value in (right, crossed)
    ]


def block_kernel(share, place_ref, left_ref, right_ref, *refs):
    out_hbm, (values, written) = refs[-3], refs[-2:]
    depth = right_ref.shape[0] // share
    rows = right_ref.shape[1]
    slots = values.shape[0]
    columns = pl.ds(pl.multiple_of(place_ref[0] * rows, rows), rows)

    def write(channel):
        slot = channel % slots
        return pltpu.make_async_copy(
            values.at[slot], out_hbm.at[channel, :, :, columns], written.at[slot]
        )

    for channel in range(share):
        slot = channel % slots
        if channel >= slots:
            write(channel - slots).wait()
        values[slot, 0], values[slot, 1] = visibility(
            left_ref[:, 2 * depth * channel : 2 * depth * (channel + 1)],
            right_ref[depth * channel : depth * (channel + 1), :],
        )
        write(channel).start()
    for channel in range(max(share - slots, 0), share):
        write(channel).wait()


def correlate(left, right, place, total, result, share):
    out_rows, rows = right.shape
    depth = out_rows // share
    slots = 4
    operands = [place, left, right]
    specs = [pl.BlockSpec(memory_space=pltpu.SMEM)] + [pl.BlockSpec(memory_space=pltpu.VMEM)] * 2
    aliases = {}
    if result is not None:
        aliases = {len(operands): 0}
        operands.append(result)
        specs.append(pl.BlockSpec(memory_space=pl.ANY))
    return pl.pallas_call(
        functools.partial(block_kernel, share),
        in_specs=specs,
        out_specs=pl.BlockSpec(memory_space=pl.ANY),
        out_shape=jax.ShapeDtypeStruct((share, 2, rows, total), jnp.float32),
        scratch_shapes=[
            pltpu.VMEM((slots, 2, rows, rows), jnp.float32),
            pltpu.SemaphoreType.DMA((slots,)),
        ],
        input_output_aliases=aliases,
        compiler_params=pltpu.CompilerParams(vmem_limit_bytes=24 * 2**20),
        cost_estimate=pl.CostEstimate(
            flops=8 * share * rows * rows * depth,
            bytes_accessed=4 * share * 2 * rows * rows,
            transcendentals=0,
        ),
        name="correlate",
    )(*operands)


def whole_kernel(left_ref, all_ref, out_ref):
    rows = left_ref.shape[0]
    for group in range(all_ref.shape[0]):
        values = visibility(left_ref[...], all_ref[group])
        for kind in range(2):
            out_ref[0, kind, :, group * rows : (group + 1) * rows] = values[kind]


def correlate_whole(left, gathered, share):
    groups, out_rows, rows = gathered.shape
    depth = out_rows // share
    return pl.pallas_call(
        whole_kernel,
        grid=(share,),
        in_specs=[
            pl.BlockSpec((rows, 2 * depth), lambda c: (0, c)),
            pl.BlockSpec((groups, depth, rows), lambda c: (0, c, 0)),
        ],
        out_specs=pl.BlockSpec((1, 2, rows, groups * rows), lambda c: (c, 0, 0, 0)),
        out_shape=jax.ShapeDtypeStruct((share, 2, rows, groups * rows), jnp.float32),
        compiler_params=pltpu.CompilerParams(vmem_limit_bytes=24 * 2**20),
        name="correlate_whole",
    )(left, gathered)


def swapped(shard, axis, step):
    if step == 0:
        return shard
    length = lax.axis_size(axis)
    return lax.ppermute(shard, axis, [(i, peer(i, step, length, 1)) for i in range(length)])


def body(voltages, gains):
    inputs_here = voltages.shape[1]
    frames_here = voltages.shape[2] // NFFT
    channels = gains.shape[2]
    owners = lax.axis_size("fgrp")
    share = channels // owners
    norm = 1.0 / math.sqrt(frames_here * owners)
    tables = filter_table(channels)
    late, ending = filter_part(voltages, tables, 1, frames_here - 1, frames_here - 1)
    voltages, ending = lax.optimization_barrier((voltages, ending))
    handed = lax.ppermute(ending, "fgrp", [(i, i + 1) for i in range(owners - 1)])
    (early,) = filter_part(voltages, tables, 0, 1, TAPS)
    handed, early = lax.optimization_barrier((handed, early))
    partial = combine(early, late, handed, jnp.swapaxes(gains, 1, 2), frames_here, owners)
    turned = lax.all_to_all(partial, "fgrp", split_axis=0, concat_axis=0, tiled=True)
    own, left = merge(turned, frames_here, share, norm)
    tiles, pols = lax.axis_size("tile"), lax.axis_size("pol")
    if inputs_here % 128:
        wide = lax.all_gather(lax.all_gather(own, "pol", axis=0), "tile", axis=0)
        return correlate_whole(left, wide.reshape((-1,) + own.shape), share)
    tile, pol = lax.axis_index("tile"), lax.axis_index("pol")

    def place(by_tile, by_pol):
        return (peer(tile, by_tile, tiles, -1) * pols + peer(pol, by_pol, pols, -1)).astype(jnp.int32)

    total = tiles * pols * inputs_here
    result = None
    for by_pol in range(pols):
        near = swapped(own, "pol", by_pol)
        if by_pol:
            near, result = lax.optimization_barrier((near, result))
        for by_tile in range(tiles):
            right = swapped(near, "tile", by_tile)
            where = place(by_tile, by_pol).reshape(1)
            result = correlate(left, right, where, total, result, share)
    return result


def solution(mesh):
    placed = (P(None, ("tile", "pol"), "fgrp"), P(None, ("tile", "pol"), None))
    return jax.shard_map(
        body,
        mesh=mesh,
        in_specs=placed,
        out_specs=P("fgrp", None, ("tile", "pol"), None),
        check_vma=False,
    )
```

```python
import functools
import math

import jax
import jax.numpy as jnp
import ml_dtypes
import numpy as np
from jax import lax
from jax.experimental import pallas as pl
from jax.experimental.pallas import tpu as pltpu
from jax.sharding import PartitionSpec as P

NFFT = 4096
TAPS = 4


def filter_taps():
    span = TAPS * NFFT
    position = np.arange(span, dtype=np.float64)
    centred = (position - span / 2 + 0.5) / NFFT
    window = 0.5 - 0.5 * np.cos(2.0 * np.pi * (position + 0.5) / span)
    return (np.sinc(centred) * window).reshape(TAPS, NFFT)


def tap_order():
    energy = (filter_taps() ** 2).sum(axis=1)
    order = list(range(TAPS))[::-1]
    return order, [t for t in order if energy[t] > 0.01 * energy.sum()]


def filter_table(channels):
    order, low_order = tap_order()
    phases = np.arange(NFFT)[:, None] * np.arange(channels)[None, :] % NFFT
    angles = phases * (2.0 * np.pi / NFFT)
    transform = np.concatenate([np.cos(angles), np.sin(angles)], axis=1) / math.sqrt(NFFT)
    blocks = {t: filter_taps()[t][:, None] * transform for t in order}
    high = {t: b.astype(np.float32).astype(ml_dtypes.bfloat16) for t, b in blocks.items()}
    low = np.concatenate([blocks[t] - high[t].astype(np.float64) for t in low_order], axis=1)
    scale = 2.0 ** np.floor(np.log2(256.0 / np.abs(low).max()))
    low = (low * scale).astype(np.float32).astype(ml_dtypes.float8_e4m3fn)
    high = np.concatenate([high[t] for t in order], axis=1)
    return np.ascontiguousarray(high.T), np.ascontiguousarray(low.T), float(1.0 / scale)


def peer(me, step, length, way):
    if length & (length - 1):
        return (me + way * step) % length
    return me ^ step


def filter_kernel(frame, low_scale, volt_hbm, table_hbm, low_hbm, *refs):
    out_refs, scratch = refs[:-9], refs[-9:]
    sums, low_sums, volts, table, low_table, volt_here, first_here, table_here, low_here = scratch
    order, low_order = tap_order()
    width = table.shape[0] // len(order)
    half = width // 2
    count = sums.shape[1] // width - (TAPS - 1)
    steps = 2 * count
    pieces = first_here.shape[0]
    depth = NFFT // pieces

    def block(step):
        slot = lax.rem(step, 2)
        samples = pl.ds(pl.multiple_of((lax.div(step, 2) + frame) * NFFT, NFFT), NFFT)
        return pltpu.make_async_copy(
            volt_hbm.at[slot, :, samples], volts.at[slot], volt_here.at[slot]
        )

    def fetch(piece):
        part = pl.ds(piece * depth, depth)
        samples = pl.ds(frame * NFFT + piece * depth, depth)
        return [
            pltpu.make_async_copy(
                volt_hbm.at[0, :, samples], volts.at[0, :, part], first_here.at[piece]
            ),
            pltpu.make_async_copy(table_hbm.at[:, part], table.at[:, part], table_here.at[piece]),
            pltpu.make_async_copy(low_hbm.at[:, part], low_table.at[:, part], low_here.at[piece]),
        ]

    def product(left, right):
        return lax.dot_general(
            left, right, (((1,), (1,)), ((), ())), preferred_element_type=jnp.float32
        )

    def add(step, start, size):
        part = lax.rem(step, 2)
        first = pl.multiple_of(lax.div(step, 2) * width, width)
        here = pl.ds(first, len(order) * width)
        low = pl.ds(first, len(low_order) * width)
        values = volts[part, :, start : start + size]
        sums[part, here, :] += product(table[:, start : start + size], values)
        low_sums[part, low, :] += product(
            low_table[:, start : start + size], values.astype(jnp.float8_e4m3fn)
        )

    for piece in range(pieces):
        for copy in fetch(piece):
            copy.start()
    block(1).start()
    sums[...] = jnp.zeros_like(sums)
    low_sums[...] = jnp.zeros_like(low_sums)
    for piece in range(pieces):
        for copy in fetch(piece):
            copy.wait()
        add(0, piece * depth, depth)

    @pl.loop(1, steps)
    def _(step):
        block(step).wait()

        @pl.when(step + 1 < steps)
        def _():
            block(step + 1).start()

        add(step, 0, NFFT)

    kept = out_refs[0].shape[0] // width
    for slot in range(sums.shape[1] // width):
        both = [sums[c, slot * width : (slot + 1) * width, :] for c in range(2)]
        at = (slot - order.index(low_order[0])) * width
        if 0 <= at < low_sums.shape[1]:
            both = [both[c] + low_scale * low_sums[c, at : at + width, :] for c in range(2)]
        raw = jnp.concatenate(
            [both[0][:half] + both[1][half:], both[1][:half] - both[0][half:]], axis=0
        )
        if slot < kept:
            out_refs[0][slot * width : (slot + 1) * width, :] = raw
        else:
            at = (slot - kept) * width
            out_refs[1][at : at + width, :] = raw.astype(jnp.bfloat16)


def filter_part(voltages, tables, frame, count, kept):
    rows = voltages.shape[1]
    table, low_table, low_scale = tables
    width = table.shape[0] // TAPS
    slots = count + TAPS - 1
    low_slots = count + len(tap_order()[1]) - 1
    shapes = [jax.ShapeDtypeStruct((kept * width, rows), jnp.float32)]
    if slots > kept:
        shapes.append(jax.ShapeDtypeStruct(((slots - kept) * width, rows), jnp.bfloat16))
    pieces = 4
    return pl.pallas_call(
        functools.partial(filter_kernel, frame, low_scale),
        in_specs=[pl.BlockSpec(memory_space=pl.ANY)] * 3,
        out_specs=[pl.BlockSpec(memory_space=pltpu.VMEM)] * len(shapes),
        out_shape=shapes,
        scratch_shapes=[
            pltpu.VMEM((2, slots * width, rows), jnp.float32),
            pltpu.VMEM((2, low_slots * width, rows), jnp.float32),
            pltpu.VMEM((2, rows, NFFT), jnp.bfloat16),
            pltpu.VMEM(table.shape, jnp.bfloat16),
            pltpu.VMEM(low_table.shape, jnp.float8_e4m3fn),
            pltpu.SemaphoreType.DMA((2,)),
            pltpu.SemaphoreType.DMA((pieces,)),
            pltpu.SemaphoreType.DMA((pieces,)),
            pltpu.SemaphoreType.DMA((pieces,)),
        ],
        compiler_params=pltpu.CompilerParams(vmem_limit_bytes=52 * 2**20),
        cost_estimate=pl.CostEstimate(
            flops=2 * 2 * rows * count * NFFT * (table.shape[0] + low_table.shape[0]),
            bytes_accessed=2 * (2 * rows * count * NFFT + NFFT * table.shape[0]),
            transcendentals=0,
        ),
        name="filter_part",
    )(voltages, jnp.asarray(table), jnp.asarray(low_table))


def combine_kernel(early_ref, late_ref, odd_ref, even_ref, gain_ref, out_ref):
    half = gain_ref.shape[1]
    width = 2 * half
    owners = out_ref.shape[0]
    share = half // owners
    for slot in range(out_ref.shape[1] // (2 * share)):
        raw = early_ref[slot * width : (slot + 1) * width, :] if slot < TAPS else 0.0
        if slot:
            raw = raw + late_ref[(slot - 1) * width : slot * width, :]
        if slot < TAPS - 1:
            for handed_ref in (odd_ref, even_ref):
                raw = raw + handed_ref[slot * width : (slot + 1) * width, :].astype(jnp.float32)
        real, imag = raw[:half], raw[half:]
        out_real = gain_ref[0] * real - gain_ref[1] * imag
        out_imag = gain_ref[0] * imag + gain_ref[1] * real
        for owner in range(owners):
            at = owner * share
            pair = jnp.concatenate([out_real[at : at + share], out_imag[at : at + share]], axis=0)
            at = 2 * share * slot
            out_ref[owner, at : at + 2 * share, :] = pair.astype(jnp.bfloat16)


def combine(early, late, to_odd, to_even, gains, frames, owners):
    _, half, rows = gains.shape
    return pl.pallas_call(
        combine_kernel,
        in_specs=[pl.BlockSpec(memory_space=pltpu.VMEM)] * 5,
        out_specs=pl.BlockSpec(memory_space=pltpu.VMEM),
        out_shape=jax.ShapeDtypeStruct((owners, frames * 2 * half // owners, rows), jnp.bfloat16),
        compiler_params=pltpu.CompilerParams(vmem_limit_bytes=16 * 2**20),
        name="combine",
    )(early, late, to_odd, to_even, gains)


def merge_kernel(frames, share, norm, in_ref, out_ref, left_ref, scratch):
    owners = in_ref.shape[0]
    depth = 2 * owners * frames
    blocks = scratch.shape[0]
    for group in range(owners):
        for frame in range(frames):
            at = 2 * share * frame
            value = in_ref[group, at : at + 2 * share, :].astype(jnp.float32)
            if value.shape[1] < 128 * blocks:
                spare = jnp.zeros((2 * share, 128 * blocks - value.shape[1]), jnp.float32)
                value = jnp.concatenate([value, spare], axis=1)
            for part in range(2):
                row = (part * owners + group) * frames + frame
                for block in range(blocks):
                    scratch[block, pl.ds(row, share, stride=depth), :] = value[
                        part * share : (part + 1) * share, block * 128 : (block + 1) * 128
                    ]
    for block in range(blocks):
        lanes = min(128, out_ref.shape[1] - block * 128)
        at = block * 128
        for channel in range(share):
            rounded = scratch[block, channel * depth : (channel + 1) * depth, :].astype(jnp.bfloat16)
            out_ref[channel * depth : (channel + 1) * depth, at : at + lanes] = rounded[:, :lanes]
            scaled = norm * rounded.astype(jnp.float32)
            high = scaled.astype(jnp.bfloat16).astype(jnp.float32)
            both = jnp.concatenate([high, scaled - high], axis=0).T
            left_ref[at : at + lanes, 2 * channel * depth : 2 * (channel + 1) * depth] = both[
                :lanes
            ].astype(jnp.bfloat16)


def merge(turned, frames, share, norm):
    owners, in_rows, rows = turned.shape
    out_rows = share * 2 * owners * frames
    return pl.pallas_call(
        functools.partial(merge_kernel, frames, share, norm),
        in_specs=[pl.BlockSpec(memory_space=pltpu.VMEM)],
        out_shape=[
            jax.ShapeDtypeStruct((out_rows, rows), jnp.bfloat16),
            jax.ShapeDtypeStruct((rows, 2 * out_rows), jnp.bfloat16),
        ],
        scratch_shapes=[pltpu.VMEM((pl.cdiv(rows, 128), out_rows, 128), jnp.float32)],
        compiler_params=pltpu.CompilerParams(vmem_limit_bytes=16 * 2**20),
        name="merge",
    )(turned)


def visibility(left, right, kind):
    if kind:
        half = right.shape[0] // 2
        right = jnp.concatenate([-right[half:], right[:half]], axis=0)
    both = jnp.concatenate([right, right], axis=0)
    return jnp.dot(left, both, preferred_element_type=jnp.float32)


def block_kernel(share, place_ref, left_ref, right_ref, *refs):
    out_hbm, (values, written) = refs[-3], refs[-2:]
    depth = right_ref.shape[0] // share
    rows = right_ref.shape[1]
    slots = values.shape[0]
    columns = pl.ds(pl.multiple_of(place_ref[0] * rows, rows), rows)

    def write(channel, kind):
        slot = channel % slots
        return pltpu.make_async_copy(
            values.at[slot, kind], out_hbm.at[channel, kind, :, columns], written.at[slot, kind]
        )

    for channel in range(share):
        slot = channel % slots
        right = right_ref[depth * channel : depth * (channel + 1), :]
        for kind in range(2):
            if channel >= slots:
                write(channel - slots, kind).wait()
            values[slot, kind] = visibility(
                left_ref[:, 2 * depth * channel : 2 * depth * (channel + 1)], right, kind
            )
            write(channel, kind).start()
    for channel in range(max(share - slots, 0), share):
        for kind in range(2):
            write(channel, kind).wait()


def correlate(left, right, place, total, result, share):
    out_rows, rows = right.shape
    depth = out_rows // share
    slots = 4
    operands = [place, left, right]
    specs = [pl.BlockSpec(memory_space=pltpu.SMEM)] + [pl.BlockSpec(memory_space=pltpu.VMEM)] * 2
    aliases = {}
    if result is not None:
        aliases = {len(operands): 0}
        operands.append(result)
        specs.append(pl.BlockSpec(memory_space=pl.ANY))
    return pl.pallas_call(
        functools.partial(block_kernel, share),
        in_specs=specs,
        out_specs=pl.BlockSpec(memory_space=pl.ANY),
        out_shape=jax.ShapeDtypeStruct((share, 2, rows, total), jnp.float32),
        scratch_shapes=[
            pltpu.VMEM((slots, 2, rows, rows), jnp.float32),
            pltpu.SemaphoreType.DMA((slots, 2)),
        ],
        input_output_aliases=aliases,
        compiler_params=pltpu.CompilerParams(vmem_limit_bytes=24 * 2**20),
        cost_estimate=pl.CostEstimate(
            flops=8 * share * rows * rows * depth,
            bytes_accessed=4 * share * 2 * rows * rows,
            transcendentals=0,
        ),
        name="correlate",
    )(*operands)


def whole_kernel(left_ref, all_ref, out_ref):
    rows = left_ref.shape[0]
    for group in range(all_ref.shape[0]):
        for kind in range(2):
            out_ref[0, kind, :, group * rows : (group + 1) * rows] = visibility(
                left_ref[...], all_ref[group], kind
            )


def correlate_whole(left, gathered, share):
    groups, out_rows, rows = gathered.shape
    depth = out_rows // share
    return pl.pallas_call(
        whole_kernel,
        grid=(share,),
        in_specs=[
            pl.BlockSpec((rows, 2 * depth), lambda c: (0, c)),
            pl.BlockSpec((groups, depth, rows), lambda c: (0, c, 0)),
        ],
        out_specs=pl.BlockSpec((1, 2, rows, groups * rows), lambda c: (c, 0, 0, 0)),
        out_shape=jax.ShapeDtypeStruct((share, 2, rows, groups * rows), jnp.float32),
        compiler_params=pltpu.CompilerParams(vmem_limit_bytes=24 * 2**20),
        name="correlate_whole",
    )(left, gathered)


def swapped(shard, axis, step):
    if step == 0:
        return shard
    length = lax.axis_size(axis)
    return lax.ppermute(shard, axis, [(i, peer(i, step, length, 1)) for i in range(length)])


def body(voltages, gains):
    inputs_here = voltages.shape[1]
    frames_here = voltages.shape[2] // NFFT
    channels = gains.shape[2]
    owners = lax.axis_size("fgrp")
    share = channels // owners
    norm = 1.0 / math.sqrt(frames_here * owners)
    tables = filter_table(channels)
    late, ending = filter_part(voltages, tables, 1, frames_here - 1, frames_here - 1)
    voltages, ending = lax.optimization_barrier((voltages, ending))
    handed = [
        lax.ppermute(ending, "fgrp", [(i, i + 1) for i in range(first, owners - 1, 2)])
        for first in range(2)
    ]
    (early,) = filter_part(voltages, tables, 0, 1, TAPS)
    handed, early = lax.optimization_barrier((handed, early))
    partial = combine(early, late, *handed, jnp.swapaxes(gains, 1, 2), frames_here, owners)
    turned = lax.all_to_all(partial, "fgrp", split_axis=0, concat_axis=0, tiled=True)
    own, left = merge(turned, frames_here, share, norm)
    tiles, pols = lax.axis_size("tile"), lax.axis_size("pol")
    if inputs_here % 128:
        wide = lax.all_gather(lax.all_gather(own, "pol", axis=0), "tile", axis=0)
        return correlate_whole(left, wide.reshape((-1,) + own.shape), share)
    tile, pol = lax.axis_index("tile"), lax.axis_index("pol")

    def place(by_tile, by_pol):
        return (peer(tile, by_tile, tiles, -1) * pols + peer(pol, by_pol, pols, -1)).astype(jnp.int32)

    total = tiles * pols * inputs_here
    result = None
    for by_pol in range(pols):
        near = swapped(own, "pol", by_pol)
        if by_pol:
            near, result = lax.optimization_barrier((near, result))
        for by_tile in range(tiles):
            right = swapped(near, "tile", by_tile)
            where = place(by_tile, by_pol).reshape(1)
            result = correlate(left, right, where, total, result, share)
    return result


def solution(mesh):
    placed = (P(None, ("tile", "pol"), "fgrp"), P(None, ("tile", "pol"), None))
    return jax.shard_map(
        body,
        mesh=mesh,
        in_specs=placed,
        out_specs=P("fgrp", None, ("tile", "pol"), None),
        check_vma=False,
    )
```

```python
import functools
import math

import jax
import jax.numpy as jnp
import ml_dtypes
import numpy as np
from jax import lax
from jax.experimental import pallas as pl
from jax.experimental.pallas import tpu as pltpu
from jax.sharding import PartitionSpec as P

NFFT = 4096
TAPS = 4


def filter_taps():
    span = TAPS * NFFT
    position = np.arange(span, dtype=np.float64)
    centred = (position - span / 2 + 0.5) / NFFT
    window = 0.5 - 0.5 * np.cos(2.0 * np.pi * (position + 0.5) / span)
    return (np.sinc(centred) * window).reshape(TAPS, NFFT)


def tap_order():
    energy = (filter_taps() ** 2).sum(axis=1)
    order = list(range(TAPS))[::-1]
    return order, [t for t in order if energy[t] > 0.01 * energy.sum()]


def filter_table(channels):
    order, low_order = tap_order()
    phases = np.arange(NFFT)[:, None] * np.arange(channels)[None, :] % NFFT
    angles = phases * (2.0 * np.pi / NFFT)
    transform = np.concatenate([np.cos(angles), np.sin(angles)], axis=1) / math.sqrt(NFFT)
    blocks = {t: filter_taps()[t][:, None] * transform for t in order}
    high = {t: b.astype(np.float32).astype(ml_dtypes.bfloat16) for t, b in blocks.items()}
    low = np.concatenate([blocks[t] - high[t].astype(np.float64) for t in low_order], axis=1)
    scale = 2.0 ** np.floor(np.log2(256.0 / np.abs(low).max()))
    low = (low * scale).astype(np.float32).astype(ml_dtypes.float8_e4m3fn)
    high = np.concatenate([high[t] for t in order], axis=1)
    return np.ascontiguousarray(high.T), np.ascontiguousarray(low.T), float(1.0 / scale)


def peer(me, step, length, way):
    if length & (length - 1):
        return (me + way * step) % length
    return me ^ step


def filter_kernel(frame, low_from, low_scale, volt_hbm, table_hbm, low_hbm, *refs):
    out_refs, scratch = refs[:-9], refs[-9:]
    sums, low_sums, volts, table, low_table, volt_here, first_here, table_here, low_here = scratch
    order, low_order = tap_order()
    width = table.shape[0] // len(order)
    half = width // 2
    count = sums.shape[1] // width - (TAPS - 1)
    steps = 2 * (low_sums.shape[1] // width - (len(low_order) - 1))
    pieces = first_here.shape[0]
    depth = NFFT // pieces

    def block(step):
        slot = lax.rem(step, 2)
        samples = pl.ds(pl.multiple_of((lax.div(step, 2) + frame) * NFFT, NFFT), NFFT)
        return pltpu.make_async_copy(
            volt_hbm.at[slot, :, samples], volts.at[slot], volt_here.at[slot]
        )

    def fetch(piece):
        part = pl.ds(piece * depth, depth)
        samples = pl.ds(frame * NFFT + piece * depth, depth)
        return [
            pltpu.make_async_copy(
                volt_hbm.at[0, :, samples], volts.at[0, :, part], first_here.at[piece]
            ),
            pltpu.make_async_copy(table_hbm.at[:, part], table.at[:, part], table_here.at[piece]),
            pltpu.make_async_copy(low_hbm.at[:, part], low_table.at[:, part], low_here.at[piece]),
        ]

    def product(left, right):
        return lax.dot_general(
            left, right, (((1,), (1,)), ((), ())), preferred_element_type=jnp.float32
        )

    def add(step, start, size):
        part = lax.rem(step, 2)
        first = pl.multiple_of(lax.div(step, 2) * width, width)
        here = pl.ds(first, len(order) * width)
        values = volts[part, :, start : start + size]
        sums[part, here, :] += product(table[:, start : start + size], values)

    def add_low(step, start, size):
        part = lax.rem(step, 2)
        first = pl.multiple_of(lax.div(step, 2) * width, width)
        here = pl.ds(first, len(low_order) * width)
        values = volts[part, :, start : start + size]
        low_sums[part, here, :] += product(
            low_table[:, start : start + size], values.astype(jnp.float8_e4m3fn)
        )

    for piece in range(pieces):
        for copy in fetch(piece):
            copy.start()
    block(1).start()
    sums[...] = jnp.zeros_like(sums)
    low_sums[...] = jnp.zeros_like(low_sums)
    for piece in range(pieces):
        for copy in fetch(piece):
            copy.wait()
        add(0, piece * depth, depth)
        if low_from == 0:
            add_low(0, piece * depth, depth)

    @pl.loop(1, steps)
    def _(step):
        block(step).wait()

        @pl.when(step + 1 < steps)
        def _():
            block(step + 1).start()

        whole = (step < 2 * count) & (step >= 2 * low_from)

        @pl.when(whole)
        def _():
            add(step, 0, NFFT)
            add_low(step, 0, NFFT)

        if low_from > 0:

            @pl.when(step < 2 * low_from)
            def _():
                add(step, 0, NFFT)

        if 2 * count < steps:

            @pl.when(step >= 2 * count)
            def _():
                add_low(step, 0, NFFT)

    kept = out_refs[0].shape[0] // width
    for slot in range(sums.shape[1] // width):
        both = [sums[c, slot * width : (slot + 1) * width, :] for c in range(2)]
        at = (slot - order.index(low_order[0])) * width
        if 0 <= at < low_sums.shape[1]:
            both = [both[c] + low_scale * low_sums[c, at : at + width, :] for c in range(2)]
        raw = jnp.concatenate(
            [both[0][:half] + both[1][half:], both[1][:half] - both[0][half:]], axis=0
        )
        if slot < kept:
            out_refs[0][slot * width : (slot + 1) * width, :] = raw
        else:
            at = (slot - kept) * width
            out_refs[1][at : at + width, :] = raw.astype(jnp.bfloat16)


def filter_part(voltages, tables, frame, count, low_from, low_to, kept):
    rows = voltages.shape[1]
    table, low_table, low_scale = tables
    width = table.shape[0] // TAPS
    slots = count + TAPS - 1
    low_slots = low_to + len(tap_order()[1]) - 1
    shapes = [jax.ShapeDtypeStruct((kept * width, rows), jnp.float32)]
    if slots > kept:
        shapes.append(jax.ShapeDtypeStruct(((slots - kept) * width, rows), jnp.bfloat16))
    pieces = 4
    return pl.pallas_call(
        functools.partial(filter_kernel, frame, low_from, low_scale),
        in_specs=[pl.BlockSpec(memory_space=pl.ANY)] * 3,
        out_specs=[pl.BlockSpec(memory_space=pltpu.VMEM)] * len(shapes),
        out_shape=shapes,
        scratch_shapes=[
            pltpu.VMEM((2, slots * width, rows), jnp.float32),
            pltpu.VMEM((2, low_slots * width, rows), jnp.float32),
            pltpu.VMEM((2, rows, NFFT), jnp.bfloat16),
            pltpu.VMEM(table.shape, jnp.bfloat16),
            pltpu.VMEM(low_table.shape, jnp.float8_e4m3fn),
            pltpu.SemaphoreType.DMA((2,)),
            pltpu.SemaphoreType.DMA((pieces,)),
            pltpu.SemaphoreType.DMA((pieces,)),
            pltpu.SemaphoreType.DMA((pieces,)),
        ],
        compiler_params=pltpu.CompilerParams(vmem_limit_bytes=52 * 2**20),
        cost_estimate=pl.CostEstimate(
            flops=2 * 2 * rows * count * NFFT * (table.shape[0] + low_table.shape[0]),
            bytes_accessed=2 * (2 * rows * count * NFFT + NFFT * table.shape[0]),
            transcendentals=0,
        ),
        name="filter_part",
    )(voltages, jnp.asarray(table), jnp.asarray(low_table))


def combine_kernel(early_ref, late_ref, handed_ref, gain_ref, out_ref):
    half = gain_ref.shape[1]
    width = 2 * half
    owners = out_ref.shape[0]
    share = half // owners
    for slot in range(out_ref.shape[1] // (2 * share)):
        raw = early_ref[slot * width : (slot + 1) * width, :] if slot < TAPS else 0.0
        if slot:
            raw = raw + late_ref[(slot - 1) * width : slot * width, :]
        if slot < TAPS - 1:
            raw = raw + handed_ref[slot * width : (slot + 1) * width, :].astype(jnp.float32)
        real, imag = raw[:half], raw[half:]
        out_real = gain_ref[0] * real - gain_ref[1] * imag
        out_imag = gain_ref[0] * imag + gain_ref[1] * real
        for owner in range(owners):
            at = owner * share
            pair = jnp.concatenate([out_real[at : at + share], out_imag[at : at + share]], axis=0)
            at = 2 * share * slot
            out_ref[owner, at : at + 2 * share, :] = pair.astype(jnp.bfloat16)


def combine(early, late, handed, gains, frames, owners):
    _, half, rows = gains.shape
    return pl.pallas_call(
        combine_kernel,
        in_specs=[pl.BlockSpec(memory_space=pltpu.VMEM)] * 4,
        out_specs=pl.BlockSpec(memory_space=pltpu.VMEM),
        out_shape=jax.ShapeDtypeStruct((owners, frames * 2 * half // owners, rows), jnp.bfloat16),
        compiler_params=pltpu.CompilerParams(vmem_limit_bytes=16 * 2**20),
        name="combine",
    )(early, late, handed, gains)


def merge_kernel(frames, share, norm, in_ref, out_ref, left_ref, scratch):
    owners = in_ref.shape[0]
    depth = 2 * owners * frames
    blocks = scratch.shape[0]
    for group in range(owners):
        for frame in range(frames):
            at = 2 * share * frame
            value = in_ref[group, at : at + 2 * share, :].astype(jnp.float32)
            if value.shape[1] < 128 * blocks:
                spare = jnp.zeros((2 * share, 128 * blocks - value.shape[1]), jnp.float32)
                value = jnp.concatenate([value, spare], axis=1)
            for part in range(2):
                row = (part * owners + group) * frames + frame
                for block in range(blocks):
                    scratch[block, pl.ds(row, share, stride=depth), :] = value[
                        part * share : (part + 1) * share, block * 128 : (block + 1) * 128
                    ]
    for block in range(blocks):
        lanes = min(128, out_ref.shape[1] - block * 128)
        at = block * 128
        for channel in range(share):
            rounded = scratch[block, channel * depth : (channel + 1) * depth, :].astype(jnp.bfloat16)
            out_ref[channel * depth : (channel + 1) * depth, at : at + lanes] = rounded[:, :lanes]
            scaled = norm * rounded.astype(jnp.float32)
            high = scaled.astype(jnp.bfloat16).astype(jnp.float32)
            both = jnp.concatenate([high, scaled - high], axis=0).T
            left_ref[at : at + lanes, 2 * channel * depth : 2 * (channel + 1) * depth] = both[
                :lanes
            ].astype(jnp.bfloat16)


def merge(turned, frames, share, norm):
    owners, in_rows, rows = turned.shape
    out_rows = share * 2 * owners * frames
    return pl.pallas_call(
        functools.partial(merge_kernel, frames, share, norm),
        in_specs=[pl.BlockSpec(memory_space=pltpu.VMEM)],
        out_shape=[
            jax.ShapeDtypeStruct((out_rows, rows), jnp.bfloat16),
            jax.ShapeDtypeStruct((rows, 2 * out_rows), jnp.bfloat16),
        ],
        scratch_shapes=[pltpu.VMEM((pl.cdiv(rows, 128), out_rows, 128), jnp.float32)],
        compiler_params=pltpu.CompilerParams(vmem_limit_bytes=16 * 2**20),
        name="merge",
    )(turned)


def visibility(left, right, kind):
    if kind:
        half = right.shape[0] // 2
        right = jnp.concatenate([-right[half:], right[:half]], axis=0)
    both = jnp.concatenate([right, right], axis=0)
    return jnp.dot(left, both, preferred_element_type=jnp.float32)


def block_kernel(share, place_ref, left_ref, right_ref, *refs):
    out_hbm, (values, written) = refs[-3], refs[-2:]
    depth = right_ref.shape[0] // share
    rows = right_ref.shape[1]
    slots = values.shape[0]
    columns = pl.ds(pl.multiple_of(place_ref[0] * rows, rows), rows)

    def write(channel, kind):
        slot = channel % slots
        return pltpu.make_async_copy(
            values.at[slot, kind], out_hbm.at[channel, kind, :, columns], written.at[slot, kind]
        )

    for channel in range(share):
        slot = channel % slots
        right = right_ref[depth * channel : depth * (channel + 1), :]
        for kind in range(2):
            if channel >= slots:
                write(channel - slots, kind).wait()
            values[slot, kind] = visibility(
                left_ref[:, 2 * depth * channel : 2 * depth * (channel + 1)], right, kind
            )
            write(channel, kind).start()
    for channel in range(max(share - slots, 0), share):
        for kind in range(2):
            write(channel, kind).wait()


def correlate(left, right, place, total, result, share):
    out_rows, rows = right.shape
    depth = out_rows // share
    slots = 4
    operands = [place, left, right]
    specs = [pl.BlockSpec(memory_space=pltpu.SMEM)] + [pl.BlockSpec(memory_space=pltpu.VMEM)] * 2
    aliases = {}
    if result is not None:
        aliases = {len(operands): 0}
        operands.append(result)
        specs.append(pl.BlockSpec(memory_space=pl.ANY))
    return pl.pallas_call(
        functools.partial(block_kernel, share),
        in_specs=specs,
        out_specs=pl.BlockSpec(memory_space=pl.ANY),
        out_shape=jax.ShapeDtypeStruct((share, 2, rows, total), jnp.float32),
        scratch_shapes=[
            pltpu.VMEM((slots, 2, rows, rows), jnp.float32),
            pltpu.SemaphoreType.DMA((slots, 2)),
        ],
        input_output_aliases=aliases,
        compiler_params=pltpu.CompilerParams(vmem_limit_bytes=24 * 2**20),
        cost_estimate=pl.CostEstimate(
            flops=8 * share * rows * rows * depth,
            bytes_accessed=4 * share * 2 * rows * rows,
            transcendentals=0,
        ),
        name="correlate",
    )(*operands)


def whole_kernel(left_ref, all_ref, out_ref):
    rows = left_ref.shape[0]
    for group in range(all_ref.shape[0]):
        for kind in range(2):
            out_ref[0, kind, :, group * rows : (group + 1) * rows] = visibility(
                left_ref[...], all_ref[group], kind
            )


def correlate_whole(left, gathered, share):
    groups, out_rows, rows = gathered.shape
    depth = out_rows // share
    return pl.pallas_call(
        whole_kernel,
        grid=(share,),
        in_specs=[
            pl.BlockSpec((rows, 2 * depth), lambda c: (0, c)),
            pl.BlockSpec((groups, depth, rows), lambda c: (0, c, 0)),
        ],
        out_specs=pl.BlockSpec((1, 2, rows, groups * rows), lambda c: (c, 0, 0, 0)),
        out_shape=jax.ShapeDtypeStruct((share, 2, rows, groups * rows), jnp.float32),
        compiler_params=pltpu.CompilerParams(vmem_limit_bytes=24 * 2**20),
        name="correlate_whole",
    )(left, gathered)


def swapped(shard, axis, step):
    if step == 0:
        return shard
    length = lax.axis_size(axis)
    return lax.ppermute(shard, axis, [(i, peer(i, step, length, 1)) for i in range(length)])


def body(voltages, gains):
    inputs_here = voltages.shape[1]
    frames_here = voltages.shape[2] // NFFT
    channels = gains.shape[2]
    owners = lax.axis_size("fgrp")
    share = channels // owners
    norm = 1.0 / math.sqrt(frames_here * owners)
    tables = filter_table(channels)
    late, ending = filter_part(
        voltages, tables, 1, frames_here - 1, 1, frames_here - 1, frames_here - 1
    )
    voltages, ending = lax.optimization_barrier((voltages, ending))
    handed = lax.ppermute(ending, "fgrp", [(i, i + 1) for i in range(owners - 1)])
    (early,) = filter_part(voltages, tables, 0, 1, 0, 2, TAPS)
    handed, early = lax.optimization_barrier((handed, early))
    partial = combine(early, late, handed, jnp.swapaxes(gains, 1, 2), frames_here, owners)
    turned = lax.all_to_all(partial, "fgrp", split_axis=0, concat_axis=0, tiled=True)
    own, left = merge(turned, frames_here, share, norm)
    tiles, pols = lax.axis_size("tile"), lax.axis_size("pol")
    if inputs_here % 128:
        wide = lax.all_gather(lax.all_gather(own, "pol", axis=0), "tile", axis=0)
        return correlate_whole(left, wide.reshape((-1,) + own.shape), share)
    tile, pol = lax.axis_index("tile"), lax.axis_index("pol")

    def place(by_tile, by_pol):
        return (peer(tile, by_tile, tiles, -1) * pols + peer(pol, by_pol, pols, -1)).astype(jnp.int32)

    total = tiles * pols * inputs_here
    result = None
    for by_pol in range(pols):
        near = swapped(own, "pol", by_pol)
        if by_pol:
            near, result = lax.optimization_barrier((near, result))
        for by_tile in range(tiles):
            right = swapped(near, "tile", by_tile)
            where = place(by_tile, by_pol).reshape(1)
            result = correlate(left, right, where, total, result, share)
    return result


def solution(mesh):
    placed = (P(None, ("tile", "pol"), "fgrp"), P(None, ("tile", "pol"), None))
    return jax.shard_map(
        body,
        mesh=mesh,
        in_specs=placed,
        out_specs=P("fgrp", None, ("tile", "pol"), None),
        check_vma=False,
    )
```

```python
import functools
import math

import jax
import jax.numpy as jnp
import ml_dtypes
import numpy as np
from jax import lax
from jax.experimental import pallas as pl
from jax.experimental.pallas import tpu as pltpu
from jax.sharding import PartitionSpec as P

NFFT = 4096
TAPS = 4


def filter_taps():
    span = TAPS * NFFT
    position = np.arange(span, dtype=np.float64)
    centred = (position - span / 2 + 0.5) / NFFT
    window = 0.5 - 0.5 * np.cos(2.0 * np.pi * (position + 0.5) / span)
    return (np.sinc(centred) * window).reshape(TAPS, NFFT)


def tap_order():
    energy = (filter_taps() ** 2).sum(axis=1)
    order = list(range(TAPS))[::-1]
    return order, [t for t in order if energy[t] > 0.01 * energy.sum()]


def filter_table(channels):
    order, low_order = tap_order()
    phases = np.arange(NFFT)[:, None] * np.arange(channels)[None, :] % NFFT
    angles = phases * (2.0 * np.pi / NFFT)
    transform = np.concatenate([np.cos(angles), np.sin(angles)], axis=1) / math.sqrt(NFFT)
    blocks = {t: filter_taps()[t][:, None] * transform for t in order}
    high = {t: b.astype(np.float32).astype(ml_dtypes.bfloat16) for t, b in blocks.items()}
    low = np.concatenate([blocks[t] - high[t].astype(np.float64) for t in low_order], axis=1)
    scale = 2.0 ** np.floor(np.log2(256.0 / np.abs(low).max()))
    low = (low * scale).astype(np.float32).astype(ml_dtypes.float8_e4m3fn)
    high = np.concatenate([high[t] for t in order], axis=1)
    return np.ascontiguousarray(high.T), np.ascontiguousarray(low.T), float(1.0 / scale)


def peer(me, step, length, way):
    if length & (length - 1):
        return (me + way * step) % length
    return me ^ step


def filter_kernel(frame, low_scale, volt_hbm, table_hbm, low_hbm, *refs):
    out_refs, scratch = refs[:-9], refs[-9:]
    sums, low_sums, volts, table, low_table, volt_here, first_here, table_here, low_here = scratch
    order, low_order = tap_order()
    width = table.shape[0] // len(order)
    half = width // 2
    count = sums.shape[1] // width - (TAPS - 1)
    pieces = first_here.shape[0]
    depth = NFFT // pieces

    def block(at, part):
        slot = 2 * lax.rem(at, 2) + part
        samples = pl.ds(pl.multiple_of((at + frame) * NFFT, NFFT), NFFT)
        return pltpu.make_async_copy(
            volt_hbm.at[part, :, samples], volts.at[slot], volt_here.at[slot]
        )

    def fetch(piece):
        part = pl.ds(piece * depth, depth)
        samples = pl.ds(frame * NFFT + piece * depth, depth)
        return [
            pltpu.make_async_copy(
                volt_hbm.at[0, :, samples], volts.at[0, :, part], first_here.at[piece]
            ),
            pltpu.make_async_copy(table_hbm.at[:, part], table.at[:, part], table_here.at[piece]),
            pltpu.make_async_copy(low_hbm.at[:, part], low_table.at[:, part], low_here.at[piece]),
        ]

    def product(left, right):
        return lax.dot_general(
            left, right, (((1,), (1,)), ((), ())), preferred_element_type=jnp.float32
        )

    def add(at, part, start, size):
        first = pl.multiple_of(at * width, width)
        here = pl.ds(first, len(order) * width)
        low = pl.ds(first, len(low_order) * width)
        values = volts[2 * lax.rem(at, 2) + part, :, start : start + size]
        sums[part, here, :] += product(table[:, start : start + size], values)
        low_sums[part, low, :] += product(
            low_table[:, start : start + size], values.astype(jnp.float8_e4m3fn)
        )

    for piece in range(pieces):
        for copy in fetch(piece):
            copy.start()
    block(0, 1).start()
    sums[...] = jnp.zeros_like(sums)
    low_sums[...] = jnp.zeros_like(low_sums)
    for piece in range(pieces):
        for copy in fetch(piece):
            copy.wait()
        add(0, 0, piece * depth, depth)
    if count > 1:
        for part in range(2):
            block(1, part).start()
    block(0, 1).wait()
    add(0, 1, 0, NFFT)

    @pl.loop(1, count)
    def _(at):
        for part in range(2):
            block(at, part).wait()

        @pl.when(at + 1 < count)
        def _():
            for part in range(2):
                block(at + 1, part).start()

        for part in range(2):
            add(at, part, 0, NFFT)

    kept = out_refs[0].shape[0] // width
    for slot in range(sums.shape[1] // width):
        both = [sums[c, slot * width : (slot + 1) * width, :] for c in range(2)]
        at = (slot - order.index(low_order[0])) * width
        if 0 <= at < low_sums.shape[1]:
            both = [both[c] + low_scale * low_sums[c, at : at + width, :] for c in range(2)]
        raw = jnp.concatenate(
            [both[0][:half] + both[1][half:], both[1][:half] - both[0][half:]], axis=0
        )
        if slot < kept:
            out_refs[0][slot * width : (slot + 1) * width, :] = raw
        else:
            at = (slot - kept) * width
            out_refs[1][at : at + width, :] = raw.astype(jnp.bfloat16)


def filter_part(voltages, tables, frame, count, kept):
    rows = voltages.shape[1]
    table, low_table, low_scale = tables
    width = table.shape[0] // TAPS
    slots = count + TAPS - 1
    low_slots = count + len(tap_order()[1]) - 1
    shapes = [jax.ShapeDtypeStruct((kept * width, rows), jnp.float32)]
    if slots > kept:
        shapes.append(jax.ShapeDtypeStruct(((slots - kept) * width, rows), jnp.bfloat16))
    pieces = 4
    return pl.pallas_call(
        functools.partial(filter_kernel, frame, low_scale),
        in_specs=[pl.BlockSpec(memory_space=pl.ANY)] * 3,
        out_specs=[pl.BlockSpec(memory_space=pltpu.VMEM)] * len(shapes),
        out_shape=shapes,
        scratch_shapes=[
            pltpu.VMEM((2, slots * width, rows), jnp.float32),
            pltpu.VMEM((2, low_slots * width, rows), jnp.float32),
            pltpu.VMEM((4, rows, NFFT), jnp.bfloat16),
            pltpu.VMEM(table.shape, jnp.bfloat16),
            pltpu.VMEM(low_table.shape, jnp.float8_e4m3fn),
            pltpu.SemaphoreType.DMA((4,)),
            pltpu.SemaphoreType.DMA((pieces,)),
            pltpu.SemaphoreType.DMA((pieces,)),
            pltpu.SemaphoreType.DMA((pieces,)),
        ],
        compiler_params=pltpu.CompilerParams(vmem_limit_bytes=52 * 2**20),
        cost_estimate=pl.CostEstimate(
            flops=2 * 2 * rows * count * NFFT * (table.shape[0] + low_table.shape[0]),
            bytes_accessed=2 * (2 * rows * count * NFFT + NFFT * table.shape[0]),
            transcendentals=0,
        ),
        name="filter_part",
    )(voltages, jnp.asarray(table), jnp.asarray(low_table))


def combine_kernel(early_ref, late_ref, handed_ref, gain_ref, out_ref):
    half = gain_ref.shape[1]
    width = 2 * half
    owners = out_ref.shape[0]
    share = half // owners
    for slot in range(out_ref.shape[1] // (2 * share)):
        raw = early_ref[slot * width : (slot + 1) * width, :] if slot < TAPS else 0.0
        if slot:
            raw = raw + late_ref[(slot - 1) * width : slot * width, :]
        if slot < TAPS - 1:
            raw = raw + handed_ref[slot * width : (slot + 1) * width, :].astype(jnp.float32)
        real, imag = raw[:half], raw[half:]
        out_real = gain_ref[0] * real - gain_ref[1] * imag
        out_imag = gain_ref[0] * imag + gain_ref[1] * real
        for owner in range(owners):
            at = owner * share
            pair = jnp.concatenate([out_real[at : at + share], out_imag[at : at + share]], axis=0)
            at = 2 * share * slot
            out_ref[owner, at : at + 2 * share, :] = pair.astype(jnp.bfloat16)


def combine(early, late, handed, gains, frames, owners):
    _, half, rows = gains.shape
    return pl.pallas_call(
        combine_kernel,
        in_specs=[pl.BlockSpec(memory_space=pltpu.VMEM)] * 4,
        out_specs=pl.BlockSpec(memory_space=pltpu.VMEM),
        out_shape=jax.ShapeDtypeStruct((owners, frames * 2 * half // owners, rows), jnp.bfloat16),
        compiler_params=pltpu.CompilerParams(vmem_limit_bytes=16 * 2**20),
        name="combine",
    )(early, late, handed, gains)


def merge_kernel(frames, share, norm, in_ref, out_ref, left_ref, scratch):
    owners = in_ref.shape[0]
    depth = 2 * owners * frames
    blocks = scratch.shape[0]
    for group in range(owners):
        for frame in range(frames):
            at = 2 * share * frame
            value = in_ref[group, at : at + 2 * share, :].astype(jnp.float32)
            if value.shape[1] < 128 * blocks:
                spare = jnp.zeros((2 * share, 128 * blocks - value.shape[1]), jnp.float32)
                value = jnp.concatenate([value, spare], axis=1)
            for part in range(2):
                row = (part * owners + group) * frames + frame
                for block in range(blocks):
                    scratch[block, pl.ds(row, share, stride=depth), :] = value[
                        part * share : (part + 1) * share, block * 128 : (block + 1) * 128
                    ]
    for block in range(blocks):
        lanes = min(128, out_ref.shape[1] - block * 128)
        at = block * 128
        for channel in range(share):
            rounded = scratch[block, channel * depth : (channel + 1) * depth, :].astype(jnp.bfloat16)
            out_ref[channel * depth : (channel + 1) * depth, at : at + lanes] = rounded[:, :lanes]
            scaled = norm * rounded.astype(jnp.float32)
            high = scaled.astype(jnp.bfloat16).astype(jnp.float32)
            both = jnp.concatenate([high, scaled - high], axis=0).T
            left_ref[at : at + lanes, 2 * channel * depth : 2 * (channel + 1) * depth] = both[
                :lanes
            ].astype(jnp.bfloat16)


def merge(turned, frames, share, norm):
    owners, in_rows, rows = turned.shape
    out_rows = share * 2 * owners * frames
    return pl.pallas_call(
        functools.partial(merge_kernel, frames, share, norm),
        in_specs=[pl.BlockSpec(memory_space=pltpu.VMEM)],
        out_shape=[
            jax.ShapeDtypeStruct((out_rows, rows), jnp.bfloat16),
            jax.ShapeDtypeStruct((rows, 2 * out_rows), jnp.bfloat16),
        ],
        scratch_shapes=[pltpu.VMEM((pl.cdiv(rows, 128), out_rows, 128), jnp.float32)],
        compiler_params=pltpu.CompilerParams(vmem_limit_bytes=16 * 2**20),
        name="merge",
    )(turned)


def visibility(left, right, kind):
    if kind:
        half = right.shape[0] // 2
        right = jnp.concatenate([-right[half:], right[:half]], axis=0)
    both = jnp.concatenate([right, right], axis=0)
    return jnp.dot(left, both, preferred_element_type=jnp.float32)


def block_kernel(share, place_ref, left_ref, right_ref, *refs):
    out_hbm, (values, written) = refs[-3], refs[-2:]
    depth = right_ref.shape[0] // share
    rows = right_ref.shape[1]
    slots = values.shape[0]
    columns = pl.ds(pl.multiple_of(place_ref[0] * rows, rows), rows)

    def write(channel, kind):
        slot = channel % slots
        return pltpu.make_async_copy(
            values.at[slot, kind], out_hbm.at[channel, kind, :, columns], written.at[slot, kind]
        )

    for channel in range(share):
        slot = channel % slots
        right = right_ref[depth * channel : depth * (channel + 1), :]
        for kind in range(2):
            if channel >= slots:
                write(channel - slots, kind).wait()
            values[slot, kind] = visibility(
                left_ref[:, 2 * depth * channel : 2 * depth * (channel + 1)], right, kind
            )
            write(channel, kind).start()
    for channel in range(max(share - slots, 0), share):
        for kind in range(2):
            write(channel, kind).wait()


def correlate(left, right, place, total, result, share):
    out_rows, rows = right.shape
    depth = out_rows // share
    slots = 4
    operands = [place, left, right]
    specs = [pl.BlockSpec(memory_space=pltpu.SMEM)] + [pl.BlockSpec(memory_space=pltpu.VMEM)] * 2
    aliases = {}
    if result is not None:
        aliases = {len(operands): 0}
        operands.append(result)
        specs.append(pl.BlockSpec(memory_space=pl.ANY))
    return pl.pallas_call(
        functools.partial(block_kernel, share),
        in_specs=specs,
        out_specs=pl.BlockSpec(memory_space=pl.ANY),
        out_shape=jax.ShapeDtypeStruct((share, 2, rows, total), jnp.float32),
        scratch_shapes=[
            pltpu.VMEM((slots, 2, rows, rows), jnp.float32),
            pltpu.SemaphoreType.DMA((slots, 2)),
        ],
        input_output_aliases=aliases,
        compiler_params=pltpu.CompilerParams(vmem_limit_bytes=24 * 2**20),
        cost_estimate=pl.CostEstimate(
            flops=8 * share * rows * rows * depth,
            bytes_accessed=4 * share * 2 * rows * rows,
            transcendentals=0,
        ),
        name="correlate",
    )(*operands)


def whole_kernel(left_ref, all_ref, out_ref):
    rows = left_ref.shape[0]
    for group in range(all_ref.shape[0]):
        for kind in range(2):
            out_ref[0, kind, :, group * rows : (group + 1) * rows] = visibility(
                left_ref[...], all_ref[group], kind
            )


def correlate_whole(left, gathered, share):
    groups, out_rows, rows = gathered.shape
    depth = out_rows // share
    return pl.pallas_call(
        whole_kernel,
        grid=(share,),
        in_specs=[
            pl.BlockSpec((rows, 2 * depth), lambda c: (0, c)),
            pl.BlockSpec((groups, depth, rows), lambda c: (0, c, 0)),
        ],
        out_specs=pl.BlockSpec((1, 2, rows, groups * rows), lambda c: (c, 0, 0, 0)),
        out_shape=jax.ShapeDtypeStruct((share, 2, rows, groups * rows), jnp.float32),
        compiler_params=pltpu.CompilerParams(vmem_limit_bytes=24 * 2**20),
        name="correlate_whole",
    )(left, gathered)


def swapped(shard, axis, step):
    if step == 0:
        return shard
    length = lax.axis_size(axis)
    return lax.ppermute(shard, axis, [(i, peer(i, step, length, 1)) for i in range(length)])


def body(voltages, gains):
    inputs_here = voltages.shape[1]
    frames_here = voltages.shape[2] // NFFT
    channels = gains.shape[2]
    owners = lax.axis_size("fgrp")
    share = channels // owners
    norm = 1.0 / math.sqrt(frames_here * owners)
    tables = filter_table(channels)
    late, ending = filter_part(voltages, tables, 1, frames_here - 1, frames_here - 1)
    voltages, ending = lax.optimization_barrier((voltages, ending))
    handed = lax.ppermute(ending, "fgrp", [(i, i + 1) for i in range(owners - 1)])
    (early,) = filter_part(voltages, tables, 0, 1, TAPS)
    handed, early = lax.optimization_barrier((handed, early))
    partial = combine(early, late, handed, jnp.swapaxes(gains, 1, 2), frames_here, owners)
    turned = lax.all_to_all(partial, "fgrp", split_axis=0, concat_axis=0, tiled=True)
    own, left = merge(turned, frames_here, share, norm)
    tiles, pols = lax.axis_size("tile"), lax.axis_size("pol")
    if inputs_here % 128:
        wide = lax.all_gather(lax.all_gather(own, "pol", axis=0), "tile", axis=0)
        return correlate_whole(left, wide.reshape((-1,) + own.shape), share)
    tile, pol = lax.axis_index("tile"), lax.axis_index("pol")

    def place(by_tile, by_pol):
        return (peer(tile, by_tile, tiles, -1) * pols + peer(pol, by_pol, pols, -1)).astype(jnp.int32)

    total = tiles * pols * inputs_here
    result = None
    for by_pol in range(pols):
        near = swapped(own, "pol", by_pol)
        if by_pol:
            near, result = lax.optimization_barrier((near, result))
        for by_tile in range(tiles):
            right = swapped(near, "tile", by_tile)
            where = place(by_tile, by_pol).reshape(1)
            result = correlate(left, right, where, total, result, share)
    return result


def solution(mesh):
    placed = (P(None, ("tile", "pol"), "fgrp"), P(None, ("tile", "pol"), None))
    return jax.shard_map(
        body,
        mesh=mesh,
        in_specs=placed,
        out_specs=P("fgrp", None, ("tile", "pol"), None),
        check_vma=False,
    )
```

```python
import functools
import math

import jax
import jax.numpy as jnp
import ml_dtypes
import numpy as np
from jax import lax
from jax.experimental import pallas as pl
from jax.experimental.pallas import tpu as pltpu
from jax.sharding import PartitionSpec as P

NFFT = 4096
TAPS = 4


def filter_taps():
    span = TAPS * NFFT
    position = np.arange(span, dtype=np.float64)
    centred = (position - span / 2 + 0.5) / NFFT
    window = 0.5 - 0.5 * np.cos(2.0 * np.pi * (position + 0.5) / span)
    return (np.sinc(centred) * window).reshape(TAPS, NFFT)


def tap_order():
    energy = (filter_taps() ** 2).sum(axis=1)
    order = list(range(TAPS))[::-1]
    return order, [t for t in order if energy[t] > 0.01 * energy.sum()]


def filter_table(channels):
    order, low_order = tap_order()
    phases = np.arange(NFFT)[:, None] * np.arange(channels)[None, :] % NFFT
    angles = phases * (2.0 * np.pi / NFFT)
    transform = np.concatenate([np.cos(angles), np.sin(angles)], axis=1) / math.sqrt(NFFT)
    blocks = {t: filter_taps()[t][:, None] * transform for t in order}
    high = {t: b.astype(np.float32).astype(ml_dtypes.bfloat16) for t, b in blocks.items()}
    low = np.concatenate([blocks[t] - high[t].astype(np.float64) for t in low_order], axis=1)
    scale = 2.0 ** np.floor(np.log2(256.0 / np.abs(low).max()))
    low = (low * scale).astype(np.float32).astype(ml_dtypes.float8_e4m3fn)
    high = np.concatenate([high[t] for t in order], axis=1)
    return np.ascontiguousarray(high.T), np.ascontiguousarray(low.T), float(1.0 / scale)


def peer(me, step, length, way):
    if length & (length - 1):
        return (me + way * step) % length
    return me ^ step


def filter_kernel(frame, low_scale, volt_hbm, table_hbm, low_hbm, *refs):
    out_refs, scratch = refs[:-9], refs[-9:]
    sums, low_sums, volts, table, low_table, volt_here, first_here, table_here, low_here = scratch
    order, low_order = tap_order()
    width = table.shape[0] // len(order)
    half = width // 2
    count = sums.shape[1] // width - (TAPS - 1)
    pieces = first_here.shape[0]
    depth = NFFT // pieces

    def block(at, part):
        slot = 2 * lax.rem(at, 2) + part
        samples = pl.ds(pl.multiple_of((at + frame) * NFFT, NFFT), NFFT)
        return pltpu.make_async_copy(
            volt_hbm.at[part, :, samples], volts.at[slot], volt_here.at[slot]
        )

    def fetch(piece):
        part = pl.ds(piece * depth, depth)
        samples = pl.ds(frame * NFFT + piece * depth, depth)
        return [
            pltpu.make_async_copy(
                volt_hbm.at[0, :, samples], volts.at[0, :, part], first_here.at[piece]
            ),
            pltpu.make_async_copy(table_hbm.at[:, part], table.at[:, part], table_here.at[piece]),
            pltpu.make_async_copy(low_hbm.at[:, part], low_table.at[:, part], low_here.at[piece]),
        ]

    def half_block(at):
        part = pl.ds(at * NFFT // 2, NFFT // 2)
        samples = pl.ds(frame * NFFT + at * NFFT // 2, NFFT // 2)
        return pltpu.make_async_copy(
            volt_hbm.at[1, :, samples], volts.at[1, :, part], volt_here.at[at]
        )

    def product(left, right):
        return lax.dot_general(
            left, right, (((1,), (1,)), ((), ())), preferred_element_type=jnp.float32
        )

    def add(at, part, start, size):
        first = pl.multiple_of(at * width, width)
        here = pl.ds(first, len(order) * width)
        low = pl.ds(first, len(low_order) * width)
        values = volts[2 * lax.rem(at, 2) + part, :, start : start + size]
        sums[part, here, :] += product(table[:, start : start + size], values)
        low_sums[part, low, :] += product(
            low_table[:, start : start + size], values.astype(jnp.float8_e4m3fn)
        )

    for piece in range(pieces):
        for copy in fetch(piece):
            copy.start()
    halves = [half_block(0), half_block(1)]
    for copy in halves:
        copy.start()
    sums[...] = jnp.zeros_like(sums)
    low_sums[...] = jnp.zeros_like(low_sums)
    for piece in range(pieces):
        for copy in fetch(piece):
            copy.wait()
        add(0, 0, piece * depth, depth)
    if count > 1:
        for part in range(2):
            block(1, part).start()
    for at, copy in enumerate(halves):
        copy.wait()
        add(0, 1, at * NFFT // 2, NFFT // 2)

    @pl.loop(1, count)
    def _(at):
        for part in range(2):
            block(at, part).wait()

        @pl.when(at + 1 < count)
        def _():
            for part in range(2):
                block(at + 1, part).start()

        for part in range(2):
            add(at, part, 0, NFFT)

    kept = out_refs[0].shape[0] // width
    for slot in range(sums.shape[1] // width):
        both = [sums[c, slot * width : (slot + 1) * width, :] for c in range(2)]
        at = (slot - order.index(low_order[0])) * width
        if 0 <= at < low_sums.shape[1]:
            both = [both[c] + low_scale * low_sums[c, at : at + width, :] for c in range(2)]
        raw = jnp.concatenate(
            [both[0][:half] + both[1][half:], both[1][:half] - both[0][half:]], axis=0
        )
        if slot < kept:
            out_refs[0][slot * width : (slot + 1) * width, :] = raw
        else:
            at = (slot - kept) * width
            out_refs[1][at : at + width, :] = raw.astype(jnp.bfloat16)


def filter_part(voltages, tables, frame, count, kept):
    rows = voltages.shape[1]
    table, low_table, low_scale = tables
    width = table.shape[0] // TAPS
    slots = count + TAPS - 1
    low_slots = count + len(tap_order()[1]) - 1
    shapes = [jax.ShapeDtypeStruct((kept * width, rows), jnp.float32)]
    if slots > kept:
        shapes.append(jax.ShapeDtypeStruct(((slots - kept) * width, rows), jnp.bfloat16))
    pieces = 4
    return pl.pallas_call(
        functools.partial(filter_kernel, frame, low_scale),
        in_specs=[pl.BlockSpec(memory_space=pl.ANY)] * 3,
        out_specs=[pl.BlockSpec(memory_space=pltpu.VMEM)] * len(shapes),
        out_shape=shapes,
        scratch_shapes=[
            pltpu.VMEM((2, slots * width, rows), jnp.float32),
            pltpu.VMEM((2, low_slots * width, rows), jnp.float32),
            pltpu.VMEM((4, rows, NFFT), jnp.bfloat16),
            pltpu.VMEM(table.shape, jnp.bfloat16),
            pltpu.VMEM(low_table.shape, jnp.float8_e4m3fn),
            pltpu.SemaphoreType.DMA((4,)),
            pltpu.SemaphoreType.DMA((pieces,)),
            pltpu.SemaphoreType.DMA((pieces,)),
            pltpu.SemaphoreType.DMA((pieces,)),
        ],
        compiler_params=pltpu.CompilerParams(vmem_limit_bytes=52 * 2**20),
        cost_estimate=pl.CostEstimate(
            flops=2 * 2 * rows * count * NFFT * (table.shape[0] + low_table.shape[0]),
            bytes_accessed=2 * (2 * rows * count * NFFT + NFFT * table.shape[0]),
            transcendentals=0,
        ),
        name="filter_part",
    )(voltages, jnp.asarray(table), jnp.asarray(low_table))


def combine_kernel(early_ref, late_ref, handed_ref, gain_ref, out_ref):
    half = gain_ref.shape[1]
    width = 2 * half
    owners = out_ref.shape[0]
    share = half // owners
    for slot in range(out_ref.shape[1] // (2 * share)):
        raw = early_ref[slot * width : (slot + 1) * width, :] if slot < TAPS else 0.0
        if slot:
            raw = raw + late_ref[(slot - 1) * width : slot * width, :]
        if slot < TAPS - 1:
            raw = raw + handed_ref[slot * width : (slot + 1) * width, :].astype(jnp.float32)
        real, imag = raw[:half], raw[half:]
        out_real = gain_ref[0] * real - gain_ref[1] * imag
        out_imag = gain_ref[0] * imag + gain_ref[1] * real
        for owner in range(owners):
            at = owner * share
            pair = jnp.concatenate([out_real[at : at + share], out_imag[at : at + share]], axis=0)
            at = 2 * share * slot
            out_ref[owner, at : at + 2 * share, :] = pair.astype(jnp.bfloat16)


def combine(early, late, handed, gains, frames, owners):
    _, half, rows = gains.shape
    return pl.pallas_call(
        combine_kernel,
        in_specs=[pl.BlockSpec(memory_space=pltpu.VMEM)] * 4,
        out_specs=pl.BlockSpec(memory_space=pltpu.VMEM),
        out_shape=jax.ShapeDtypeStruct((owners, frames * 2 * half // owners, rows), jnp.bfloat16),
        compiler_params=pltpu.CompilerParams(vmem_limit_bytes=16 * 2**20),
        name="combine",
    )(early, late, handed, gains)


def merge_kernel(frames, share, norm, in_ref, out_ref, left_ref, scratch):
    owners = in_ref.shape[0]
    depth = 2 * owners * frames
    blocks = scratch.shape[0]
    for group in range(owners):
        for frame in range(frames):
            at = 2 * share * frame
            value = in_ref[group, at : at + 2 * share, :].astype(jnp.float32)
            if value.shape[1] < 128 * blocks:
                spare = jnp.zeros((2 * share, 128 * blocks - value.shape[1]), jnp.float32)
                value = jnp.concatenate([value, spare], axis=1)
            for part in range(2):
                row = (part * owners + group) * frames + frame
                for block in range(blocks):
                    scratch[block, pl.ds(row, share, stride=depth), :] = value[
                        part * share : (part + 1) * share, block * 128 : (block + 1) * 128
                    ]
    for block in range(blocks):
        lanes = min(128, out_ref.shape[1] - block * 128)
        at = block * 128
        for channel in range(share):
            rounded = scratch[block, channel * depth : (channel + 1) * depth, :].astype(jnp.bfloat16)
            out_ref[channel * depth : (channel + 1) * depth, at : at + lanes] = rounded[:, :lanes]
            scaled = norm * rounded.astype(jnp.float32)
            high = scaled.astype(jnp.bfloat16).astype(jnp.float32)
            both = jnp.concatenate([high, scaled - high], axis=0).T
            left_ref[at : at + lanes, 2 * channel * depth : 2 * (channel + 1) * depth] = both[
                :lanes
            ].astype(jnp.bfloat16)


def merge(turned, frames, share, norm):
    owners, in_rows, rows = turned.shape
    out_rows = share * 2 * owners * frames
    return pl.pallas_call(
        functools.partial(merge_kernel, frames, share, norm),
        in_specs=[pl.BlockSpec(memory_space=pltpu.VMEM)],
        out_shape=[
            jax.ShapeDtypeStruct((out_rows, rows), jnp.bfloat16),
            jax.ShapeDtypeStruct((rows, 2 * out_rows), jnp.bfloat16),
        ],
        scratch_shapes=[pltpu.VMEM((pl.cdiv(rows, 128), out_rows, 128), jnp.float32)],
        compiler_params=pltpu.CompilerParams(vmem_limit_bytes=16 * 2**20),
        name="merge",
    )(turned)


def visibility(left, right, kind):
    if kind:
        half = right.shape[0] // 2
        right = jnp.concatenate([-right[half:], right[:half]], axis=0)
    both = jnp.concatenate([right, right], axis=0)
    return jnp.dot(left, both, preferred_element_type=jnp.float32)


def block_kernel(share, place_ref, left_ref, right_ref, *refs):
    out_hbm, (values, written) = refs[-3], refs[-2:]
    depth = right_ref.shape[0] // share
    rows = right_ref.shape[1]
    slots = values.shape[0]
    columns = pl.ds(pl.multiple_of(place_ref[0] * rows, rows), rows)

    def write(channel, kind):
        slot = channel % slots
        return pltpu.make_async_copy(
            values.at[slot, kind], out_hbm.at[channel, kind, :, columns], written.at[slot, kind]
        )

    for channel in range(share):
        slot = channel % slots
        right = right_ref[depth * channel : depth * (channel + 1), :]
        for kind in range(2):
            if channel >= slots:
                write(channel - slots, kind).wait()
            values[slot, kind] = visibility(
                left_ref[:, 2 * depth * channel : 2 * depth * (channel + 1)], right, kind
            )
            write(channel, kind).start()
    for channel in range(max(share - slots, 0), share):
        for kind in range(2):
            write(channel, kind).wait()


def correlate(left, right, place, total, result, share):
    out_rows, rows = right.shape
    depth = out_rows // share
    slots = 4
    operands = [place, left, right]
    specs = [pl.BlockSpec(memory_space=pltpu.SMEM)] + [pl.BlockSpec(memory_space=pltpu.VMEM)] * 2
    aliases = {}
    if result is not None:
        aliases = {len(operands): 0}
        operands.append(result)
        specs.append(pl.BlockSpec(memory_space=pl.ANY))
    return pl.pallas_call(
        functools.partial(block_kernel, share),
        in_specs=specs,
        out_specs=pl.BlockSpec(memory_space=pl.ANY),
        out_shape=jax.ShapeDtypeStruct((share, 2, rows, total), jnp.float32),
        scratch_shapes=[
            pltpu.VMEM((slots, 2, rows, rows), jnp.float32),
            pltpu.SemaphoreType.DMA((slots, 2)),
        ],
        input_output_aliases=aliases,
        compiler_params=pltpu.CompilerParams(vmem_limit_bytes=24 * 2**20),
        cost_estimate=pl.CostEstimate(
            flops=8 * share * rows * rows * depth,
            bytes_accessed=4 * share * 2 * rows * rows,
            transcendentals=0,
        ),
        name="correlate",
    )(*operands)


def whole_kernel(left_ref, all_ref, out_ref):
    rows = left_ref.shape[0]
    for group in range(all_ref.shape[0]):
        for kind in range(2):
            out_ref[0, kind, :, group * rows : (group + 1) * rows] = visibility(
                left_ref[...], all_ref[group], kind
            )


def correlate_whole(left, gathered, share):
    groups, out_rows, rows = gathered.shape
    depth = out_rows // share
    return pl.pallas_call(
        whole_kernel,
        grid=(share,),
        in_specs=[
            pl.BlockSpec((rows, 2 * depth), lambda c: (0, c)),
            pl.BlockSpec((groups, depth, rows), lambda c: (0, c, 0)),
        ],
        out_specs=pl.BlockSpec((1, 2, rows, groups * rows), lambda c: (c, 0, 0, 0)),
        out_shape=jax.ShapeDtypeStruct((share, 2, rows, groups * rows), jnp.float32),
        compiler_params=pltpu.CompilerParams(vmem_limit_bytes=24 * 2**20),
        name="correlate_whole",
    )(left, gathered)


def swapped(shard, axis, step):
    if step == 0:
        return shard
    length = lax.axis_size(axis)
    return lax.ppermute(shard, axis, [(i, peer(i, step, length, 1)) for i in range(length)])


def body(voltages, gains):
    inputs_here = voltages.shape[1]
    frames_here = voltages.shape[2] // NFFT
    channels = gains.shape[2]
    owners = lax.axis_size("fgrp")
    share = channels // owners
    norm = 1.0 / math.sqrt(frames_here * owners)
    tables = filter_table(channels)
    late, ending = filter_part(voltages, tables, 1, frames_here - 1, frames_here - 1)
    voltages, ending = lax.optimization_barrier((voltages, ending))
    handed = lax.ppermute(ending, "fgrp", [(i, i + 1) for i in range(owners - 1)])
    (early,) = filter_part(voltages, tables, 0, 1, TAPS)
    handed, early = lax.optimization_barrier((handed, early))
    partial = combine(early, late, handed, jnp.swapaxes(gains, 1, 2), frames_here, owners)
    turned = lax.all_to_all(partial, "fgrp", split_axis=0, concat_axis=0, tiled=True)
    own, left = merge(turned, frames_here, share, norm)
    tiles, pols = lax.axis_size("tile"), lax.axis_size("pol")
    if inputs_here % 128:
        wide = lax.all_gather(lax.all_gather(own, "pol", axis=0), "tile", axis=0)
        return correlate_whole(left, wide.reshape((-1,) + own.shape), share)
    tile, pol = lax.axis_index("tile"), lax.axis_index("pol")

    def place(by_tile, by_pol):
        return (peer(tile, by_tile, tiles, -1) * pols + peer(pol, by_pol, pols, -1)).astype(jnp.int32)

    total = tiles * pols * inputs_here
    result = None
    far = [swapped(own, "pol", by_pol) for by_pol in range(pols)]
    for by_pol in range(pols):
        near = far[by_pol]
        if by_pol:
            near, result = lax.optimization_barrier((near, result))
        for by_tile in range(tiles):
            right = swapped(near, "tile", by_tile)
            where = place(by_tile, by_pol).reshape(1)
            result = correlate(left, right, where, total, result, share)
    return result


def solution(mesh):
    placed = (P(None, ("tile", "pol"), "fgrp"), P(None, ("tile", "pol"), None))
    return jax.shard_map(
        body,
        mesh=mesh,
        in_specs=placed,
        out_specs=P("fgrp", None, ("tile", "pol"), None),
        check_vma=False,
    )
```

```python
import functools
import math

import jax
import jax.numpy as jnp
import ml_dtypes
import numpy as np
from jax import lax
from jax.experimental import pallas as pl
from jax.experimental.pallas import tpu as pltpu
from jax.sharding import PartitionSpec as P

NFFT = 4096
TAPS = 4


def filter_taps():
    span = TAPS * NFFT
    position = np.arange(span, dtype=np.float64)
    centred = (position - span / 2 + 0.5) / NFFT
    window = 0.5 - 0.5 * np.cos(2.0 * np.pi * (position + 0.5) / span)
    return (np.sinc(centred) * window).reshape(TAPS, NFFT)


def tap_order():
    energy = (filter_taps() ** 2).sum(axis=1)
    order = list(range(TAPS))[::-1]
    return order, [t for t in order if energy[t] > 0.01 * energy.sum()]


def filter_table(channels):
    order, low_order = tap_order()
    phases = np.arange(NFFT)[:, None] * np.arange(channels)[None, :] % NFFT
    angles = phases * (2.0 * np.pi / NFFT)
    transform = np.concatenate([np.cos(angles), np.sin(angles)], axis=1) / math.sqrt(NFFT)
    blocks = {t: filter_taps()[t][:, None] * transform for t in order}
    high = {t: b.astype(np.float32).astype(ml_dtypes.bfloat16) for t, b in blocks.items()}
    low = np.concatenate([blocks[t] - high[t].astype(np.float64) for t in low_order], axis=1)
    scale = 2.0 ** np.floor(np.log2(256.0 / np.abs(low).max()))
    low = (low * scale).astype(np.float32).astype(ml_dtypes.float8_e4m3fn)
    high = np.concatenate([high[t] for t in order], axis=1)
    return np.ascontiguousarray(high.T), np.ascontiguousarray(low.T), float(1.0 / scale)


def peer(me, step, length, way):
    if length & (length - 1):
        return (me + way * step) % length
    return me ^ step


def filter_kernel(frame, low_scale, volt_hbm, table_hbm, low_hbm, *refs):
    out_refs, scratch = refs[:-9], refs[-9:]
    sums, low_sums, volts, table, low_table, volt_here, first_here, table_here, low_here = scratch
    order, low_order = tap_order()
    width = table.shape[0] // len(order)
    half = width // 2
    count = sums.shape[1] // width - (TAPS - 1)
    pieces = first_here.shape[0]
    depth = NFFT // pieces

    def block(at, part):
        slot = 2 * lax.rem(at, 2) + part
        samples = pl.ds(pl.multiple_of((at + frame) * NFFT, NFFT), NFFT)
        return pltpu.make_async_copy(
            volt_hbm.at[part, :, samples], volts.at[slot], volt_here.at[slot]
        )

    def fetch(piece):
        part = pl.ds(piece * depth, depth)
        samples = pl.ds(frame * NFFT + piece * depth, depth)
        return [
            pltpu.make_async_copy(
                volt_hbm.at[0, :, samples], volts.at[0, :, part], first_here.at[piece]
            ),
            pltpu.make_async_copy(table_hbm.at[:, part], table.at[:, part], table_here.at[piece]),
            pltpu.make_async_copy(low_hbm.at[:, part], low_table.at[:, part], low_here.at[piece]),
        ]

    def product(left, right):
        return lax.dot_general(
            left, right, (((1,), (1,)), ((), ())), preferred_element_type=jnp.float32
        )

    def add(at, part, start, size, kinds=(0, 1)):
        first = pl.multiple_of(at * width, width)
        here = pl.ds(first, len(order) * width)
        low = pl.ds(first, len(low_order) * width)
        values = volts[2 * lax.rem(at, 2) + part, :, start : start + size]
        if 0 in kinds:
            sums[part, here, :] += product(table[:, start : start + size], values)
        if 1 in kinds:
            low_sums[part, low, :] += product(
                low_table[:, start : start + size], values.astype(jnp.float8_e4m3fn)
            )

    for piece in range(pieces):
        for copy in fetch(piece):
            copy.start()
    block(0, 1).start()
    sums[...] = jnp.zeros_like(sums)
    low_sums[...] = jnp.zeros_like(low_sums)
    for piece in range(pieces):
        for copy in fetch(piece):
            copy.wait()
        add(0, 0, piece * depth, depth)
    if count > 1:
        for part in range(2):
            block(1, part).start()
    block(0, 1).wait()
    add(0, 1, 0, NFFT)

    @pl.loop(1, count)
    def _(at):
        for part in range(2):
            block(at, part).wait()

        @pl.when(at + 1 < count)
        def _():
            for part in range(2):
                block(at + 1, part).start()

        for kind in range(2):
            for part in range(2):
                add(at, part, 0, NFFT, (kind,))

    kept = out_refs[0].shape[0] // width
    for slot in range(sums.shape[1] // width):
        both = [sums[c, slot * width : (slot + 1) * width, :] for c in range(2)]
        at = (slot - order.index(low_order[0])) * width
        if 0 <= at < low_sums.shape[1]:
            both = [both[c] + low_scale * low_sums[c, at : at + width, :] for c in range(2)]
        raw = jnp.concatenate(
            [both[0][:half] + both[1][half:], both[1][:half] - both[0][half:]], axis=0
        )
        if slot < kept:
            out_refs[0][slot * width : (slot + 1) * width, :] = raw
        else:
            at = (slot - kept) * width
            out_refs[1][at : at + width, :] = raw.astype(jnp.bfloat16)


def filter_part(voltages, tables, frame, count, kept):
    rows = voltages.shape[1]
    table, low_table, low_scale = tables
    width = table.shape[0] // TAPS
    slots = count + TAPS - 1
    low_slots = count + len(tap_order()[1]) - 1
    shapes = [jax.ShapeDtypeStruct((kept * width, rows), jnp.float32)]
    if slots > kept:
        shapes.append(jax.ShapeDtypeStruct(((slots - kept) * width, rows), jnp.bfloat16))
    pieces = 4
    return pl.pallas_call(
        functools.partial(filter_kernel, frame, low_scale),
        in_specs=[pl.BlockSpec(memory_space=pl.ANY)] * 3,
        out_specs=[pl.BlockSpec(memory_space=pltpu.VMEM)] * len(shapes),
        out_shape=shapes,
        scratch_shapes=[
            pltpu.VMEM((2, slots * width, rows), jnp.float32),
            pltpu.VMEM((2, low_slots * width, rows), jnp.float32),
            pltpu.VMEM((4, rows, NFFT), jnp.bfloat16),
            pltpu.VMEM(table.shape, jnp.bfloat16),
            pltpu.VMEM(low_table.shape, jnp.float8_e4m3fn),
            pltpu.SemaphoreType.DMA((4,)),
            pltpu.SemaphoreType.DMA((pieces,)),
            pltpu.SemaphoreType.DMA((pieces,)),
            pltpu.SemaphoreType.DMA((pieces,)),
        ],
        compiler_params=pltpu.CompilerParams(vmem_limit_bytes=52 * 2**20),
        cost_estimate=pl.CostEstimate(
            flops=2 * 2 * rows * count * NFFT * (table.shape[0] + low_table.shape[0]),
            bytes_accessed=2 * (2 * rows * count * NFFT + NFFT * table.shape[0]),
            transcendentals=0,
        ),
        name="filter_part",
    )(voltages, jnp.asarray(table), jnp.asarray(low_table))


def combine_kernel(early_ref, late_ref, handed_ref, gain_ref, out_ref):
    half = gain_ref.shape[1]
    width = 2 * half
    owners = out_ref.shape[0]
    share = half // owners
    for slot in range(out_ref.shape[1] // (2 * share)):
        raw = early_ref[slot * width : (slot + 1) * width, :] if slot < TAPS else 0.0
        if slot:
            raw = raw + late_ref[(slot - 1) * width : slot * width, :]
        if slot < TAPS - 1:
            raw = raw + handed_ref[slot * width : (slot + 1) * width, :].astype(jnp.float32)
        real, imag = raw[:half], raw[half:]
        out_real = gain_ref[0] * real - gain_ref[1] * imag
        out_imag = gain_ref[0] * imag + gain_ref[1] * real
        for owner in range(owners):
            at = owner * share
            pair = jnp.concatenate([out_real[at : at + share], out_imag[at : at + share]], axis=0)
            at = 2 * share * slot
            out_ref[owner, at : at + 2 * share, :] = pair.astype(jnp.bfloat16)


def combine(early, late, handed, gains, frames, owners):
    _, half, rows = gains.shape
    return pl.pallas_call(
        combine_kernel,
        in_specs=[pl.BlockSpec(memory_space=pltpu.VMEM)] * 4,
        out_specs=pl.BlockSpec(memory_space=pltpu.VMEM),
        out_shape=jax.ShapeDtypeStruct((owners, frames * 2 * half // owners, rows), jnp.bfloat16),
        compiler_params=pltpu.CompilerParams(vmem_limit_bytes=16 * 2**20),
        name="combine",
    )(early, late, handed, gains)


def merge_kernel(frames, share, norm, in_ref, out_ref, left_ref, scratch):
    owners = in_ref.shape[0]
    depth = 2 * owners * frames
    blocks = scratch.shape[0]
    for group in range(owners):
        for frame in range(frames):
            at = 2 * share * frame
            value = in_ref[group, at : at + 2 * share, :].astype(jnp.float32)
            if value.shape[1] < 128 * blocks:
                spare = jnp.zeros((2 * share, 128 * blocks - value.shape[1]), jnp.float32)
                value = jnp.concatenate([value, spare], axis=1)
            for part in range(2):
                row = (part * owners + group) * frames + frame
                for block in range(blocks):
                    scratch[block, pl.ds(row, share, stride=depth), :] = value[
                        part * share : (part + 1) * share, block * 128 : (block + 1) * 128
                    ]
    for block in range(blocks):
        lanes = min(128, out_ref.shape[1] - block * 128)
        at = block * 128
        for channel in range(share):
            rounded = scratch[block, channel * depth : (channel + 1) * depth, :].astype(jnp.bfloat16)
            out_ref[channel * depth : (channel + 1) * depth, at : at + lanes] = rounded[:, :lanes]
            scaled = norm * rounded.astype(jnp.float32)
            high = scaled.astype(jnp.bfloat16).astype(jnp.float32)
            both = jnp.concatenate([high, scaled - high], axis=0).T
            left_ref[at : at + lanes, 2 * channel * depth : 2 * (channel + 1) * depth] = both[
                :lanes
            ].astype(jnp.bfloat16)


def merge(turned, frames, share, norm):
    owners, in_rows, rows = turned.shape
    out_rows = share * 2 * owners * frames
    return pl.pallas_call(
        functools.partial(merge_kernel, frames, share, norm),
        in_specs=[pl.BlockSpec(memory_space=pltpu.VMEM)],
        out_shape=[
            jax.ShapeDtypeStruct((out_rows, rows), jnp.bfloat16),
            jax.ShapeDtypeStruct((rows, 2 * out_rows), jnp.bfloat16),
        ],
        scratch_shapes=[pltpu.VMEM((pl.cdiv(rows, 128), out_rows, 128), jnp.float32)],
        compiler_params=pltpu.CompilerParams(vmem_limit_bytes=16 * 2**20),
        name="merge",
    )(turned)


def visibility(left, right, kind):
    if kind:
        half = right.shape[0] // 2
        right = jnp.concatenate([-right[half:], right[:half]], axis=0)
    both = jnp.concatenate([right, right], axis=0)
    return jnp.dot(left, both, preferred_element_type=jnp.float32)


def block_kernel(share, place_ref, left_ref, right_ref, *refs):
    out_hbm, (values, written) = refs[-3], refs[-2:]
    depth = right_ref.shape[0] // share
    rows = right_ref.shape[1]
    slots = values.shape[0]
    columns = pl.ds(pl.multiple_of(place_ref[0] * rows, rows), rows)

    def write(channel, kind):
        slot = channel % slots
        return pltpu.make_async_copy(
            values.at[slot, kind], out_hbm.at[channel, kind, :, columns], written.at[slot, kind]
        )

    for channel in range(share):
        slot = channel % slots
        right = right_ref[depth * channel : depth * (channel + 1), :]
        for kind in range(2):
            if channel >= slots:
                write(channel - slots, kind).wait()
            values[slot, kind] = visibility(
                left_ref[:, 2 * depth * channel : 2 * depth * (channel + 1)], right, kind
            )
            write(channel, kind).start()
    for channel in range(max(share - slots, 0), share):
        for kind in range(2):
            write(channel, kind).wait()


def correlate(left, right, place, total, result, share):
    out_rows, rows = right.shape
    depth = out_rows // share
    slots = 4
    operands = [place, left, right]
    specs = [pl.BlockSpec(memory_space=pltpu.SMEM)] + [pl.BlockSpec(memory_space=pltpu.VMEM)] * 2
    aliases = {}
    if result is not None:
        aliases = {len(operands): 0}
        operands.append(result)
        specs.append(pl.BlockSpec(memory_space=pl.ANY))
    return pl.pallas_call(
        functools.partial(block_kernel, share),
        in_specs=specs,
        out_specs=pl.BlockSpec(memory_space=pl.ANY),
        out_shape=jax.ShapeDtypeStruct((share, 2, rows, total), jnp.float32),
        scratch_shapes=[
            pltpu.VMEM((slots, 2, rows, rows), jnp.float32),
            pltpu.SemaphoreType.DMA((slots, 2)),
        ],
        input_output_aliases=aliases,
        compiler_params=pltpu.CompilerParams(vmem_limit_bytes=24 * 2**20),
        cost_estimate=pl.CostEstimate(
            flops=8 * share * rows * rows * depth,
            bytes_accessed=4 * share * 2 * rows * rows,
            transcendentals=0,
        ),
        name="correlate",
    )(*operands)


def whole_kernel(left_ref, all_ref, out_ref):
    rows = left_ref.shape[0]
    for group in range(all_ref.shape[0]):
        for kind in range(2):
            out_ref[0, kind, :, group * rows : (group + 1) * rows] = visibility(
                left_ref[...], all_ref[group], kind
            )


def correlate_whole(left, gathered, share):
    groups, out_rows, rows = gathered.shape
    depth = out_rows // share
    return pl.pallas_call(
        whole_kernel,
        grid=(share,),
        in_specs=[
            pl.BlockSpec((rows, 2 * depth), lambda c: (0, c)),
            pl.BlockSpec((groups, depth, rows), lambda c: (0, c, 0)),
        ],
        out_specs=pl.BlockSpec((1, 2, rows, groups * rows), lambda c: (c, 0, 0, 0)),
        out_shape=jax.ShapeDtypeStruct((share, 2, rows, groups * rows), jnp.float32),
        compiler_params=pltpu.CompilerParams(vmem_limit_bytes=24 * 2**20),
        name="correlate_whole",
    )(left, gathered)


def swapped(shard, axis, step):
    if step == 0:
        return shard
    length = lax.axis_size(axis)
    return lax.ppermute(shard, axis, [(i, peer(i, step, length, 1)) for i in range(length)])


def body(voltages, gains):
    inputs_here = voltages.shape[1]
    frames_here = voltages.shape[2] // NFFT
    channels = gains.shape[2]
    owners = lax.axis_size("fgrp")
    share = channels // owners
    norm = 1.0 / math.sqrt(frames_here * owners)
    tables = filter_table(channels)
    late, ending = filter_part(voltages, tables, 1, frames_here - 1, frames_here - 1)
    voltages, ending = lax.optimization_barrier((voltages, ending))
    handed = lax.ppermute(ending, "fgrp", [(i, i + 1) for i in range(owners - 1)])
    (early,) = filter_part(voltages, tables, 0, 1, TAPS)
    handed, early = lax.optimization_barrier((handed, early))
    partial = combine(early, late, handed, jnp.swapaxes(gains, 1, 2), frames_here, owners)
    turned = lax.all_to_all(partial, "fgrp", split_axis=0, concat_axis=0, tiled=True)
    own, left = merge(turned, frames_here, share, norm)
    tiles, pols = lax.axis_size("tile"), lax.axis_size("pol")
    if inputs_here % 128:
        wide = lax.all_gather(lax.all_gather(own, "pol", axis=0), "tile", axis=0)
        return correlate_whole(left, wide.reshape((-1,) + own.shape), share)
    tile, pol = lax.axis_index("tile"), lax.axis_index("pol")

    def place(by_tile, by_pol):
        return (peer(tile, by_tile, tiles, -1) * pols + peer(pol, by_pol, pols, -1)).astype(jnp.int32)

    total = tiles * pols * inputs_here
    result = None
    for by_pol in range(pols):
        near = swapped(own, "pol", by_pol)
        if by_pol:
            near, result = lax.optimization_barrier((near, result))
        for by_tile in range(tiles):
            right = swapped(near, "tile", by_tile)
            where = place(by_tile, by_pol).reshape(1)
            result = correlate(left, right, where, total, result, share)
    return result


def solution(mesh):
    placed = (P(None, ("tile", "pol"), "fgrp"), P(None, ("tile", "pol"), None))
    return jax.shard_map(
        body,
        mesh=mesh,
        in_specs=placed,
        out_specs=P("fgrp", None, ("tile", "pol"), None),
        check_vma=False,
    )
```
